32 devices in a mesh: row: 8 (over z, x), col: 4 (over y, core).
Axes of the slice: x: 2, y: 2, z: 4, core: 2. Of those that a mesh axis runs over, the one named last changes fastest.
Arguments:
- tokens: float32 [2560, 2048], P('row'), may hold values from -8 to 8
- cotangent: float32 [2560, 2048], P('row'), may hold values from -8 to 8
- w_query: float32 [2048, 2048], P('row', 'col'), may hold values from -0.125 to 0.125
- w_key: float32 [2048, 2048], P('row', 'col'), may hold values from -0.125 to 0.125
- w_value: float32 [2048, 2048], P('row', 'col'), may hold values from -0.125 to 0.125
- w_output: float32 [2048, 2048], P('row', 'col'), may hold values from -0.125 to 0.125
- gain_attn: float32 [2048], P('row'), may hold values from 0.1 to 1.9
- lambda_query_first: float32 [128], P('row'), may hold values from -1.75 to 1.75
- lambda_key_first: float32 [128], P('row'), may hold values from -1.75 to 1.75
- lambda_query_second: float32 [128], P('row'), may hold values from -1.75 to 1.75
- lambda_key_second: float32 [128], P('row'), may hold values from -1.75 to 1.75
- gain_head: float32 [256], P('row'), may hold values from 0.1 to 1.9
- w_gate: float32 [2048, 5632], P('row', 'col'), may hold values from -0.125 to 0.125
- w_up: float32 [2048, 5632], P('row', 'col'), may hold values from -0.125 to 0.125
- w_down: float32 [2048, 5632], P('row', 'col'), may hold values from -0.078125 to 0.078125
- gain_ffn: float32 [2048], P('row'), may hold values from 0.1 to 1.9
- tau: float32 [1], replicated, may hold values from 1.5 to 3
- parent_slot: int32 [40], replicated, may hold values from 0 to 39, as said below
- depth: int32 [2560], P('row'), may hold values from 0 to 639, as said below
Outputs:
- output: float32 [2560, 2048], P('row')
- grad_tokens: float32 [2560, 2048], P('row')
- grad_query: float32 [2048, 2048], P('row', 'col')
- grad_key: float32 [2048, 2048], P('row', 'col')
- grad_value: float32 [2048, 2048], P('row', 'col')
- grad_output: float32 [2048, 2048], P('row', 'col')
- grad_gain_attn: float32 [2048], P('row')
- grad_mix: float32 [1], replicated
- grad_gain_head: float32 [256], P('row')
- grad_gate: float32 [2048, 5632], P('row', 'col')
- grad_up: float32 [2048, 5632], P('row', 'col')
- grad_down: float32 [2048, 5632], P('row', 'col')
- grad_gain_ffn: float32 [2048], P('row')
- maxima: float32 [16], replicated
- clipped_query: float32 [2048, 2048], P('row', 'col')
- clipped_key: float32 [2048, 2048], P('row', 'col')
The draws below stay inside these ranges and needn't reach their ends.
Inputs may be any that keep to these rules, and one draw needn't show every extreme that they name: `parent_slot`: every tree has 8 trunk segments in a chain, 4 branch segments whose parent is the last trunk segment and 2 leaf segments on each branch; a tree's first trunk segment is its own parent; the slots of all trees are spread over the devices of row, 5 slots on each. depth[t] = 64 times the number of strict ancestors of t's slot plus t's offset within its slot.
All inputs are finite; a program needn't handle non-finite values.
Results may differ from the reference program's by a relative error of at most 0.0003.
Values sent between devices are 32-bit elements; how exact they have to be, the bound alone decides.
No kernel may reach another device: no remote copies, remote signals or barrier semaphores. Data moves between devices by JAX's collectives and lax.ppermute only.
A program may use at most 256 MiB of HBM per device.

```python
import math
import jax
import jax.numpy as jnp
import numpy as np
from jax import lax

D = 2048
FF = 5632
HEADS = 8
HD = 128
VD = 256
SEG = 64
SEGS_DEV = 5
TRUNK_SEGS = 8
NSEG = 40
TOKENS = 2560


def tree_layout(key):
    tree_size = TRUNK_SEGS + 12
    node_ids = np.arange(tree_size)
    parent_node = np.where(node_ids < TRUNK_SEGS, np.maximum(node_ids - 1, 0), np.where(node_ids < TRUNK_SEGS + 4, TRUNK_SEGS - 1, TRUNK_SEGS + (node_ids - TRUNK_SEGS - 4) // 2))
    depth_node = np.where(node_ids < TRUNK_SEGS, node_ids, np.where(node_ids < TRUNK_SEGS + 4, TRUNK_SEGS, TRUNK_SEGS + 1))
    tree_count = NSEG // tree_size
    global_ids = np.arange(NSEG)
    parent_global = jnp.asarray(global_ids // tree_size * tree_size + parent_node[global_ids % tree_size], dtype=jnp.int32)
    depth_global = jnp.asarray(depth_node[global_ids % tree_size], dtype=jnp.int32)
    tree_of = jnp.asarray(global_ids // tree_size, dtype=jnp.int32)
    slot_ids = jnp.arange(NSEG, dtype=jnp.int32)
    key_tree, key_slot, key_node = jax.random.split(key, 3)
    chosen = jax.random.randint(key_tree, (), 0, tree_count)
    row_count = NSEG // SEGS_DEV
    required = jnp.array([0, row_count // 2 * SEGS_DEV, (row_count - 1) * SEGS_DEV], dtype=jnp.int32)
    slot_score = jax.random.randint(key_slot, (NSEG,), 0, 1 << 16) * NSEG + slot_ids + 8
    slot_score = slot_score.at[required].set(jnp.arange(3, dtype=jnp.int32))
    slot_order = jnp.argsort(slot_score, stable=True).astype(jnp.int32)
    node_score = jax.random.randint(key_node, (NSEG,), 0, 1 << 16) * NSEG + slot_ids
    node_score = jnp.where(tree_of == chosen, node_score, node_score + (1 << 28))
    node_order = jnp.argsort(node_score, stable=True).astype(jnp.int32)
    slot_of_node = jnp.zeros((NSEG,), jnp.int32).at[node_order].set(slot_order)
    parent_slot = jnp.zeros((NSEG,), jnp.int32).at[slot_of_node].set(slot_of_node[parent_global])
    depth_slot = jnp.zeros((NSEG,), jnp.int32).at[slot_of_node].set(depth_global)
    return (parent_slot, depth_slot)


def draw_parent_slot(key, part):
    parent_slot, depth_slot = tree_layout(key)
    return parent_slot


def draw_depth(key, part):
    parent_slot, depth_slot = tree_layout(key)
    token_ids = jnp.arange(TOKENS, dtype=jnp.int32)
    return (depth_slot[token_ids // SEG] * SEG + token_ids % SEG).astype(jnp.int32)


def strengthened(values, stream_key, source, target, parts, factor):
    owner, partner = [(jnp.arange(values.shape[position]) // (values.shape[position] // parts)).reshape([-1 if axis == position else 1 for axis in range(values.ndim)]) for position in (source, target)]
    chosen = jax.random.permutation(stream_key, parts)[partner]
    strong = (owner == chosen) | (owner == (partner + parts // 2) % parts)
    return jnp.where(strong, factor * values, values)


def block_levels(own_key, dims, shards, low, high):
    gain, own = 1.0, jax.random.fold_in(own_key, 6)
    for position, shards_of in shards:
        heights = jnp.exp(jax.random.uniform(jax.random.fold_in(own, position), (shards_of,), jnp.float32, low / len(shards), high / len(shards)))
        gain = gain * jnp.repeat(heights, dims[position] // shards_of).reshape([-1 if axis == position else 1 for axis in range(len(dims))])
    return gain


def bell_draw(own_key, dims, spread, most, pieces=(), kind=jnp.bfloat16):
    values = spread * jax.random.normal(own_key, dims, jnp.float32)
    if pieces:
        values = values * block_levels(own_key, dims, pieces, -0.22, 0.18)
    return jnp.clip(values, -most, most).astype(kind)


def bell_draw_with(key, shape, scale, most, cuts, heavy, kind=jnp.bfloat16):
    entries = scale * jax.random.normal(key, shape, jnp.float32)
    if cuts:
        entries = entries * block_levels(key, shape, cuts, -0.22, 0.18)
    return jnp.clip(strengthened(entries, jax.random.fold_in(key, 3), *heavy), -most, most).astype(kind)


def setup_inputs(seed: int = 0) -> dict:
    key_of = jax.random.split(jax.random.key(seed), 20)
    return {
        "tokens": bell_draw_with(key_of[0], (TOKENS, D), 1.0, 8.0, ((0, 8),), (0, 1, 8, 2.0), jnp.float32),
        "cotangent": bell_draw_with(key_of[1], (TOKENS, D), 1.0, 8.0, ((0, 8),), (0, 1, 8, 2.0), jnp.float32),
        "w_query": bell_draw(key_of[2], (D, HEADS * 2 * HD), D ** -0.5, 0.125, ((0, 8), (1, 4)), jnp.float32),
        "w_key": bell_draw(key_of[3], (D, HEADS * 2 * HD), D ** -0.5, 0.125, ((0, 8), (1, 4)), jnp.float32),
        "w_value": bell_draw(key_of[4], (D, HEADS * VD), D ** -0.5, 0.125, ((0, 8), (1, 4)), jnp.float32),
        "w_output": bell_draw(key_of[5], (D, HEADS * VD), (HEADS * VD) ** -0.5, 0.125, ((0, 8), (1, 4)), jnp.float32),
        "gain_attn": jnp.clip(1.0 + 0.18 * jax.random.normal(key_of[6], (D,), jnp.float32), 0.1, 1.9),
        "lambda_query_first": bell_draw(key_of[7], (HD,), 0.3, 1.75, ((0, 8),), jnp.float32),
        "lambda_key_first": bell_draw(key_of[8], (HD,), 0.3, 1.75, ((0, 8),), jnp.float32),
        "lambda_query_second": bell_draw(key_of[9], (HD,), 0.3, 1.75, ((0, 8),), jnp.float32),
        "lambda_key_second": bell_draw(key_of[10], (HD,), 0.3, 1.75, ((0, 8),), jnp.float32),
        "gain_head": jnp.clip(1.0 + 0.18 * jax.random.normal(key_of[11], (VD,), jnp.float32), 0.1, 1.9),
        "w_gate": bell_draw(key_of[12], (D, FF), D ** -0.5, 0.125, ((0, 8), (1, 4)), jnp.float32),
        "w_up": bell_draw(key_of[13], (D, FF), D ** -0.5, 0.125, ((0, 8), (1, 4)), jnp.float32),
        "w_down": bell_draw(key_of[14], (D, FF), FF ** -0.5, 0.078125, ((0, 8), (1, 4)), jnp.float32),
        "gain_ffn": jnp.clip(1.0 + 0.18 * jax.random.normal(key_of[15], (D,), jnp.float32), 0.1, 1.9),
        "tau": jnp.clip(jax.random.uniform(key_of[16], (1,), jnp.float32, 1.5, 3.0), 1.5, 3.0),
        "parent_slot": draw_parent_slot(jax.random.fold_in(key_of[19], 71), 0),
        "depth": draw_depth(jax.random.fold_in(key_of[19], 71), 0),
    }


epsilon = 1e-05
lambda_init = 0.2
rope_log_base = 9.210340371976184
highest = lax.Precision.HIGHEST

@jax.custom_vjp
def low(v):
    return lax.optimization_barrier(v.astype(jnp.bfloat16)).astype(jnp.float32)

@jax.custom_vjp
def low_back(v):
    return v

def low_keep(v):
    return (low(v), None)

def low_pass(kept, grad):
    return (grad,)

def back_keep(v):
    return (v, None)

def back_low(kept, grad):
    return (low(grad),)
low.defvjp(low_keep, low_pass)
low_back.defvjp(back_keep, back_low)

def rms_scale(values, gain_vec):
    return values * lax.rsqrt(lax.optimization_barrier(jnp.mean(values * values, axis=-1, keepdims=True)) + epsilon) * gain_vec

def rotate(values, positions):
    half_dim = values.shape[-1] // 2
    frequency = jnp.exp(-rope_log_base * jnp.arange(half_dim, dtype=jnp.float32) / half_dim)
    angles = positions.astype(jnp.float32)[:, None] * frequency[None, :]
    cosine_part = jnp.cos(angles)[:, None, None, :]
    sine_part = jnp.sin(angles)[:, None, None, :]
    lead_half = values[..., :half_dim]
    tail_half = values[..., half_dim:]
    return jnp.concatenate([lead_half * cosine_part - tail_half * sine_part, tail_half * cosine_part + lead_half * sine_part], axis=-1)

def ancestors(parent_slot):
    count = parent_slot.shape[0]
    slot_ids = jnp.arange(count, dtype=jnp.int32)
    current = slot_ids
    marked = jnp.zeros((count, count), dtype=bool)
    for climb_step in range(TRUNK_SEGS + 2):
        current = parent_slot[current]
        marked = marked | (current[:, None] == slot_ids[None, :])
    return marked & (slot_ids[:, None] != slot_ids[None, :])

def reference(tokens, cotangent, w_query, w_key, w_value, w_output, gain_attn, lambda_query_first, lambda_key_first, lambda_query_second, lambda_key_second, gain_head, w_gate, w_up, w_down, gain_ffn, tau, parent_slot, depth):
    strict = ancestors(parent_slot)
    token_total = tokens.shape[0]
    block_rows = math.gcd(token_total, 128)
    key_index = jnp.arange(token_total, dtype=jnp.int32)
    key_slots = key_index // SEG
    logit_scale = 1.0 / math.sqrt(HD)
    mix_value = jnp.exp(jnp.sum(lambda_query_first * lambda_key_first)) - jnp.exp(jnp.sum(lambda_query_second * lambda_key_second)) + lambda_init
    mix_vec = jnp.reshape(mix_value, (1,)).astype(jnp.float32)

    def layer(tokens, w_query, w_key, w_value, w_output, gain_attn, mix_in, gain_head, w_gate, w_up, w_down, gain_ffn):
        normed = rms_scale(tokens, gain_attn)
        queries = jnp.dot(normed, w_query, precision=highest).reshape(token_total, HEADS, 2, HD)
        queries = rotate(queries, depth)
        key_rows = jnp.dot(normed, w_key, precision=highest).reshape(token_total, HEADS, 2, HD)
        key_rows = rotate(key_rows, depth)
        values = jnp.dot(normed, w_value, precision=highest).reshape(token_total, HEADS, VD)

        def attend_block(block_start):
            query_block = lax.dynamic_slice_in_dim(queries, block_start, block_rows, 0)
            rows = block_start + jnp.arange(block_rows, dtype=jnp.int32)
            row_slots = rows // SEG
            allowed = strict[row_slots][:, key_slots] | (row_slots[:, None] == key_slots[None, :]) & (key_index[None, :] <= rows[:, None])
            scores = jnp.einsum('thjd,khjd->jhtk', query_block, key_rows, precision=highest) * logit_scale
            masked = jnp.where(allowed[None, None], scores, -1e+30)
            peak_logit = lax.optimization_barrier(jnp.max(masked, axis=-1, keepdims=True))
            weights = jnp.where(allowed[None, None], jnp.exp(masked - peak_logit), 0.0)
            probs = weights / lax.optimization_barrier(jnp.sum(weights, axis=-1, keepdims=True))
            mixed = jnp.einsum('jhtk,khv->jhtv', probs, values, precision=highest)
            return (mixed, lax.optimization_barrier(jnp.max(peak_logit[..., 0], axis=-1)))
        starts = jnp.arange(0, token_total, block_rows, dtype=jnp.int32)
        mixed, block_peak = lax.map(jax.checkpoint(attend_block), starts)
        mixed = jnp.moveaxis(mixed, 0, 2).reshape(2, HEADS, token_total, VD)
        contrast = mixed[0] - mix_in[0] * mixed[1]
        headed = rms_scale(contrast, gain_head) * (1.0 - lambda_init)
        joined = jnp.transpose(headed, (1, 0, 2)).reshape(token_total, HEADS * VD)
        residual = tokens + jnp.dot(joined, w_output.T, precision=highest)
        normed_ffn = rms_scale(residual, gain_ffn)
        gating = jnp.dot(normed_ffn, w_gate, precision=highest)
        up_proj = jnp.dot(normed_ffn, w_up, precision=highest)
        hidden = jax.nn.silu(gating) * up_proj
        output = residual + jnp.dot(hidden, w_down.T, precision=highest)
        maxima = lax.optimization_barrier(jnp.max(block_peak, axis=0)).T.reshape(2 * HEADS)
        return (output, maxima)
    output, pullback, maxima = jax.vjp(layer, tokens, w_query, w_key, w_value, w_output, gain_attn, mix_vec, gain_head, w_gate, w_up, w_down, gain_ffn, has_aux=True)
    grads = pullback(cotangent)
    factor = tau[0] / jnp.maximum(maxima, tau[0])
    root_factor = jnp.sqrt(factor).reshape(1, HEADS, 2, 1)
    clipped_query = (w_query.reshape(D, HEADS, 2, HD) * root_factor).reshape(w_query.shape)
    clipped_key = (w_key.reshape(D, HEADS, 2, HD) * root_factor).reshape(w_key.shape)
    return (output, grads[0], grads[1], grads[2], grads[3], grads[4], grads[5], grads[6], grads[7], grads[8], grads[9], grads[10], grads[11], maxima, clipped_query, clipped_key)
```

```python
import math

import jax
import jax.numpy as jnp
from jax import lax
from jax.experimental import pallas as pl
from jax.experimental.pallas import tpu as pltpu
from jax.sharding import Mesh
from jax.sharding import PartitionSpec as P

HEADS = 8
HD = 128
VD = 256
SEG = 64
ZN = 4
KN = 2
BLOCKS = ZN
TRUNK_SEGS = 8

epsilon = 1e-05
lambda_init = 0.2
rope_log_base = 9.210340371976184
high = lax.Precision.HIGH
highest = lax.Precision.HIGHEST
f32 = jnp.float32
bf16 = jnp.bfloat16
VMEM_BYTES = 60 * 1024 * 1024


def dot(a, b, contract_a=1, contract_b=0):
    return lax.dot_general(
        a, b, (((contract_a,), (contract_b,)), ((), ())), precision=high, preferred_element_type=f32
    )


def fine(a, b, contract_a=1, contract_b=0):
    return lax.dot_general(
        a, b, (((contract_a,), (contract_b,)), ((), ())), precision=highest, preferred_element_type=f32
    )


def thirds(v):
    top = v.astype(bf16)
    rest = v - top.astype(f32)
    low = rest.astype(bf16)
    return top, low, (rest - low.astype(f32)).astype(bf16)


def six(a, b):
    (a1, a2, a3), (b1, b2, b3) = a, b
    return mm(a1, b1) + (mm(a1, b2) + mm(a2, b1)) + (mm(a2, b2) + mm(a1, b3) + mm(a3, b1))


def halves(v):
    top = v.astype(bf16)
    return top, (v - top.astype(f32)).astype(bf16)


def mm(a, b):
    return jnp.dot(a, b, preferred_element_type=f32)


def after(v, *others):
    return lax.optimization_barrier((v,) + others)[0]


def shifted(v, axis, n, shift):
    return lax.ppermute(v, axis, [(i, (i + shift) % n) for i in range(n)])


def at(v, index, dim):
    return lax.dynamic_index_in_dim(v, index, dim, keepdims=False)


def part(v, index, rows):
    return lax.dynamic_slice_in_dim(v, index * rows, rows)


def exchanged(v, axis, n):
    i = lax.axis_index(axis)
    rows = v.shape[0] // n
    return [part(v, i, rows)] + [
        shifted(part(v, (i + s) % n, rows), axis, n, s) for s in range(1, n)
    ]


def in_order(pieces, axis, n, dim=0):
    i = lax.axis_index(axis)

    def source(j):
        shift = (i + n - j) % n
        out = pieces[0]
        for s in range(1, n):
            out = jnp.where(shift == s, pieces[s], out)
        return out

    return jnp.concatenate([source(j) for j in range(n)], axis=dim)


def small_gather(v, axis, n):
    return in_order([v[None]] + [shifted(v[None], axis, n, s) for s in range(1, n)], axis, n)


def small_fold(v, axis, n, fold):
    out = v
    for s in range(1, n):
        out = fold(out, shifted(v, axis, n, s))
    return out


def direct(v, xn, yn):
    out = {}
    for s in range(xn):
        for t in range(yn):
            pairs = [
                (a * yn + b, (a + s) % xn * yn + (b + t) % yn) for a in range(xn) for b in range(yn)
            ]
            out[s, t] = lax.ppermute(v, ("x", "y"), pairs) if s or t else v
    return out


def square_out(v, first, sizes):
    n = sizes[first]
    return [v] + [shifted(v, first, n, s) for s in range(1, n)]


def side_out(v, first, sizes):
    second = "y" if first == "x" else "x"
    n = sizes[second]
    return [shifted(v, second, n, t) for t in range(1, n)]


def square_on(came, first, sizes, side=None):
    second = "y" if first == "x" else "x"
    n = sizes[second]
    out = {}
    for s, v in enumerate(came):
        out[s, 0] = v
        for t in range(1, n):
            out[s, t] = side[t - 1] if side and s == 0 else shifted(v, second, n, t)
    return out if first == "x" else {(s, t): v for (t, s), v in out.items()}


def along_first(pieces, first):
    return pieces if first == "x" else {(t, s): v for (s, t), v in pieces.items()}


def square_back(pieces, first, sizes):
    m, n = sizes[first], sizes["y" if first == "x" else "x"]
    v = along_first(pieces, first)
    return [shifted(v[s, t], first, m, -s) for t in reversed(range(n)) for s in range(1, m)]


def square_added(pieces, came, first, sizes):
    m, n = sizes[first], sizes["y" if first == "x" else "x"]
    v = along_first(pieces, first)
    out = [v[0, t] for t in range(n)]
    order = [t for t in reversed(range(n)) for s in range(1, m)]
    for t, what in zip(order, came):
        out[t] = out[t] + what
    return out


def square_back_on(sums, second, sizes):
    n = sizes[second]
    return [shifted(sums[t], second, n, -t) for t in range(1, n)]


def logits_chunk(keys_wide, queries, rows, j):
    first, last = keys_wide[0, j, rows, :], keys_wide[1, j, rows, :]
    top, low, rest = queries[j]
    return mm(first, top) + (mm(first, low) + mm(last, rest))


def split_keys(keys, keys_wide, rows):
    for j in range(2):
        top, low, rest = thirds(keys[:, j * HD : (j + 1) * HD])
        keys_wide[0, j, rows, :HD] = top
        keys_wide[0, j, rows, HD:] = low
        keys_wide[1, j, rows, :HD] = top
        keys_wide[1, j, rows, HD:] = rest


def split_queries(q):
    out = []
    for j in range(2):
        top, low, rest = thirds(q[:, j * HD : (j + 1) * HD].T)
        out.append([jnp.concatenate(p, axis=0) for p in ((top, top), (low, low), (rest, top))])
    return out


def chunk_rows(c, size):
    return pl.ds(pl.multiple_of(c * size, size), size)


def brought(run, start_ref, first, count, source, target):
    def move(i, carry):
        target[chunk_rows(i, run), :] = source[chunk_rows(start_ref[first + i], run), :]
        return carry

    lax.fori_loop(0, count, move, 0)


def taken_back(run, start_ref, first, count, source, target):
    def move(i, carry):
        target[chunk_rows(start_ref[first + i], run), :] = source[chunk_rows(i, run), :]
        return carry

    lax.fori_loop(0, count, move, 0)


def forward_kernel(
    run, mix_ref, seen_ref, count_ref, key_ref, own_ref, q_ref, k_ref, v_ref, bias_ref,
    o_ref, stat_ref, keys_wide, vt, held, sorted_rows, sorted_q,
):
    total = k_ref.shape[0]
    chunk = vt.shape[3]
    count = total // chunk
    tile = pl.program_id(0)

    @pl.when(tile == 0)
    def _():
        brought(run, own_ref, 0, q_ref.shape[0] // run, q_ref, sorted_q)
        brought(run, key_ref, 0, total // run, k_ref, sorted_rows)

        def split(c, carry):
            rows = chunk_rows(c, chunk)
            split_keys(sorted_rows[rows, :], keys_wide, rows)
            return carry

        lax.fori_loop(0, count, split, 0)
        brought(run, key_ref, 0, total // run, v_ref, sorted_rows)

        def turn(c, carry):
            for i, p in enumerate(thirds(sorted_rows[chunk_rows(c, chunk), :].T)):
                vt[i, c] = p
            return carry

        lax.fori_loop(0, count, turn, 0)

    split = split_queries(sorted_q[chunk_rows(tile, TILE), :])
    visits = count_ref[tile]

    def score(i, peaks):
        rows = chunk_rows(seen_ref[tile * count + i], chunk)
        out = []
        for j in range(2):
            s = logits_chunk(keys_wide, split, rows, j) + bias_ref[rows, :]
            held[j, rows, :] = s
            out.append(jnp.maximum(peaks[j], jnp.max(s, axis=0, keepdims=True)))
        return tuple(out)

    peaks = lax.fori_loop(0, visits, score, (jnp.full((1, TILE), -1e30, f32),) * 2)

    def weigh(i, sums):
        rows = chunk_rows(seen_ref[tile * count + i], chunk)
        out = []
        for j in range(2):
            w = jnp.exp(held[j, rows, :] - peaks[j])
            held[j, rows, :] = w
            out.append(sums[j] + jnp.sum(w, axis=0, keepdims=True))
        return tuple(out)

    sums = lax.fori_loop(0, visits, weigh, (jnp.zeros((1, TILE), f32),) * 2)
    first, second = 1.0 / sums[0], mix_ref[0] / sums[1]

    def collect(i, acc):
        c = seen_ref[tile * count + i]
        rows = chunk_rows(c, chunk)
        both = thirds(held[0, rows, :] * first - held[1, rows, :] * second)
        return acc + six([vt[i, c] for i in range(3)], both)

    out = lax.fori_loop(0, visits, collect, jnp.zeros((VD, TILE), f32)).T
    for i in range(TILE // run):
        o_ref[chunk_rows(own_ref[tile * (TILE // run) + i], run), :] = out[i * run : (i + 1) * run, :]
    for j in range(2):
        stat_ref[j : j + 1, :] = peaks[j] + jnp.log(sums[j])
        stat_ref[2 + j : 3 + j, :] = peaks[j]
    stat_ref[4:8, :] = jnp.zeros((4, TILE), f32)


def backward_kernel(
    run, mix_ref, seen_ref, count_ref, key_ref, own_ref, q_ref, dc_ref, stat_ref, k_ref, v_ref, bias_ref,
    dq_ref, dk_ref, dv_ref, inner_ref, keys_wide, kt, held, cross, sorted_v, sorted_q, sorted_dc,
):
    total = k_ref.shape[0]
    chunk = kt.shape[3]
    count = total // chunk
    mix = mix_ref[0]
    tile = pl.program_id(0)

    @pl.when(tile == 0)
    def _():
        brought(run, own_ref, 0, q_ref.shape[0] // run, q_ref, sorted_q)
        brought(run, own_ref, 0, q_ref.shape[0] // run, dc_ref, sorted_dc)
        brought(run, key_ref, 0, total // run, k_ref, sorted_v)

        def prepare(c, carry):
            rows = chunk_rows(c, chunk)
            keys = sorted_v[rows, :]
            split_keys(keys, keys_wide, rows)
            for i, p in enumerate(halves(keys.T)):
                kt[i, c] = p
            dk_ref[rows, :] = jnp.zeros(keys.shape, f32)
            dv_ref[rows, :] = jnp.zeros(keys.shape, f32)
            return carry

        lax.fori_loop(0, count, prepare, 0)
        brought(run, key_ref, 0, total // run, v_ref, sorted_v)

    queries, cotangents = sorted_q[chunk_rows(tile, TILE), :], sorted_dc[chunk_rows(tile, TILE), :]
    split = split_queries(queries)
    dct = thirds(cotangents.T)
    dc_top, dc_low = halves(cotangents)
    dc_wide = jnp.concatenate([dc_top, dc_top], axis=0)
    q_top, q_low = halves(queries)
    q_wide = jnp.concatenate([q_top, q_top], axis=0)
    norms = [stat_ref[j : j + 1, :] for j in range(2)]
    visits = count_ref[tile]

    def first(i, inner):
        rows = chunk_rows(seen_ref[tile * count + i], chunk)
        bias = bias_ref[rows, :]
        both = six(thirds(sorted_v[rows, :]), dct)
        cross[rows, :] = both
        out, probs = [], []
        for j in range(2):
            p = jnp.exp(logits_chunk(keys_wide, split, rows, j) + bias - norms[j])
            held[j, rows, :] = p
            probs.append(p)
            out.append(inner[j] + jnp.sum(p * both, axis=0, keepdims=True))
        top, low = halves(probs[0] - mix * probs[1])
        dv_ref[rows, :] += mm(jnp.concatenate([top, low], axis=1), dc_wide) + mm(top, dc_low)
        return tuple(out)

    inner = lax.fori_loop(0, visits, first, (jnp.zeros((1, TILE), f32),) * 2)

    def second(i, acc):
        c = seen_ref[tile * count + i]
        rows = chunk_rows(c, chunk)
        both = cross[rows, :]
        out = []
        for j in range(2):
            d = held[j, rows, :] * (both - inner[j])
            if j == 1:
                d = d * (-mix)
            top, low = halves(d)
            cols = slice(j * HD, (j + 1) * HD)
            dk_ref[rows, cols] += mm(jnp.concatenate([top, low], axis=1), q_wide[:, cols]) + mm(
                top, q_low[:, cols]
            )
            kt_top, kt_low = kt[0, c, cols, :], kt[1, c, cols, :]
            out.append(acc[j] + (mm(kt_top, top) + (mm(kt_top, low) + mm(kt_low, top))))
        return tuple(out)

    dq = lax.fori_loop(0, visits, second, (jnp.zeros((HD, TILE), f32),) * 2)
    dq = jnp.concatenate(dq, axis=0).T
    for i in range(TILE // run):
        dq_ref[chunk_rows(own_ref[tile * (TILE // run) + i], run), :] = dq[i * run : (i + 1) * run, :]
    for j in range(2):
        inner_ref[j : j + 1, :] = inner[j]
    inner_ref[2:8, :] = jnp.zeros((6, TILE), f32)

    @pl.when(tile == pl.num_programs(0) - 1)
    def _():
        for ref in (dk_ref, dv_ref):

            def keep(c, carry):
                rows = chunk_rows(c, chunk)
                sorted_v[rows, :] = ref[rows, :]
                return carry

            lax.fori_loop(0, count, keep, 0)
            taken_back(run, key_ref, 0, total // run, sorted_v, ref)


TILE = 128
CHUNK = 256


def whole():
    return pl.BlockSpec(memory_space=pltpu.VMEM)


def table():
    return pl.BlockSpec(memory_space=pltpu.SMEM)


def attend(run, mix, tables, queries, keys, values, bias):
    total, count = keys.shape[0], queries.shape[0]
    chunk = math.gcd(total, CHUNK)
    lanes = lambda rows: pl.BlockSpec((rows, TILE), lambda i: (0, i))
    return pl.pallas_call(
        lambda *refs: forward_kernel(run, *refs),
        grid=(count // TILE,),
        in_specs=[table()] * 5 + [whole()] * 3 + [lanes(total)],
        out_specs=[whole(), lanes(8)],
        out_shape=[
            jax.ShapeDtypeStruct((count, VD), f32), jax.ShapeDtypeStruct((8, count), f32),
        ],
        scratch_shapes=[
            pltpu.VMEM((2, 2, total, 2 * HD), bf16),
            pltpu.VMEM((3, total // chunk, VD, chunk), bf16),
            pltpu.VMEM((2, total, TILE), f32),
            pltpu.VMEM((total, 2 * HD), f32),
            pltpu.VMEM((count, 2 * HD), f32),
        ],
        compiler_params=pltpu.CompilerParams(vmem_limit_bytes=VMEM_BYTES),
        cost_estimate=pl.CostEstimate(flops=4 * 10**10, bytes_accessed=0, transcendentals=0),
        name="attend",
    )(mix, *tables, queries, keys, values, bias)


def attend_back(run, mix, tables, queries, contrast, stat, keys, values, bias):
    total, count = keys.shape[0], queries.shape[0]
    chunk = math.gcd(total, CHUNK)
    lanes = lambda rows: pl.BlockSpec((rows, TILE), lambda i: (0, i))
    return pl.pallas_call(
        lambda *refs: backward_kernel(run, *refs),
        grid=(count // TILE,),
        in_specs=[table()] * 5 + [whole()] * 2 + [lanes(8)] + [whole()] * 2 + [lanes(total)],
        out_specs=[whole(), whole(), whole(), lanes(8)],
        out_shape=[
            jax.ShapeDtypeStruct((count, 2 * HD), f32),
            jax.ShapeDtypeStruct((total, 2 * HD), f32),
            jax.ShapeDtypeStruct((total, VD), f32),
            jax.ShapeDtypeStruct((8, count), f32),
        ],
        scratch_shapes=[
            pltpu.VMEM((2, 2, total, 2 * HD), bf16),
            pltpu.VMEM((2, total // chunk, 2 * HD, chunk), bf16),
            pltpu.VMEM((2, total, TILE), f32),
            pltpu.VMEM((total, TILE), f32),
            pltpu.VMEM((total, VD), f32),
            pltpu.VMEM((count, 2 * HD), f32),
            pltpu.VMEM((count, VD), f32),
        ],
        compiler_params=pltpu.CompilerParams(vmem_limit_bytes=VMEM_BYTES),
        cost_estimate=pl.CostEstimate(flops=4 * 10**10, bytes_accessed=0, transcendentals=0),
        name="attend_back",
    )(mix, *tables, queries, contrast, stat, keys, values, bias)


def layer(xn, yn):
    sizes = {"x": xn, "y": yn}
    places = [(s, t) for s in range(xn) for t in range(yn)]

    def shards(
        tokens, cotangent, w_query, w_key, w_value, w_output, gain_attn, lambda_query_first,
        lambda_key_first, lambda_query_second, lambda_key_second, gain_head, w_gate, w_up, w_down,
        gain_ffn, tau, parent_slot, depth,
    ):
        z, x, y, k = (lax.axis_index(a) for a in "zxyk")
        home_rows, width = tokens.shape
        segs = home_rows // SEG
        run = SEG // (yn * KN)
        piece_rows = segs * run
        group = ZN * KN * piece_rows
        sub = BLOCKS // yn
        held_rows = w_query.shape[0]
        part_rows = held_rows // yn
        square_rows = ZN * part_rows
        total = ZN * xn * home_rows
        slot_total = parent_slot.shape[0]
        hidden_cols = w_gate.shape[1] // sub

        def block(v, i):
            return v[:, i * part_rows : (i + 1) * part_rows]

        def by_index(i, n, order):
            out = order(0)
            for j in range(1, n):
                out = jnp.where(i == j, order(j), out)
            return out

        def to_distance_x(v):
            return by_index(x, xn, lambda j: jnp.concatenate(
                [block(v, (c * xn + (j + xn - s) % xn) * yn + t)
                 for s in range(xn) for c in range(ZN) for t in range(yn)], axis=1))

        def from_distance_x(v):
            return by_index(x, xn, lambda j: jnp.concatenate(
                [block(v, ((j + xn - a) % xn * ZN + c) * yn + t)
                 for c in range(ZN) for a in range(xn) for t in range(yn)], axis=1))

        def to_distance_y(v):
            return by_index(y, yn, lambda j: jnp.concatenate(
                [block(v, (s * ZN + c) * yn + (j + yn - t) % yn)
                 for s in range(xn) for t in range(yn) for c in range(ZN)], axis=1))

        def from_distance_y(v):
            return by_index(y, yn, lambda j: jnp.concatenate(
                [block(v, (s * yn + (j + yn - t) % yn) * ZN + c)
                 for s in range(xn) for c in range(ZN) for t in range(yn)], axis=1))

        def piece(v):
            v = v.reshape(segs, yn * KN, run, width)
            return to_distance_x(at(v, y * KN + k, 1).reshape(piece_rows, width))

        def home_along(v, axis, n):
            return [v] + [shifted(v, axis, n, s) for s in range(1, n)]

        def homed(v):
            v = v.reshape(KN, yn, segs, run, width)
            return jnp.transpose(v, (2, 1, 0, 3, 4)).reshape(home_rows, width)

        def group_gather(v):
            return lax.all_gather(v, ("z", "k"), axis=0, tiled=True)

        def group_sum(v):
            return lax.psum_scatter(v, ("z", "k"), scatter_dimension=0, tiled=True)

        def packed(mats, blocks):
            rows = mats[0].shape[1] // blocks
            mats = [m.T for m in mats]
            return jnp.concatenate([m[s * rows : (s + 1) * rows] for s in range(blocks) for m in mats])

        def lanes(v, index, size):
            return lax.dynamic_slice_in_dim(v, index * size, size, 1)

        def along_y(v):
            mine = lanes(v, y, part_rows)
            return [mine] + [shifted(lanes(v, (y + s) % yn, part_rows), "y", yn, s) for s in range(1, yn)]

        def back_along_z(mats):
            v = jnp.concatenate(mats)
            size = v.shape[1] // ZN
            mine = lanes(v, z, size)
            return [mine] + [shifted(lanes(v, (z + s) % ZN, size), "z", ZN, s) for s in range(1, ZN)]

        def unpacked(v, mats, blocks):
            cols = v.shape[0] // (blocks * mats)
            part = lambda s, m: v[(s * mats + m) * cols : (s * mats + m + 1) * cols]
            return [jnp.concatenate([part(s, m) for s in range(blocks)]).T for m in range(mats)]

        def joined_up(pieces):
            return jnp.concatenate([pieces[p] for p in places], axis=1)

        def cut(g):
            return {p: g[:, i * square_rows : (i + 1) * square_rows] for i, p in enumerate(places)}

        def tiled_up(pieces):
            return jnp.concatenate(
                [jnp.concatenate([pieces[s, t] for s in range(xn)], axis=1) for t in range(yn)]
            )

        def tiles(g):
            r, c = g.shape[0] // yn, g.shape[1] // xn
            return {(s, t): g[t * r : (t + 1) * r, s * c : (s + 1) * c] for s, t in places}

        def halved(v):
            mid = v.shape[0] // 2
            return v[:mid], v[mid:]

        def rowsum(w, g):
            return jnp.sum(w * g, axis=1)

        last = []

        def now(*v):
            out = lax.optimization_barrier(tuple(v) + tuple(last))[: len(v)]
            return out[0] if len(v) == 1 else out

        def then(*v):
            last[:] = v
            return v[0] if len(v) == 1 else v

        def take(*v):
            out = now(*v)
            return then(*(out if len(v) > 1 else (out,)))

        def take_all(pieces):
            out = lax.optimization_barrier(tuple(pieces) + tuple(last))[: len(pieces)]
            then(*out)
            return list(out)

        attn_gain, ffn_gain = gain_attn[:, None], gain_ffn[:, None]
        sent = along_y(packed([w_query, w_key, w_value], sub))
        small = jnp.concatenate(
            [gain_head, lambda_query_first, lambda_key_first, lambda_query_second, lambda_key_second]
        )
        small_sent = home_along(small[None], "x", xn)
        mine = piece(tokens)
        scale = lax.rsqrt(jnp.mean(mine * mine, axis=1, keepdims=True) + epsilon)
        plain_mine = then(to_distance_y(mine) * scale)
        small = in_order(take_all(small_sent), "x", xn).reshape(1, -1)
        small_sent = home_along(small, "z", ZN)
        down_sent = w_down.T
        then(down_sent)
        small = in_order(take_all(small_sent), "z", ZN)
        attn_y = in_order(take_all(sent), "y", yn)
        y_gain = part(gain_attn, y, part_rows)[None, :]
        sent = exchanged(attn_y * y_gain, "z", ZN)
        output_sent = along_y(after(packed([w_output], sub), attn_y))
        small = small.reshape(ZN * xn, -1)
        n_gain, n_lambda = gain_head.shape[0], lambda_key_first.shape[0]
        head_gain = small[:, :n_gain].reshape(1, -1)
        query_first, key_first, query_second, key_second = (
            small[:, n_gain + i * n_lambda : n_gain + (i + 1) * n_lambda] for i in range(4)
        )
        mix = (
            jnp.exp(jnp.sum(query_first * key_first))
            - jnp.exp(jnp.sum(query_second * key_second))
            + lambda_init
        ).reshape(1)

        slot_ids = jnp.arange(slot_total, dtype=jnp.int32)
        same = slot_ids[:, None] == slot_ids[None, :]
        reach = (same | (parent_slot[:, None] == slot_ids[None, :])).astype(f32)
        for _ in range(4):
            reach = (jnp.dot(reach, reach) > 0.5).astype(f32)
        strict = jnp.where(same, 0.0, reach)
        depth_of = jnp.sum(strict, axis=1)

        ids = slot_ids.astype(f32)
        root = jnp.sum(reach * jnp.where(depth_of == 0, ids, 0.0)[None, :], axis=1)
        branch_slot = jnp.sum(reach * jnp.where(depth_of == TRUNK_SEGS, ids + 1.0, 0.0)[None, :], axis=1)
        leaf = jnp.where(depth_of > TRUNK_SEGS, ids + 1.0, 0.0)
        place = jnp.where(
            depth_of < TRUNK_SEGS, depth_of, TRUNK_SEGS + branch_slot * (slot_total + 1) + leaf
        )
        ordinal = (root * (TRUNK_SEGS + (slot_total + 1) ** 2 + 1) + place).astype(jnp.int32)
        before = (ordinal[None, :] < ordinal[:, None]) | (
            (ordinal[None, :] == ordinal[:, None]) & (slot_ids[None, :] < slot_ids[:, None])
        )
        rank = jnp.sum(before, axis=1)
        mine_too = slot_ids // segs % xn == x
        own_rank = jnp.sum(before & mine_too[None, :], axis=1)
        own_slots = ZN * segs
        key_order = jnp.sum(jnp.where(rank[:, None] == slot_ids[None, :], slot_ids[:, None], 0), axis=0)
        own_order = jnp.sum(
            jnp.where(
                (own_rank[:, None] == jnp.arange(own_slots)[None, :]) & mine_too[:, None],
                slot_ids[:, None], 0,
            ),
            axis=0,
        )

        def run_at(slot, k_of):
            return ((slot // (xn * segs)) * KN + k_of) * segs + slot % segs

        ks = jnp.arange(KN, dtype=jnp.int32)
        own_runs = run_at(own_order[:, None], ks[None, :]).reshape(-1)
        ys = jnp.arange(yn, dtype=jnp.int32)[None, :, None]
        slot = key_order[:, None, None]
        piece_of = ((x + xn - slot // segs % xn) % xn) * yn + (y + yn - ys) % yn
        key_runs = (piece_of * (group // run) + run_at(slot, ks[None, None, :])).reshape(-1)

        padded = -(-group // TILE) * TILE
        extra = padded - group
        own_slot = jnp.repeat(own_order, group // own_slots)
        own_offset = y * KN * run + jnp.arange(group, dtype=jnp.int32) % (KN * run)
        key_slot, key_offset = jnp.repeat(key_order, SEG), jnp.arange(total, dtype=jnp.int32) % SEG
        own_hot = (own_slot[:, None] == slot_ids[None, :]).astype(f32)
        key_hot = (key_slot[:, None] == slot_ids[None, :]).astype(f32)
        own_path = jnp.dot(own_hot, strict)
        seen = jnp.dot(key_hot, own_path.T) > 0.5
        seen = seen | (
            (key_slot[:, None] == own_slot[None, :]) & (key_offset[:, None] <= own_offset[None, :])
        )
        seen = jnp.pad(seen, ((0, 0), (0, extra)))
        own_runs = jnp.concatenate([own_runs, jnp.arange(group // run, padded // run, dtype=own_runs.dtype)])
        bias = jnp.where(seen, 0.0, -1e30).astype(f32)
        chunk = math.gcd(total, CHUNK)
        chunks = total // chunk
        slot_seen = (own_path + own_hot > 0.5).astype(f32)
        slot_seen = jnp.pad(slot_seen, ((0, extra), (0, 0))).reshape(padded // TILE, TILE, slot_total)
        slot_seen = jnp.max(slot_seen, axis=1)
        in_chunk = (rank[:, None] * SEG // chunk == jnp.arange(chunks)[None, :]).astype(f32)
        visited = jnp.dot(slot_seen, in_chunk) > 0.5
        visits = jnp.sum(visited, axis=1).astype(jnp.int32)
        turn = jnp.cumsum(visited, axis=1) - 1
        listed = (turn[:, :, None] == jnp.arange(chunks)[None, None, :]) & visited[:, :, None]
        listed = jnp.sum(jnp.where(listed, jnp.arange(chunks)[None, :, None], 0), axis=1)
        tables = tuple(
            v.reshape(-1).astype(jnp.int32) for v in (listed, visits, key_runs, own_runs)
        )

        def padded_rows(v):
            return jnp.pad(v, ((0, extra), (0, 0)))

        shape = (ZN, KN, segs, run)
        zs, ks, gs, rs = (lax.broadcasted_iota(jnp.int32, shape, d) for d in range(4))
        lying_slot = ((zs * xn + x) * segs + gs).reshape(group)
        own_hot = (lying_slot[:, None] == slot_ids[None, :]).astype(f32)
        own_offset = ((y * KN + ks) * run + rs).reshape(group)
        position = jnp.dot(own_hot, depth_of[:, None], precision=lax.Precision.HIGHEST) * SEG
        position = position + own_offset[:, None].astype(f32)
        half_dim = HD // 2
        frequency = jnp.exp(-rope_log_base * jnp.arange(half_dim, dtype=f32) / half_dim)
        angles = position * frequency[None, :]
        cosine, sine = jnp.cos(angles), jnp.sin(angles)
        cosine = jnp.concatenate([cosine] * 4, axis=1)
        sine = jnp.concatenate([-sine, sine] * 2, axis=1)

        def rotate(v, sign):
            parts = [v[:, i * half_dim : (i + 1) * half_dim] for i in (1, 0, 3, 2)]
            return v * cosine + jnp.concatenate(parts, axis=1) * (sign * sine)

        gate_up_sent = packed([w_up * ffn_gain, w_gate * ffn_gain], 1)
        cot_mine = piece(cotangent)
        then(gate_up_sent, cot_mine, bias, cosine, sine, mix, *tables)
        output_y = in_order(take_all(output_sent), "y", yn)
        attn_z = in_order(take_all(sent), "z", ZN, 1)
        upper, lower = halved(attn_z)
        upper_out, lower_out = square_out(upper, "x", sizes), square_out(lower, "y", sizes)
        upper_side, lower_side = side_out(upper, "x", sizes), side_out(lower, "y", sizes)
        plain_sent = group_gather(after(plain_mine, attn_z))
        upper_on = square_on(take_all(upper_out), "x", sizes, upper_side)
        lower_on = square_on(take_all(lower_out), "y", sizes, lower_side)

        plain = take(plain_sent)
        up_sent, gate_sent = halved(gate_up_sent)
        down_sent = exchanged(after(down_sent, plain), "z", ZN)
        output_sent = exchanged(after(output_y, plain), "z", ZN)
        upper = joined_up(dict(zip(places, take_all([upper_on[p] for p in places]), strict=True)))
        lower = joined_up(dict(zip(places, take_all([lower_on[p] for p in places]), strict=True)))
        wqkv = jnp.concatenate([upper, lower])
        wqk, wv = wqkv[: 4 * HD], wqkv[4 * HD :]
        then(wqkv)
        logit_scale = 1.0 / math.sqrt(HD)
        key_own = then(rotate(fine(now(plain), wqk[2 * HD :], 1, 1), 1.0))
        key_sent = square_out(key_own, "x", sizes)
        value_own = then(fine(now(plain), wv, 1, 1))
        value_sent = square_out(value_own, "y", sizes)
        queries = rotate(fine(now(plain), wqk[: 2 * HD], 1, 1), 1.0)
        queries = then(padded_rows(queries * logit_scale))
        key_sent = square_on(take_all(key_sent), "x", sizes)
        value_sent = square_on(take_all(value_sent), "y", sizes)
        down_z = in_order(take_all(down_sent), "z", ZN, 1)
        up_sent = exchanged(after(up_sent, queries), "z", ZN)
        gate_sent = exchanged(after(gate_sent, down_z), "z", ZN)
        output_z = in_order(take_all(output_sent), "z", ZN, 1)
        key_list = take_all([key_sent[p] for p in places])
        value_list = take_all([value_sent[p] for p in places])
        up_w = in_order(take_all(up_sent), "z", ZN, 1)
        output_sent = direct(after(output_z, *value_list), xn, yn)
        down_z = after(down_z, *value_list)
        down_out, down_side = square_out(down_z, "x", sizes), side_out(down_z, "x", sizes)
        keys, values = jnp.concatenate(key_list), jnp.concatenate(value_list)
        contrast, stat = attend(run, mix, tables, now(queries), keys, values, bias)
        then(contrast)
        gate_w = in_order(take_all(gate_sent), "z", ZN, 1)
        output_sent = dict(zip(places, take_all([output_sent[p] for p in places]), strict=True))
        wo = joined_up(output_sent)
        contrast = now(contrast)[:group]
        head_scale = lax.rsqrt(jnp.mean(contrast * contrast, axis=1, keepdims=True) + epsilon)
        head_plain = contrast * head_scale
        joined = head_plain * head_gain * (1.0 - lambda_init)
        branch_part = then(fine(joined, wo))
        branch_sent = group_sum(branch_part)

        down_out, down_side = take_all(down_out), take_all(down_side)
        down_on = square_on(down_out, "x", sizes, down_side)
        up_w = after(up_w, *down_out)
        up_out, up_side = square_out(up_w, "y", sizes), side_out(up_w, "y", sizes)
        down_pieces = dict(zip(places, take_all([down_on[p] for p in places]), strict=True))
        up_side = take_all(up_side)
        gate_top, gate_low = halved(after(gate_w, *up_side))
        top_out, low_out = square_out(gate_top, "x", sizes), square_out(gate_low, "y", sizes)
        top_side, low_side = side_out(gate_top, "x", sizes), side_out(gate_low, "y", sizes)
        branch = take(branch_sent)
        residual = mine + from_distance_y(branch)
        ffn_scale = lax.rsqrt(jnp.mean(residual * residual, axis=1, keepdims=True) + epsilon)
        ffn_mine = then(residual * ffn_scale)
        ffn_sent = group_gather(ffn_mine)
        wd = then(tiled_up(down_pieces))
        top_out, low_side = take_all(top_out), take_all(low_side)
        up_on = square_on(take_all(up_out), "y", sizes, up_side)
        top_on = square_on(top_out, "x", sizes, top_side)
        low_on = square_on(take_all(low_out), "y", sizes, low_side)
        up_pieces = dict(zip(places, take_all([up_on[p] for p in places]), strict=True))
        ffn_plain = take(ffn_sent)
        cot_sent = group_gather(after(cot_mine, ffn_plain))
        wu = tiled_up(up_pieces)
        up_proj = then(fine(wu, ffn_plain, 1, 1))
        top_list = take_all([top_on[p] for p in places])
        low_list = take_all([low_on[p] for p in places])
        wg = tiled_up({p: jnp.concatenate(v) for p, *v in zip(places, top_list, low_list, strict=True)})

        gating = then(fine(wg, ffn_plain, 1, 1))
        gate = lax.logistic(gating)
        active = gating * gate
        hidden = active * up_proj
        cot = take(cot_sent)
        grad_hidden = fine(wd, cot, 1, 1)
        grad_up_proj = grad_hidden * active
        grad_gating = grad_hidden * up_proj * gate * (1.0 + gating * (1.0 - gate))
        grad_ffn_part = then(fine(grad_gating, wg, 0, 0) + fine(grad_up_proj, wu, 0, 0))
        grad_ffn_sent = group_sum(grad_ffn_part)
        down_grad = then(dot(now(hidden), cot))
        down_first = tiles(down_grad)
        down_sent = square_back(down_first, "x", sizes)
        up_grad = then(dot(now(grad_up_proj), ffn_plain))
        up_first = tiles(up_grad)
        up_sent = square_back(up_first, "y", sizes)
        gate_grad = then(dot(now(grad_gating), ffn_plain))
        gate_tiles = {p: halved(v) for p, v in tiles(gate_grad).items()}
        top_first = {p: v[0] for p, v in gate_tiles.items()}
        low_first = {p: v[1] for p, v in gate_tiles.items()}
        out_part = then(dot(now(hidden), wd, 0, 0))
        early = (xn - 1) * (yn - 1)
        down_sent[:early], up_sent[:early] = take_all(down_sent[:early]), take_all(up_sent[:early])
        down_first = square_added(down_first, down_sent[:early], "x", sizes)
        down_sent_on = square_back_on(down_first, "y", sizes)
        up_first = square_added(up_first, up_sent[:early], "y", sizes)
        up_sent_on = square_back_on(up_first, "x", sizes)
        then(*down_first[1:], *up_first[1:])
        scaled = take(grad_ffn_sent)
        grad_residual = cot_mine + ffn_scale * (
            scaled - ffn_mine * jnp.mean(scaled * ffn_mine, axis=1, keepdims=True)
        )
        grad_residual_attn = then(to_distance_y(grad_residual))
        grad_branch_sent = group_gather(grad_residual_attn)
        down_grad = sum(take_all(down_sent[early:]), down_first[0])
        up_grad = sum(take_all(up_sent[early:]), up_first[0])
        then(down_grad, up_grad)
        grad_branch = take(grad_branch_sent)

        out_sent = group_sum(after(out_part, grad_branch))
        grad_joined = fine(grad_branch, wo, 1, 1) * (1.0 - lambda_init)
        grad_head_gain = jnp.sum(grad_joined * head_plain, axis=0)
        scaled = grad_joined * head_gain
        grad_contrast = padded_rows(
            head_scale * (scaled - head_plain * jnp.mean(scaled * head_plain, axis=1, keepdims=True))
        )
        grad_contrast = then(grad_contrast)
        down_grad = sum(take_all(down_sent_on), down_grad)
        down_back = back_along_z([down_grad])
        up_grad = sum(take_all(up_sent_on), up_grad)
        up_back = back_along_z([up_grad])
        then(down_grad, up_grad)
        top_sent = square_back({p: after(v, down_grad) for p, v in top_first.items()}, "x", sizes)
        low_sent = square_back({p: after(v, up_grad) for p, v in low_first.items()}, "y", sizes)
        grad_contrast = now(grad_contrast)
        grad_queries, grad_keys, grad_values, inner = attend_back(
            run, mix, tables, queries, grad_contrast, stat, keys, values, bias
        )
        then(grad_queries, grad_keys, grad_values)
        rows_cut = lambda g: {p: g[i * group : (i + 1) * group] for i, p in enumerate(places)}
        key_first, value_first = rows_cut(grad_keys), rows_cut(grad_values)
        key_sent = square_back(key_first, "x", sizes)
        value_sent = square_back(value_first, "y", sizes)
        def reduced(v):
            return jnp.concatenate([jnp.max(v[:, :2], axis=0), jnp.sum(v[:, 2:], axis=0)])[None]

        peak = jnp.max(stat[2:4, :group], axis=1)
        every = jnp.concatenate([peak, grad_head_gain, -jnp.sum(inner[1:2, :group], axis=1)])[None]
        every_sent = home_along(every, "x", xn)
        top_first = square_added(top_first, take_all(top_sent), "x", sizes)
        low_first = square_added(low_first, take_all(low_sent), "y", sizes)
        then(*top_first, *low_first)
        key_first = square_added(key_first, take_all(key_sent), "x", sizes)
        key_sent = square_back_on(key_first, "y", sizes)
        value_first = square_added(value_first, take_all(value_sent), "y", sizes)
        value_sent = square_back_on(value_first, "x", sizes)
        then(*key_first, *value_first)
        every_sent = home_along(reduced(in_order(take_all(every_sent), "x", xn)), "y", yn)
        top_sent = square_back_on([after(v, *key_first) for v in top_first], "y", sizes)
        low_sent = square_back_on([after(v, *value_first) for v in low_first], "x", sizes)
        grad_q = rotate(grad_queries[:group] * logit_scale, -1.0)
        query_grad = dot(grad_q, plain, 0, 0)
        output_grad = dot(joined, grad_branch, 0, 0)
        then(query_grad, output_grad)
        down_back = in_order(take_all(down_back), "z", ZN)
        grad_k = rotate(sum(take_all(key_sent), key_first[0]), -1.0)
        grad_value_own = sum(take_all(value_sent), value_first[0])
        every = reduced(in_order(take_all(every_sent), "y", yn))
        every_sent = home_along(every, "k", KN)
        query_first, output_first = (
            cut(after(g, grad_k, grad_value_own)) for g in (query_grad, output_grad)
        )
        query_sent = square_back(query_first, "x", sizes)
        output_sent = square_back(output_first, "y", sizes)
        key_grad = then(dot(grad_k, plain, 0, 0))
        key_first = cut(key_grad)
        key_sent = square_back(key_first, "x", sizes)
        value_grad = then(dot(grad_value_own, plain, 0, 0))
        value_first = cut(value_grad)
        value_sent = square_back(value_first, "y", sizes)
        grad_qk = now(jnp.concatenate([grad_q, grad_k], axis=1))
        grad_part = then(dot(grad_qk, wqk) + dot(grad_value_own, wv))
        grad_attn_sent = group_sum(grad_part)

        every = in_order(take_all(every_sent), "k", KN)
        every = jnp.concatenate([every[:, :2].reshape(1, -1), jnp.sum(every[:, 2:], axis=0, keepdims=True)], axis=1)
        every_sent = home_along(every, "z", ZN)
        top_grad = sum(take_all(top_sent), top_first[0])
        low_grad = sum(take_all(low_sent), low_first[0])
        gate_back = back_along_z([jnp.concatenate([top_grad, low_grad])])
        query_first = square_added(query_first, take_all(query_sent), "x", sizes)
        query_sent = square_back_on(query_first, "y", sizes)
        output_first = square_added(output_first, take_all(output_sent), "y", sizes)
        output_sent = square_back_on(output_first, "x", sizes)
        then(*query_first, *output_first)
        key_first = square_added(key_first, take_all(key_sent), "x", sizes)
        key_sent = square_back_on(key_first, "y", sizes)
        value_first = square_added(value_first, take_all(value_sent), "y", sizes)
        value_sent = square_back_on(value_first, "x", sizes)
        then(*key_first, *value_first)
        every = in_order(take_all(every_sent), "z", ZN)
        up_back = in_order(take_all(up_back), "z", ZN)
        out_sum = take(out_sent)
        output = residual + out_sum
        out_sent = home_along(from_distance_x(output), "y", yn)
        query_grad = sum(take_all(query_sent), query_first[0])
        output_grad = sum(take_all(output_sent), output_first[0])
        early_sent = back_along_z([query_grad, output_grad])
        grad_down, grad_up = (v.T for v in now(down_back, up_back))
        then(grad_down, grad_up)
        key_grad = sum(take_all(key_sent), key_first[0])
        value_grad = sum(take_all(value_sent), value_first[0])
        late_sent = back_along_z([key_grad, value_grad])
        grad_gate = then(in_order(take_all(gate_back), "z", ZN).T)
        out_sent = home_along(in_order(take_all(out_sent), "y", yn), "k", KN)
        ffn_gain_part = then(rowsum(w_gate, grad_gate) + rowsum(w_up, grad_up))
        scaled = take(grad_attn_sent)
        grad_mine = grad_residual_attn + scale * (
            scaled - plain_mine * jnp.mean(scaled * plain_mine, axis=1, keepdims=True)
        )
        grad_mine = then(from_distance_x(from_distance_y(grad_mine)))
        tokens_sent = home_along(grad_mine, "y", yn)
        output = then(homed(in_order(take_all(out_sent), "k", KN)))
        early = in_order(take_all(early_sent), "z", ZN)
        early_sent = exchanged(early, "y", yn)
        tokens_sent = home_along(in_order(take_all(tokens_sent), "y", yn), "k", KN)
        late = in_order(take_all(late_sent), "z", ZN)
        late_sent = exchanged(late, "y", yn)
        grad_tokens = then(homed(in_order(take_all(tokens_sent), "k", KN)))
        by_block = lambda v, mats: v.reshape(BLOCKS, mats, 2 * HD, part_rows)
        held_w, held_early, held_late = by_block(attn_y, 3), by_block(early, 2), by_block(late, 2)
        attn_gain_part = (
            jnp.sum(held_w[:, 0] * held_early[:, 0], axis=(0, 1))
            + jnp.sum(held_w[:, 1] * held_late[:, 0], axis=(0, 1))
            + jnp.sum(held_w[:, 2] * held_late[:, 1], axis=(0, 1))
        )
        gains = then(jnp.concatenate([attn_gain_part, ffn_gain_part]))[None]
        gains_sent = home_along(gains, "k", KN)
        early = in_order(take_all(early_sent), "y", yn, 1)
        grad_query, grad_output = unpacked(early, 2, sub)
        then(grad_query, grad_output)
        gains = jnp.sum(in_order(take_all(gains_sent), "k", KN), axis=0, keepdims=True)
        gains_sent = home_along(gains, "y", yn)
        sums = jnp.sum(every[:, 2 * KN :], axis=0)
        size = gain_head.shape[0]
        grad_head_gain = lax.dynamic_slice_in_dim(sums[:VD], (z * xn + x) * size, size)
        grad_mix = sums[VD:]
        peak = every[:, : 2 * KN].reshape(yn, sub, KN, 2)
        maxima = jnp.transpose(peak, (0, 2, 1, 3)).reshape(2 * HEADS)
        late = in_order(take_all(late_sent), "y", yn, 1)
        grad_key, grad_value = unpacked(late, 2, sub)
        gains = in_order(take_all(gains_sent), "y", yn)
        grad_attn_gain = gains[:, :part_rows].reshape(-1)
        grad_ffn_gain = jnp.sum(gains[:, part_rows:], axis=0)
        factor = jnp.sqrt(tau[0] / jnp.maximum(maxima, tau[0]))
        mine_factor = lax.dynamic_slice_in_dim(factor, (y * KN + k) * 2 * sub, 2 * sub)
        wide_factor = jnp.repeat(mine_factor, HD)[None, :]
        return (
            output, grad_tokens, grad_query * attn_gain, grad_key * attn_gain, grad_value * attn_gain,
            grad_output, grad_attn_gain, grad_mix, grad_head_gain, grad_gate * ffn_gain,
            grad_up * ffn_gain, grad_down, grad_ffn_gain, maxima,
            w_query * wide_factor, w_key * wide_factor,
        )

    return shards


def solution(mesh):
    xn, yn = mesh.shape["row"] // ZN, mesh.shape["col"] // KN
    split = Mesh(mesh.devices.reshape(ZN, xn, yn, KN), ("z", "x", "y", "k"))
    row, col = ("z", "x"), ("y", "k")
    rows, both, vector = P(row, None), P(row, col), P(row)
    return jax.shard_map(
        layer(xn, yn),
        mesh=split,
        in_specs=(rows, rows, both, both, both, both, vector, vector, vector, vector, vector, vector,
                  both, both, both, vector, P(), P(), vector),
        out_specs=(rows, rows, both, both, both, both, vector, P(), vector, both, both, both, vector,
                   P(), both, both),
        check_vma=False,
    )
```

```python
import math

import jax
import jax.numpy as jnp
from jax import lax
from jax.experimental import pallas as pl
from jax.experimental.pallas import tpu as pltpu
from jax.sharding import Mesh
from jax.sharding import PartitionSpec as P

HEADS = 8
HD = 128
VD = 256
SEG = 64
ZN = 4
KN = 2
BLOCKS = ZN
TRUNK_SEGS = 8

epsilon = 1e-05
lambda_init = 0.2
rope_log_base = 9.210340371976184
high = lax.Precision.HIGH
highest = lax.Precision.HIGHEST
f32 = jnp.float32
bf16 = jnp.bfloat16
VMEM_BYTES = 60 * 1024 * 1024


def dot(a, b, contract_a=1, contract_b=0):
    return lax.dot_general(
        a, b, (((contract_a,), (contract_b,)), ((), ())), precision=high, preferred_element_type=f32
    )


def fine(a, b, contract_a=1, contract_b=0):
    return lax.dot_general(
        a, b, (((contract_a,), (contract_b,)), ((), ())), precision=highest, preferred_element_type=f32
    )


def thirds(v):
    top = v.astype(bf16)
    rest = v - top.astype(f32)
    low = rest.astype(bf16)
    return top, low, (rest - low.astype(f32)).astype(bf16)


def six(a, b):
    (a1, a2, a3), (b1, b2, b3) = a, b
    return mm(a1, b1) + (mm(a1, b2) + mm(a2, b1)) + (mm(a2, b2) + mm(a1, b3) + mm(a3, b1))


def halves(v):
    top = v.astype(bf16)
    return top, (v - top.astype(f32)).astype(bf16)


def mm(a, b):
    return jnp.dot(a, b, preferred_element_type=f32)


def after(v, *others):
    return lax.optimization_barrier((v,) + others)[0]


def shifted(v, axis, n, shift):
    return lax.ppermute(v, axis, [(i, (i + shift) % n) for i in range(n)])


def at(v, index, dim):
    return lax.dynamic_index_in_dim(v, index, dim, keepdims=False)


def part(v, index, rows):
    return lax.dynamic_slice_in_dim(v, index * rows, rows)


def exchanged(v, axis, n):
    i = lax.axis_index(axis)
    rows = v.shape[0] // n
    return [part(v, i, rows)] + [
        shifted(part(v, (i + s) % n, rows), axis, n, s) for s in range(1, n)
    ]


def in_order(pieces, axis, n, dim=0):
    i = lax.axis_index(axis)

    def source(j):
        shift = (i + n - j) % n
        out = pieces[0]
        for s in range(1, n):
            out = jnp.where(shift == s, pieces[s], out)
        return out

    return jnp.concatenate([source(j) for j in range(n)], axis=dim)


def small_gather(v, axis, n):
    return in_order([v[None]] + [shifted(v[None], axis, n, s) for s in range(1, n)], axis, n)


def small_fold(v, axis, n, fold):
    out = v
    for s in range(1, n):
        out = fold(out, shifted(v, axis, n, s))
    return out


def direct(v, xn, yn):
    out = {}
    for s in range(xn):
        for t in range(yn):
            pairs = [
                (a * yn + b, (a + s) % xn * yn + (b + t) % yn) for a in range(xn) for b in range(yn)
            ]
            out[s, t] = lax.ppermute(v, ("x", "y"), pairs) if s or t else v
    return out


def square_out(v, first, sizes):
    n = sizes[first]
    return [v] + [shifted(v, first, n, s) for s in range(1, n)]


def side_out(v, first, sizes):
    second = "y" if first == "x" else "x"
    n = sizes[second]
    return [shifted(v, second, n, t) for t in range(1, n)]


def square_on(came, first, sizes, side=None):
    second = "y" if first == "x" else "x"
    n = sizes[second]
    out = {}
    for s, v in enumerate(came):
        out[s, 0] = v
        for t in range(1, n):
            out[s, t] = side[t - 1] if side and s == 0 else shifted(v, second, n, t)
    return out if first == "x" else {(s, t): v for (t, s), v in out.items()}


def along_first(pieces, first):
    return pieces if first == "x" else {(t, s): v for (s, t), v in pieces.items()}


def square_back(pieces, first, sizes):
    m, n = sizes[first], sizes["y" if first == "x" else "x"]
    v = along_first(pieces, first)
    return [shifted(v[s, t], first, m, -s) for t in reversed(range(n)) for s in range(1, m)]


def square_added(pieces, came, first, sizes):
    m, n = sizes[first], sizes["y" if first == "x" else "x"]
    v = along_first(pieces, first)
    out = [v[0, t] for t in range(n)]
    order = [t for t in reversed(range(n)) for s in range(1, m)]
    for t, what in zip(order, came):
        out[t] = out[t] + what
    return out


def square_back_on(sums, second, sizes):
    n = sizes[second]
    return [shifted(sums[t], second, n, -t) for t in range(1, n)]


def table_kernel(sizes, shape, parent_ref, at_ref, seen_ref, count_ref, key_ref, own_ref, code_ref, depth_ref, order, rank, own):
    xn, yn, segs, run, pieces_run = sizes
    slots, own_slots, padded_slots, tiles, chunks = shape
    x, y = at_ref[0], at_ref[1]
    per_chunk, per_tile = slots // chunks, padded_slots // tiles

    def climb(s, carry):
        def step(i, now):
            above = parent_ref[now[0]]
            return above, now[1] + (above != now[0]).astype(jnp.int32)

        root, depth = lax.fori_loop(0, TRUNK_SEGS + 2, step, (s, jnp.int32(0)))
        depth_ref[s] = depth
        branch = jnp.where(depth == TRUNK_SEGS, s, parent_ref[s])
        past = (branch + 1) * (slots + 1) + jnp.where(depth > TRUNK_SEGS, s + 1, 0)
        place = jnp.where(depth < TRUNK_SEGS, depth, TRUNK_SEGS + past)
        order[s] = (root * (TRUNK_SEGS + (slots + 1) * (slots + 2)) + place) * slots + s
        return carry

    lax.fori_loop(0, slots, climb, 0)

    def place_slot(s, carry):
        here, mine = jnp.int32(0), jnp.int32(0)
        for t in range(slots):
            less = (order[t] < order[s]).astype(jnp.int32)
            here = here + less
            mine = mine + less * (t // segs % xn == x).astype(jnp.int32)
        rank[s] = here
        own[s] = mine
        zs = lax.div(s, xn * segs)
        xs = lax.rem(lax.div(s, segs), xn)
        for k in range(KN):
            row = (zs * KN + k) * segs + lax.rem(s, segs)
            for t in range(yn):
                piece = lax.rem(x + xn - xs, xn) * yn + lax.rem(y + yn - t, yn)
                key_ref[(here * yn + t) * KN + k] = piece * pieces_run + row

            @pl.when(xs == x)
            def _():
                own_ref[mine * KN + k] = row

        return carry

    lax.fori_loop(0, slots, place_slot, 0)
    for r in range(own_slots * KN, padded_slots * KN):
        own_ref[r] = jnp.int32(r)

    def clear(i, carry):
        for j in range(padded_slots):
            code_ref[i * padded_slots + j] = jnp.int32(0 if j < own_slots else 1)
        return carry

    lax.fori_loop(0, slots, clear, 0)

    def mark(s, carry):
        @pl.when(lax.rem(lax.div(s, segs), xn) == x)
        def _():
            def step(i, now):
                code_ref[rank[now] * padded_slots + own[s]] = jnp.int32(1)
                return parent_ref[now]

            lax.fori_loop(0, TRUNK_SEGS + 2, step, parent_ref[s])
            code_ref[rank[s] * padded_slots + own[s]] = jnp.int32(2)

        return carry

    lax.fori_loop(0, slots, mark, 0)

    def visit(tile, carry):
        def look(c, count):
            some = jnp.int32(0)
            for i in range(per_chunk):
                for j in range(per_tile):
                    at = tile * per_tile + j
                    code = code_ref[(c * per_chunk + i) * padded_slots + at]
                    some = some | jnp.where(at < own_slots, code, 0)

            @pl.when(some > 0)
            def _():
                seen_ref[tile * chunks + count] = c

            return count + (some > 0).astype(jnp.int32)

        count_ref[tile] = lax.fori_loop(0, chunks, look, jnp.int32(0))
        return carry

    lax.fori_loop(0, tiles, visit, 0)


def mask(code_ref, y, run, tile, c, chunk, padded_slots):
    wide = KN * run
    per_tile = TILE // wide
    lane = lax.broadcasted_iota(jnp.int32, (1, TILE), 1)
    row = lax.broadcasted_iota(jnp.int32, (SEG, TILE), 0)
    which = lax.div(lane, wide)
    offset = y * wide + lax.rem(lane, wide)
    blocks = []
    for i in range(chunk // SEG):
        code = jnp.zeros((1, TILE), jnp.int32)
        for j in range(per_tile):
            one = code_ref[(c * (chunk // SEG) + i) * padded_slots + tile * per_tile + j]
            code = jnp.where(which == j, one, code)
        last = jnp.where(code == 0, -1, jnp.where(code == 1, SEG, offset))
        blocks.append(jnp.where(row <= last, 0.0, -1e30).astype(f32))
    return jnp.concatenate(blocks, axis=0)


def logits_chunk(keys_wide, queries, rows, j):
    first, last = keys_wide[0, j, rows, :], keys_wide[1, j, rows, :]
    top, low, rest = queries[j]
    return mm(first, top) + (mm(first, low) + mm(last, rest))


def split_keys(keys, keys_wide, rows):
    for j in range(2):
        top, low, rest = thirds(keys[:, j * HD : (j + 1) * HD])
        keys_wide[0, j, rows, :HD] = top
        keys_wide[0, j, rows, HD:] = low
        keys_wide[1, j, rows, :HD] = top
        keys_wide[1, j, rows, HD:] = rest


def split_queries(q):
    out = []
    for j in range(2):
        top, low, rest = thirds(q[:, j * HD : (j + 1) * HD].T)
        out.append([jnp.concatenate(p, axis=0) for p in ((top, top), (low, low), (rest, top))])
    return out


def chunk_rows(c, size):
    return pl.ds(pl.multiple_of(c * size, size), size)


def brought(run, start_ref, first, count, source, target):
    def move(i, carry):
        target[chunk_rows(i, run), :] = source[chunk_rows(start_ref[first + i], run), :]
        return carry

    lax.fori_loop(0, count, move, 0)


def taken_back(run, start_ref, first, count, source, target):
    def move(i, carry):
        target[chunk_rows(start_ref[first + i], run), :] = source[chunk_rows(i, run), :]
        return carry

    lax.fori_loop(0, count, move, 0)


def forward_kernel(
    run, mix_ref, at_ref, seen_ref, count_ref, key_ref, own_ref, code_ref, q_ref, k_ref, v_ref,
    o_ref, stat_ref, keys_wide, vt, held, sorted_rows, sorted_q,
):
    total = k_ref.shape[0]
    chunk = vt.shape[3]
    count = total // chunk
    tile = pl.program_id(0)

    @pl.when(tile == 0)
    def _():
        brought(run, own_ref, 0, q_ref.shape[0] // run, q_ref, sorted_q)
        brought(run, key_ref, 0, total // run, k_ref, sorted_rows)

        def split(c, carry):
            rows = chunk_rows(c, chunk)
            split_keys(sorted_rows[rows, :], keys_wide, rows)
            return carry

        lax.fori_loop(0, count, split, 0)
        brought(run, key_ref, 0, total // run, v_ref, sorted_rows)

        def turn(c, carry):
            for i, p in enumerate(thirds(sorted_rows[chunk_rows(c, chunk), :].T)):
                vt[i, c] = p
            return carry

        lax.fori_loop(0, count, turn, 0)

    split = split_queries(sorted_q[chunk_rows(tile, TILE), :])
    visits = count_ref[tile]

    padded_slots = q_ref.shape[0] // (KN * run)

    def score(i, peaks):
        c = seen_ref[tile * count + i]
        rows = chunk_rows(c, chunk)
        bias = mask(code_ref, at_ref[1], run, tile, c, chunk, padded_slots)
        out = []
        for j in range(2):
            s = logits_chunk(keys_wide, split, rows, j) + bias
            held[j, rows, :] = s
            out.append(jnp.maximum(peaks[j], jnp.max(s, axis=0, keepdims=True)))
        return tuple(out)

    peaks = lax.fori_loop(0, visits, score, (jnp.full((1, TILE), -1e30, f32),) * 2)

    def weigh(i, sums):
        rows = chunk_rows(seen_ref[tile * count + i], chunk)
        out = []
        for j in range(2):
            w = jnp.exp(held[j, rows, :] - peaks[j])
            held[j, rows, :] = w
            out.append(sums[j] + jnp.sum(w, axis=0, keepdims=True))
        return tuple(out)

    sums = lax.fori_loop(0, visits, weigh, (jnp.zeros((1, TILE), f32),) * 2)
    first, second = 1.0 / sums[0], mix_ref[0] / sums[1]

    def collect(i, acc):
        c = seen_ref[tile * count + i]
        rows = chunk_rows(c, chunk)
        both = thirds(held[0, rows, :] * first - held[1, rows, :] * second)
        return acc + six([vt[i, c] for i in range(3)], both)

    out = lax.fori_loop(0, visits, collect, jnp.zeros((VD, TILE), f32)).T
    for i in range(TILE // run):
        o_ref[chunk_rows(own_ref[tile * (TILE // run) + i], run), :] = out[i * run : (i + 1) * run, :]
    for j in range(2):
        stat_ref[j : j + 1, :] = peaks[j] + jnp.log(sums[j])
        stat_ref[2 + j : 3 + j, :] = peaks[j]
    stat_ref[4:8, :] = jnp.zeros((4, TILE), f32)


def backward_kernel(
    run, mix_ref, at_ref, seen_ref, count_ref, key_ref, own_ref, code_ref, q_ref, dc_ref, stat_ref, k_ref, v_ref,
    dq_ref, dk_ref, dv_ref, inner_ref, keys_wide, kt, held, cross, sorted_v, sorted_q, sorted_dc,
):
    total = k_ref.shape[0]
    chunk = kt.shape[3]
    count = total // chunk
    mix = mix_ref[0]
    tile = pl.program_id(0)

    @pl.when(tile == 0)
    def _():
        brought(run, own_ref, 0, q_ref.shape[0] // run, q_ref, sorted_q)
        brought(run, own_ref, 0, q_ref.shape[0] // run, dc_ref, sorted_dc)
        brought(run, key_ref, 0, total // run, k_ref, sorted_v)

        def prepare(c, carry):
            rows = chunk_rows(c, chunk)
            keys = sorted_v[rows, :]
            split_keys(keys, keys_wide, rows)
            for i, p in enumerate(halves(keys.T)):
                kt[i, c] = p
            dk_ref[rows, :] = jnp.zeros(keys.shape, f32)
            dv_ref[rows, :] = jnp.zeros(keys.shape, f32)
            return carry

        lax.fori_loop(0, count, prepare, 0)
        brought(run, key_ref, 0, total // run, v_ref, sorted_v)

    queries, cotangents = sorted_q[chunk_rows(tile, TILE), :], sorted_dc[chunk_rows(tile, TILE), :]
    split = split_queries(queries)
    dct = thirds(cotangents.T)
    dc_top, dc_low = halves(cotangents)
    dc_wide = jnp.concatenate([dc_top, dc_top], axis=0)
    q_top, q_low = halves(queries)
    q_wide = jnp.concatenate([q_top, q_top], axis=0)
    norms = [stat_ref[j : j + 1, :] for j in range(2)]
    visits = count_ref[tile]

    padded_slots = q_ref.shape[0] // (KN * run)

    def first(i, inner):
        c = seen_ref[tile * count + i]
        rows = chunk_rows(c, chunk)
        bias = mask(code_ref, at_ref[1], run, tile, c, chunk, padded_slots)
        both = six(thirds(sorted_v[rows, :]), dct)
        cross[rows, :] = both
        out, probs = [], []
        for j in range(2):
            p = jnp.exp(logits_chunk(keys_wide, split, rows, j) + bias - norms[j])
            held[j, rows, :] = p
            probs.append(p)
            out.append(inner[j] + jnp.sum(p * both, axis=0, keepdims=True))
        top, low = halves(probs[0] - mix * probs[1])
        dv_ref[rows, :] += mm(jnp.concatenate([top, low], axis=1), dc_wide) + mm(top, dc_low)
        return tuple(out)

    inner = lax.fori_loop(0, visits, first, (jnp.zeros((1, TILE), f32),) * 2)

    def second(i, acc):
        c = seen_ref[tile * count + i]
        rows = chunk_rows(c, chunk)
        both = cross[rows, :]
        out = []
        for j in range(2):
            d = held[j, rows, :] * (both - inner[j])
            if j == 1:
                d = d * (-mix)
            top, low = halves(d)
            cols = slice(j * HD, (j + 1) * HD)
            dk_ref[rows, cols] += mm(jnp.concatenate([top, low], axis=1), q_wide[:, cols]) + mm(
                top, q_low[:, cols]
            )
            kt_top, kt_low = kt[0, c, cols, :], kt[1, c, cols, :]
            out.append(acc[j] + (mm(kt_top, top) + (mm(kt_top, low) + mm(kt_low, top))))
        return tuple(out)

    dq = lax.fori_loop(0, visits, second, (jnp.zeros((HD, TILE), f32),) * 2)
    dq = jnp.concatenate(dq, axis=0).T
    for i in range(TILE // run):
        dq_ref[chunk_rows(own_ref[tile * (TILE // run) + i], run), :] = dq[i * run : (i + 1) * run, :]
    for j in range(2):
        inner_ref[j : j + 1, :] = inner[j]
    inner_ref[2:8, :] = jnp.zeros((6, TILE), f32)

    @pl.when(tile == pl.num_programs(0) - 1)
    def _():
        for ref in (dk_ref, dv_ref):

            def keep(c, carry):
                rows = chunk_rows(c, chunk)
                sorted_v[rows, :] = ref[rows, :]
                return carry

            lax.fori_loop(0, count, keep, 0)
            taken_back(run, key_ref, 0, total // run, sorted_v, ref)


TILE = 128
CHUNK = 256


def whole():
    return pl.BlockSpec(memory_space=pltpu.VMEM)


def table():
    return pl.BlockSpec(memory_space=pltpu.SMEM)


def tables_of(sizes, shape, parent_slot, place):
    slots, own_slots, padded_slots, tiles, chunks = shape
    yn = sizes[1]
    counts = (tiles * chunks, tiles, slots * yn * KN, padded_slots * KN, slots * padded_slots, slots)
    return pl.pallas_call(
        lambda *refs: table_kernel(sizes, shape, *refs),
        in_specs=[table()] * 2,
        out_specs=[table()] * len(counts),
        out_shape=[jax.ShapeDtypeStruct((n,), jnp.int32) for n in counts],
        scratch_shapes=[pltpu.SMEM((slots,), jnp.int32)] * 3,
        name="tables",
    )(parent_slot, place)


def attend(run, mix, tables, queries, keys, values):
    total, count = keys.shape[0], queries.shape[0]
    chunk = math.gcd(total, CHUNK)
    lanes = lambda rows: pl.BlockSpec((rows, TILE), lambda i: (0, i))
    return pl.pallas_call(
        lambda *refs: forward_kernel(run, *refs),
        grid=(count // TILE,),
        in_specs=[table()] * 7 + [whole()] * 3,
        out_specs=[whole(), lanes(8)],
        out_shape=[
            jax.ShapeDtypeStruct((count, VD), f32), jax.ShapeDtypeStruct((8, count), f32),
        ],
        scratch_shapes=[
            pltpu.VMEM((2, 2, total, 2 * HD), bf16),
            pltpu.VMEM((3, total // chunk, VD, chunk), bf16),
            pltpu.VMEM((2, total, TILE), f32),
            pltpu.VMEM((total, 2 * HD), f32),
            pltpu.VMEM((count, 2 * HD), f32),
        ],
        compiler_params=pltpu.CompilerParams(vmem_limit_bytes=VMEM_BYTES),
        cost_estimate=pl.CostEstimate(flops=4 * 10**10, bytes_accessed=0, transcendentals=0),
        name="attend",
    )(mix, *tables, queries, keys, values)


def attend_back(run, mix, tables, queries, contrast, stat, keys, values):
    total, count = keys.shape[0], queries.shape[0]
    chunk = math.gcd(total, CHUNK)
    lanes = lambda rows: pl.BlockSpec((rows, TILE), lambda i: (0, i))
    return pl.pallas_call(
        lambda *refs: backward_kernel(run, *refs),
        grid=(count // TILE,),
        in_specs=[table()] * 7 + [whole()] * 2 + [lanes(8)] + [whole()] * 2,
        out_specs=[whole(), whole(), whole(), lanes(8)],
        out_shape=[
            jax.ShapeDtypeStruct((count, 2 * HD), f32),
            jax.ShapeDtypeStruct((total, 2 * HD), f32),
            jax.ShapeDtypeStruct((total, VD), f32),
            jax.ShapeDtypeStruct((8, count), f32),
        ],
        scratch_shapes=[
            pltpu.VMEM((2, 2, total, 2 * HD), bf16),
            pltpu.VMEM((2, total // chunk, 2 * HD, chunk), bf16),
            pltpu.VMEM((2, total, TILE), f32),
            pltpu.VMEM((total, TILE), f32),
            pltpu.VMEM((total, VD), f32),
            pltpu.VMEM((count, 2 * HD), f32),
            pltpu.VMEM((count, VD), f32),
        ],
        compiler_params=pltpu.CompilerParams(vmem_limit_bytes=VMEM_BYTES),
        cost_estimate=pl.CostEstimate(flops=4 * 10**10, bytes_accessed=0, transcendentals=0),
        name="attend_back",
    )(mix, *tables, queries, contrast, stat, keys, values)


def layer(xn, yn):
    sizes = {"x": xn, "y": yn}
    places = [(s, t) for s in range(xn) for t in range(yn)]

    def shards(
        tokens, cotangent, w_query, w_key, w_value, w_output, gain_attn, lambda_query_first,
        lambda_key_first, lambda_query_second, lambda_key_second, gain_head, w_gate, w_up, w_down,
        gain_ffn, tau, parent_slot, depth,
    ):
        z, x, y, k = (lax.axis_index(a) for a in "zxyk")
        home_rows, width = tokens.shape
        segs = home_rows // SEG
        run = SEG // (yn * KN)
        piece_rows = segs * run
        group = ZN * KN * piece_rows
        sub = BLOCKS // yn
        held_rows = w_query.shape[0]
        part_rows = held_rows // yn
        square_rows = ZN * part_rows
        total = ZN * xn * home_rows
        slot_total = parent_slot.shape[0]
        hidden_cols = w_gate.shape[1] // sub

        def block(v, i):
            return v[:, i * part_rows : (i + 1) * part_rows]

        def by_index(i, n, order):
            out = order(0)
            for j in range(1, n):
                out = jnp.where(i == j, order(j), out)
            return out

        def to_distance_x(v):
            return by_index(x, xn, lambda j: jnp.concatenate(
                [block(v, (c * xn + (j + xn - s) % xn) * yn + t)
                 for s in range(xn) for c in range(ZN) for t in range(yn)], axis=1))

        def from_distance_x(v):
            return by_index(x, xn, lambda j: jnp.concatenate(
                [block(v, ((j + xn - a) % xn * ZN + c) * yn + t)
                 for c in range(ZN) for a in range(xn) for t in range(yn)], axis=1))

        def to_distance_y(v):
            return by_index(y, yn, lambda j: jnp.concatenate(
                [block(v, (s * ZN + c) * yn + (j + yn - t) % yn)
                 for s in range(xn) for t in range(yn) for c in range(ZN)], axis=1))

        def from_distance_y(v):
            return by_index(y, yn, lambda j: jnp.concatenate(
                [block(v, (s * yn + (j + yn - t) % yn) * ZN + c)
                 for s in range(xn) for c in range(ZN) for t in range(yn)], axis=1))

        def piece(v):
            v = v.reshape(segs, yn * KN, run, width)
            return to_distance_x(at(v, y * KN + k, 1).reshape(piece_rows, width))

        def home_along(v, axis, n):
            return [v] + [shifted(v, axis, n, s) for s in range(1, n)]

        def homed(v):
            v = v.reshape(KN, yn, segs, run, width)
            return jnp.transpose(v, (2, 1, 0, 3, 4)).reshape(home_rows, width)

        def group_gather(v):
            return lax.all_gather(v, ("z", "k"), axis=0, tiled=True)

        def group_sum(v):
            return lax.psum_scatter(v, ("z", "k"), scatter_dimension=0, tiled=True)

        def packed(mats, blocks):
            rows = mats[0].shape[1] // blocks
            mats = [m.T for m in mats]
            return jnp.concatenate([m[s * rows : (s + 1) * rows] for s in range(blocks) for m in mats])

        def lanes(v, index, size):
            return lax.dynamic_slice_in_dim(v, index * size, size, 1)

        def along_y(v):
            mine = lanes(v, y, part_rows)
            return [mine] + [shifted(lanes(v, (y + s) % yn, part_rows), "y", yn, s) for s in range(1, yn)]

        def back_along_z(mats):
            v = jnp.concatenate(mats)
            size = v.shape[1] // ZN
            mine = lanes(v, z, size)
            return [mine] + [shifted(lanes(v, (z + s) % ZN, size), "z", ZN, s) for s in range(1, ZN)]

        def unpacked(v, mats, blocks):
            cols = v.shape[0] // (blocks * mats)
            part = lambda s, m: v[(s * mats + m) * cols : (s * mats + m + 1) * cols]
            return [jnp.concatenate([part(s, m) for s in range(blocks)]).T for m in range(mats)]

        def joined_up(pieces):
            return jnp.concatenate([pieces[p] for p in places], axis=1)

        def cut(g):
            return {p: g[:, i * square_rows : (i + 1) * square_rows] for i, p in enumerate(places)}

        def tiled_up(pieces):
            return jnp.concatenate(
                [jnp.concatenate([pieces[s, t] for s in range(xn)], axis=1) for t in range(yn)]
            )

        def tiles(g):
            r, c = g.shape[0] // yn, g.shape[1] // xn
            return {(s, t): g[t * r : (t + 1) * r, s * c : (s + 1) * c] for s, t in places}

        def halved(v):
            mid = v.shape[0] // 2
            return v[:mid], v[mid:]

        def rowsum(w, g):
            return jnp.sum(w * g, axis=1)

        last = []

        def now(*v):
            out = lax.optimization_barrier(tuple(v) + tuple(last))[: len(v)]
            return out[0] if len(v) == 1 else out

        def then(*v):
            last[:] = v
            return v[0] if len(v) == 1 else v

        def take(*v):
            out = now(*v)
            return then(*(out if len(v) > 1 else (out,)))

        def take_all(pieces):
            out = lax.optimization_barrier(tuple(pieces) + tuple(last))[: len(pieces)]
            then(*out)
            return list(out)

        attn_gain, ffn_gain = gain_attn[:, None], gain_ffn[:, None]
        sent = along_y(packed([w_query, w_key, w_value], sub))
        small = jnp.concatenate(
            [gain_head, lambda_query_first, lambda_key_first, lambda_query_second, lambda_key_second]
        )
        small_sent = home_along(small[None], "x", xn)
        attn_y = in_order(take_all(sent), "y", yn)
        y_gain = part(gain_attn, y, part_rows)[None, :]
        sent = exchanged(attn_y * y_gain, "z", ZN)
        output_sent = along_y(after(packed([w_output], sub), attn_y))
        sent[: 2] = take_all(sent[: 2])
        padded = -(-group // TILE) * TILE
        own_slots = ZN * segs
        chunks = total // math.gcd(total, CHUNK)
        *tables, depth_of = tables_of(
            (xn, yn, segs, run, group // run),
            (slot_total, own_slots, padded // (KN * run), padded // TILE, chunks),
            now(parent_slot), jnp.stack([x, y]),
        )
        tables = [jnp.stack([x, y])] + tables
        mine = piece(now(tokens))
        scale = lax.rsqrt(jnp.mean(mine * mine, axis=1, keepdims=True) + epsilon)
        plain_mine = then(to_distance_y(mine) * scale)
        down_sent = now(w_down).T
        then(down_sent, plain_mine, *tables)
        small = in_order(take_all(small_sent), "x", xn).reshape(1, -1)
        small_sent = home_along(small, "z", ZN)
        output_y = in_order(take_all(output_sent), "y", yn)
        shares = down_sent.shape[1] // part_rows
        output_y = output_y.reshape(BLOCKS, shares, VD // shares, part_rows)
        output_y = jnp.concatenate([output_y[:, i] for i in range(shares)], axis=2)
        output_down = jnp.concatenate(
            [output_y, down_sent.reshape(BLOCKS, -1, down_sent.shape[1])], axis=1
        ).reshape(-1, down_sent.shape[1])
        then(output_down)
        attn_z = in_order(sent[:2] + take_all(sent[2:]), "z", ZN, 1)
        upper, lower = halved(attn_z)
        upper_out, lower_out = square_out(upper, "x", sizes), square_out(lower, "y", sizes)
        upper_side, lower_side = side_out(upper, "x", sizes), side_out(lower, "y", sizes)
        plain_sent = group_gather(after(plain_mine, attn_z))
        upper_on = square_on(take_all(upper_out), "x", sizes, upper_side)
        lower_on = square_on(take_all(lower_out), "y", sizes, lower_side)

        small = in_order(take_all(small_sent), "z", ZN).reshape(ZN * xn, -1)
        n_gain, n_lambda = gain_head.shape[0], lambda_key_first.shape[0]
        head_gain = small[:, :n_gain].reshape(1, -1)
        query_first, key_first, query_second, key_second = (
            small[:, n_gain + i * n_lambda : n_gain + (i + 1) * n_lambda] for i in range(4)
        )
        mix = (
            jnp.exp(jnp.sum(query_first * key_first))
            - jnp.exp(jnp.sum(query_second * key_second))
            + lambda_init
        ).reshape(1)

        def padded_rows(v):
            return jnp.pad(v, ((0, padded - group), (0, 0)))

        shape = (ZN, KN, segs, run)
        ks, rs = (lax.broadcasted_iota(jnp.int32, shape, d) for d in (1, 3))
        depths = at(depth_of.reshape(ZN, xn, segs), x, 1)[:, None, :, None]
        position = (depths * SEG + (y * KN + ks) * run + rs).reshape(group, 1).astype(f32)
        half_dim = HD // 2
        frequency = jnp.exp(-rope_log_base * jnp.arange(half_dim, dtype=f32) / half_dim)
        angles = position * frequency[None, :]
        cosine, sine = jnp.cos(angles), jnp.sin(angles)
        cosine = jnp.concatenate([cosine] * 4, axis=1)
        sine = jnp.concatenate([-sine, sine] * 2, axis=1)

        def rotate(v, sign):
            parts = [v[:, i * half_dim : (i + 1) * half_dim] for i in (1, 0, 3, 2)]
            return v * cosine + jnp.concatenate(parts, axis=1) * (sign * sine)

        cot_mine = piece(cotangent)
        upper = joined_up(dict(zip(places, take_all([upper_on[p] for p in places]), strict=True)))
        lower = joined_up(dict(zip(places, take_all([lower_on[p] for p in places]), strict=True)))
        plain = take(plain_sent)
        down_sent = exchanged(after(output_down, plain), "z", ZN)
        cot_sent = group_gather(after(cot_mine, plain))
        wqkv = jnp.concatenate([upper, lower])
        wqk, wv = wqkv[: 4 * HD], wqkv[4 * HD :]
        then(wqkv)
        logit_scale = 1.0 / math.sqrt(HD)
        key_own = then(rotate(fine(now(plain), wqk[2 * HD :], 1, 1), 1.0))
        key_sent = square_out(key_own, "x", sizes)
        value_own = then(fine(now(plain), wv, 1, 1))
        value_sent = square_out(value_own, "y", sizes)
        queries = rotate(fine(now(plain), wqk[: 2 * HD], 1, 1), 1.0)
        queries = then(padded_rows(queries * logit_scale))
        gate_up_sent = packed([now(w_up) * ffn_gain, now(w_gate) * ffn_gain], BLOCKS)
        then(queries, gate_up_sent)
        key_sent = square_on(take_all(key_sent), "x", sizes)
        value_sent = square_on(take_all(value_sent), "y", sizes)
        came = take_all(down_sent)
        output_rows = VD // shares
        down_z = in_order([v[output_rows:] for v in came], "z", ZN, 1)
        output_z = in_order(
            [
                jnp.concatenate([v[:output_rows, i * part_rows : (i + 1) * part_rows] for i in range(shares)])
                for v in came
            ],
            "z", ZN, 1,
        )
        gate_up_sent = exchanged(after(gate_up_sent, down_z), "z", ZN)
        key_list = take_all([key_sent[p] for p in places])
        value_list = take_all([value_sent[p] for p in places])
        output_sent = direct(after(output_z, *value_list), xn, yn)
        down_z = after(down_z, *value_list)
        down_out, down_side = square_out(down_z, "x", sizes), side_out(down_z, "x", sizes)
        keys, values = jnp.concatenate(key_list), jnp.concatenate(value_list)
        cot = take(cot_sent)
        contrast, stat = attend(run, mix, tables, now(queries), keys, values)
        then(contrast)
        gate_up_sent = take_all(gate_up_sent)
        output_sent = dict(zip(places, take_all([output_sent[p] for p in places]), strict=True))
        wo = joined_up(output_sent)
        contrast = now(contrast)[:group]
        head_scale = lax.rsqrt(jnp.mean(contrast * contrast, axis=1, keepdims=True) + epsilon)
        head_plain = contrast * head_scale
        joined = head_plain * head_gain * (1.0 - lambda_init)
        branch_part = then(fine(joined, wo))
        branch_sent = group_sum(branch_part)
        up_w, gate_w = halved(in_order(gate_up_sent, "z", ZN, 1))

        down_out, down_side = take_all(down_out), take_all(down_side)
        down_on = square_on(down_out, "x", sizes, down_side)
        up_w = after(up_w, *down_out)
        up_out, up_side = square_out(up_w, "y", sizes), side_out(up_w, "y", sizes)
        down_pieces = dict(zip(places, take_all([down_on[p] for p in places]), strict=True))
        up_side = take_all(up_side)
        gate_top, gate_low = halved(after(gate_w, *up_side))
        top_out, low_out = square_out(gate_top, "x", sizes), square_out(gate_low, "y", sizes)
        top_side, low_side = side_out(gate_top, "x", sizes), side_out(gate_low, "y", sizes)
        branch = take(branch_sent)
        residual = mine + from_distance_y(branch)
        ffn_scale = lax.rsqrt(jnp.mean(residual * residual, axis=1, keepdims=True) + epsilon)
        ffn_mine = then(residual * ffn_scale)
        ffn_sent = group_gather(ffn_mine)
        wd = tiled_up(down_pieces)
        grad_hidden = then(fine(wd, cot, 1, 1))
        top_out, low_side = take_all(top_out), take_all(low_side)
        up_on = square_on(take_all(up_out), "y", sizes, up_side)
        top_on = square_on(top_out, "x", sizes, top_side)
        low_on = square_on(take_all(low_out), "y", sizes, low_side)
        up_pieces = dict(zip(places, take_all([up_on[p] for p in places]), strict=True))
        ffn_plain = take(ffn_sent)
        top_list = take_all([top_on[p] for p in places])
        low_list = take_all([low_on[p] for p in places])
        wug = jnp.concatenate(
            [
                jnp.concatenate([v[s, t] for s in range(xn)], axis=1)
                for t in range(yn)
                for v in (up_pieces,)
            ]
            + [
                jnp.concatenate([v[s, t] for s in range(xn)], axis=1)
                for t in range(yn)
                for v in (dict(zip(places, top_list, strict=True)), dict(zip(places, low_list, strict=True)))
            ]
        )

        both = fine(wug, ffn_plain, 1, 1)
        up_proj, gating = halved(both)
        gate = lax.logistic(gating)
        active = gating * gate
        hidden = active * up_proj
        grad_both = jnp.concatenate(
            [grad_hidden * active, grad_hidden * up_proj * gate * (1.0 + gating * (1.0 - gate))]
        )
        grad_ffn_part = then(fine(grad_both, wug, 0, 0))
        grad_up_proj, grad_gating = halved(grad_both)
        grad_ffn_sent = group_sum(grad_ffn_part)
        down_grad = then(dot(now(hidden), cot))
        down_first = tiles(down_grad)
        down_sent = square_back(down_first, "x", sizes)
        up_grad = then(dot(now(grad_up_proj), ffn_plain))
        up_first = tiles(up_grad)
        up_sent = square_back(up_first, "y", sizes)
        gate_grad = then(dot(now(grad_gating), ffn_plain))
        gate_tiles = {p: halved(v) for p, v in tiles(gate_grad).items()}
        top_first = {p: v[0] for p, v in gate_tiles.items()}
        low_first = {p: v[1] for p, v in gate_tiles.items()}
        out_part = then(dot(now(hidden), wd, 0, 0))
        early = (xn - 1) * (yn - 1)
        down_sent[:early], up_sent[:early] = take_all(down_sent[:early]), take_all(up_sent[:early])
        down_first = square_added(down_first, down_sent[:early], "x", sizes)
        down_sent_on = square_back_on(down_first, "y", sizes)
        up_first = square_added(up_first, up_sent[:early], "y", sizes)
        up_sent_on = square_back_on(up_first, "x", sizes)
        then(*down_first[1:], *up_first[1:])
        scaled = take(grad_ffn_sent)
        grad_residual = cot_mine + ffn_scale * (
            scaled - ffn_mine * jnp.mean(scaled * ffn_mine, axis=1, keepdims=True)
        )
        grad_residual_attn = then(to_distance_y(grad_residual))
        grad_branch_sent = group_gather(grad_residual_attn)
        down_grad = sum(take_all(down_sent[early:]), down_first[0])
        up_grad = sum(take_all(up_sent[early:]), up_first[0])
        then(down_grad, up_grad)
        grad_branch = take(grad_branch_sent)

        out_sent = group_sum(after(out_part, grad_branch))
        grad_joined = fine(grad_branch, wo, 1, 1) * (1.0 - lambda_init)
        grad_head_gain = jnp.sum(grad_joined * head_plain, axis=0)
        scaled = grad_joined * head_gain
        grad_contrast = padded_rows(
            head_scale * (scaled - head_plain * jnp.mean(scaled * head_plain, axis=1, keepdims=True))
        )
        grad_contrast = then(grad_contrast)
        down_grad = sum(take_all(down_sent_on), down_grad)
        down_back = back_along_z([down_grad])
        up_grad = sum(take_all(up_sent_on), up_grad)
        up_back = back_along_z([up_grad])
        then(down_grad, up_grad)
        top_sent = square_back({p: after(v, down_grad) for p, v in top_first.items()}, "x", sizes)
        low_sent = square_back({p: after(v, up_grad) for p, v in low_first.items()}, "y", sizes)
        grad_contrast = now(grad_contrast)
        grad_queries, grad_keys, grad_values, inner = attend_back(
            run, mix, tables, queries, grad_contrast, stat, keys, values
        )
        then(grad_queries, grad_keys, grad_values)
        rows_cut = lambda g: {p: g[i * group : (i + 1) * group] for i, p in enumerate(places)}
        key_first, value_first = rows_cut(grad_keys), rows_cut(grad_values)
        key_sent = square_back(key_first, "x", sizes)
        value_sent = square_back(value_first, "y", sizes)
        def reduced(v):
            return jnp.concatenate([jnp.max(v[:, :2], axis=0), jnp.sum(v[:, 2:], axis=0)])[None]

        peak = jnp.max(stat[2:4, :group], axis=1)
        every = jnp.concatenate([peak, grad_head_gain, -jnp.sum(inner[1:2, :group], axis=1)])[None]
        every_sent = home_along(every, "x", xn)
        top_first = square_added(top_first, take_all(top_sent), "x", sizes)
        low_first = square_added(low_first, take_all(low_sent), "y", sizes)
        then(*top_first, *low_first)
        key_first = square_added(key_first, take_all(key_sent), "x", sizes)
        key_sent = square_back_on(key_first, "y", sizes)
        value_first = square_added(value_first, take_all(value_sent), "y", sizes)
        value_sent = square_back_on(value_first, "x", sizes)
        then(*key_first, *value_first)
        every_sent = home_along(reduced(in_order(take_all(every_sent), "x", xn)), "y", yn)
        top_sent = square_back_on([after(v, *key_first) for v in top_first], "y", sizes)
        low_sent = square_back_on([after(v, *value_first) for v in low_first], "x", sizes)
        grad_q = rotate(grad_queries[:group] * logit_scale, -1.0)
        query_grad = dot(grad_q, plain, 0, 0)
        output_grad = dot(joined, grad_branch, 0, 0)
        then(query_grad, output_grad)
        down_back = in_order(take_all(down_back), "z", ZN)
        grad_k = rotate(sum(take_all(key_sent), key_first[0]), -1.0)
        grad_value_own = sum(take_all(value_sent), value_first[0])
        every = reduced(in_order(take_all(every_sent), "y", yn))
        every_sent = home_along(every, "k", KN)
        query_first, output_first = (
            cut(after(g, grad_k, grad_value_own)) for g in (query_grad, output_grad)
        )
        query_sent = square_back(query_first, "x", sizes)
        output_sent = square_back(output_first, "y", sizes)
        key_grad = then(dot(grad_k, plain, 0, 0))
        key_first = cut(key_grad)
        key_sent = square_back(key_first, "x", sizes)
        value_grad = then(dot(grad_value_own, plain, 0, 0))
        value_first = cut(value_grad)
        value_sent = square_back(value_first, "y", sizes)
        grad_qk = now(jnp.concatenate([grad_q, grad_k], axis=1))
        grad_part = then(dot(grad_qk, wqk) + dot(grad_value_own, wv))
        grad_attn_sent = group_sum(grad_part)

        every = in_order(take_all(every_sent), "k", KN)
        every = jnp.concatenate([every[:, :2].reshape(1, -1), jnp.sum(every[:, 2:], axis=0, keepdims=True)], axis=1)
        every_sent = home_along(every, "z", ZN)
        top_grad = sum(take_all(top_sent), top_first[0])
        low_grad = sum(take_all(low_sent), low_first[0])
        gate_back = back_along_z([jnp.concatenate([top_grad, low_grad])])
        query_first = square_added(query_first, take_all(query_sent), "x", sizes)
        query_sent = square_back_on(query_first, "y", sizes)
        output_first = square_added(output_first, take_all(output_sent), "y", sizes)
        output_sent = square_back_on(output_first, "x", sizes)
        then(*query_first, *output_first)
        key_first = square_added(key_first, take_all(key_sent), "x", sizes)
        key_sent = square_back_on(key_first, "y", sizes)
        value_first = square_added(value_first, take_all(value_sent), "y", sizes)
        value_sent = square_back_on(value_first, "x", sizes)
        then(*key_first, *value_first)
        every = in_order(take_all(every_sent), "z", ZN)
        up_back = in_order(take_all(up_back), "z", ZN)
        out_sum = take(out_sent)
        output = residual + out_sum
        out_sent = home_along(from_distance_x(output), "y", yn)
        query_grad = sum(take_all(query_sent), query_first[0])
        output_grad = sum(take_all(output_sent), output_first[0])
        early_sent = back_along_z([query_grad, output_grad])
        grad_down, grad_up = (v.T for v in now(down_back, up_back))
        then(grad_down, grad_up)
        key_grad = sum(take_all(key_sent), key_first[0])
        value_grad = sum(take_all(value_sent), value_first[0])
        late_sent = back_along_z([key_grad, value_grad])
        grad_gate = then(in_order(take_all(gate_back), "z", ZN).T)
        out_sent = home_along(in_order(take_all(out_sent), "y", yn), "k", KN)
        ffn_gain_part = then(rowsum(w_gate, grad_gate) + rowsum(w_up, grad_up))
        scaled = take(grad_attn_sent)
        grad_mine = grad_residual_attn + scale * (
            scaled - plain_mine * jnp.mean(scaled * plain_mine, axis=1, keepdims=True)
        )
        grad_mine = then(from_distance_x(from_distance_y(grad_mine)))
        tokens_sent = home_along(grad_mine, "y", yn)
        output = then(homed(in_order(take_all(out_sent), "k", KN)))
        early = in_order(take_all(early_sent), "z", ZN)
        early_sent = exchanged(early, "y", yn)
        tokens_sent = home_along(in_order(take_all(tokens_sent), "y", yn), "k", KN)
        late = in_order(take_all(late_sent), "z", ZN)
        late_sent = exchanged(late, "y", yn)
        grad_tokens = then(homed(in_order(take_all(tokens_sent), "k", KN)))
        by_block = lambda v, mats: v.reshape(BLOCKS, mats, 2 * HD, part_rows)
        held_w, held_early, held_late = by_block(attn_y, 3), by_block(early, 2), by_block(late, 2)
        attn_gain_part = (
            jnp.sum(held_w[:, 0] * held_early[:, 0], axis=(0, 1))
            + jnp.sum(held_w[:, 1] * held_late[:, 0], axis=(0, 1))
            + jnp.sum(held_w[:, 2] * held_late[:, 1], axis=(0, 1))
        )
        gains = then(jnp.concatenate([attn_gain_part, ffn_gain_part]))[None]
        gains_sent = home_along(gains, "k", KN)
        early = in_order(take_all(early_sent), "y", yn, 1)
        grad_query, grad_output = unpacked(early, 2, sub)
        then(grad_query, grad_output)
        gains = jnp.sum(in_order(take_all(gains_sent), "k", KN), axis=0, keepdims=True)
        gains_sent = home_along(gains, "y", yn)
        sums = jnp.sum(every[:, 2 * KN :], axis=0)
        size = gain_head.shape[0]
        grad_head_gain = lax.dynamic_slice_in_dim(sums[:VD], (z * xn + x) * size, size)
        grad_mix = sums[VD:]
        peak = every[:, : 2 * KN].reshape(yn, sub, KN, 2)
        maxima = jnp.transpose(peak, (0, 2, 1, 3)).reshape(2 * HEADS)
        late = in_order(take_all(late_sent), "y", yn, 1)
        grad_key, grad_value = unpacked(late, 2, sub)
        gains = in_order(take_all(gains_sent), "y", yn)
        grad_attn_gain = gains[:, :part_rows].reshape(-1)
        grad_ffn_gain = jnp.sum(gains[:, part_rows:], axis=0)
        factor = jnp.sqrt(tau[0] / jnp.maximum(maxima, tau[0]))
        mine_factor = lax.dynamic_slice_in_dim(factor, (y * KN + k) * 2 * sub, 2 * sub)
        wide_factor = jnp.repeat(mine_factor, HD)[None, :]
        return (
            output, grad_tokens, grad_query * attn_gain, grad_key * attn_gain, grad_value * attn_gain,
            grad_output, grad_attn_gain, grad_mix, grad_head_gain, grad_gate * ffn_gain,
            grad_up * ffn_gain, grad_down, grad_ffn_gain, maxima,
            w_query * wide_factor, w_key * wide_factor,
        )

    return shards


def solution(mesh):
    xn, yn = mesh.shape["row"] // ZN, mesh.shape["col"] // KN
    split = Mesh(mesh.devices.reshape(ZN, xn, yn, KN), ("z", "x", "y", "k"))
    row, col = ("z", "x"), ("y", "k")
    rows, both, vector = P(row, None), P(row, col), P(row)
    return jax.shard_map(
        layer(xn, yn),
        mesh=split,
        in_specs=(rows, rows, both, both, both, both, vector, vector, vector, vector, vector, vector,
                  both, both, both, vector, P(), P(), vector),
        out_specs=(rows, rows, both, both, both, both, vector, P(), vector, both, both, both, vector,
                   P(), both, both),
        check_vma=False,
    )
```

```python
import math

import jax
import jax.numpy as jnp
from jax import lax
from jax.experimental import pallas as pl
from jax.experimental.pallas import tpu as pltpu
from jax.sharding import Mesh
from jax.sharding import PartitionSpec as P

HEADS = 8
HD = 128
VD = 256
SEG = 64
ZN = 4
KN = 2
BLOCKS = ZN
TRUNK_SEGS = 8

epsilon = 1e-05
lambda_init = 0.2
rope_log_base = 9.210340371976184
high = lax.Precision.HIGH
highest = lax.Precision.HIGHEST
f32 = jnp.float32
bf16 = jnp.bfloat16
VMEM_BYTES = 60 * 1024 * 1024


def dot(a, b, contract_a=1, contract_b=0):
    return lax.dot_general(
        a, b, (((contract_a,), (contract_b,)), ((), ())), precision=high, preferred_element_type=f32
    )


def fine(a, b, contract_a=1, contract_b=0):
    return lax.dot_general(
        a, b, (((contract_a,), (contract_b,)), ((), ())), precision=highest, preferred_element_type=f32
    )


def thirds(v):
    top = v.astype(bf16)
    rest = v - top.astype(f32)
    low = rest.astype(bf16)
    return top, low, (rest - low.astype(f32)).astype(bf16)


def six(a, b):
    (a1, a2, a3), (b1, b2, b3) = a, b
    return mm(a1, b1) + (mm(a1, b2) + mm(a2, b1)) + (mm(a2, b2) + mm(a1, b3) + mm(a3, b1))


def halves(v):
    top = v.astype(bf16)
    return top, (v - top.astype(f32)).astype(bf16)


def mm(a, b):
    return jnp.dot(a, b, preferred_element_type=f32)


def after(v, *others):
    return lax.optimization_barrier((v,) + others)[0]


def shifted(v, axis, n, shift):
    return lax.ppermute(v, axis, [(i, (i + shift) % n) for i in range(n)])


def at(v, index, dim):
    return lax.dynamic_index_in_dim(v, index, dim, keepdims=False)


def part(v, index, rows):
    return lax.dynamic_slice_in_dim(v, index * rows, rows)


def exchanged(v, axis, n):
    i = lax.axis_index(axis)
    rows = v.shape[0] // n
    return [part(v, i, rows)] + [
        shifted(part(v, (i + s) % n, rows), axis, n, s) for s in range(1, n)
    ]


def in_order(pieces, axis, n, dim=0):
    i = lax.axis_index(axis)

    def source(j):
        shift = (i + n - j) % n
        out = pieces[0]
        for s in range(1, n):
            out = jnp.where(shift == s, pieces[s], out)
        return out

    return jnp.concatenate([source(j) for j in range(n)], axis=dim)


def small_gather(v, axis, n):
    return in_order([v[None]] + [shifted(v[None], axis, n, s) for s in range(1, n)], axis, n)


def small_fold(v, axis, n, fold):
    out = v
    for s in range(1, n):
        out = fold(out, shifted(v, axis, n, s))
    return out


def direct(v, xn, yn):
    out = {}
    for s in range(xn):
        for t in range(yn):
            pairs = [
                (a * yn + b, (a + s) % xn * yn + (b + t) % yn) for a in range(xn) for b in range(yn)
            ]
            out[s, t] = lax.ppermute(v, ("x", "y"), pairs) if s or t else v
    return out


def square_out(v, first, sizes):
    n = sizes[first]
    return [v] + [shifted(v, first, n, s) for s in range(1, n)]


def side_out(v, first, sizes):
    second = "y" if first == "x" else "x"
    n = sizes[second]
    return [shifted(v, second, n, t) for t in range(1, n)]


def square_on(came, first, sizes, side=None):
    second = "y" if first == "x" else "x"
    n = sizes[second]
    out = {}
    for s, v in enumerate(came):
        out[s, 0] = v
        for t in range(1, n):
            out[s, t] = side[t - 1] if side and s == 0 else shifted(v, second, n, t)
    return out if first == "x" else {(s, t): v for (t, s), v in out.items()}


def along_first(pieces, first):
    return pieces if first == "x" else {(t, s): v for (s, t), v in pieces.items()}


def square_back(pieces, first, sizes):
    m, n = sizes[first], sizes["y" if first == "x" else "x"]
    v = along_first(pieces, first)
    return [shifted(v[s, t], first, m, -s) for t in reversed(range(n)) for s in range(1, m)]


def square_added(pieces, came, first, sizes):
    m, n = sizes[first], sizes["y" if first == "x" else "x"]
    v = along_first(pieces, first)
    out = [v[0, t] for t in range(n)]
    order = [t for t in reversed(range(n)) for s in range(1, m)]
    for t, what in zip(order, came):
        out[t] = out[t] + what
    return out


def square_back_on(sums, second, sizes):
    n = sizes[second]
    return [shifted(sums[t], second, n, -t) for t in range(1, n)]


def table_kernel(sizes, shape, parent_ref, at_ref, seen_ref, count_ref, key_ref, own_ref, code_ref, depth_ref, order, rank, own):
    xn, yn, segs, run, pieces_run = sizes
    slots, own_slots, padded_slots, tiles, chunks = shape
    x, y = at_ref[0], at_ref[1]
    per_chunk, per_tile = slots // chunks, padded_slots // tiles

    def climb(s, carry):
        def step(i, now):
            above = parent_ref[now[0]]
            return above, now[1] + (above != now[0]).astype(jnp.int32)

        root, depth = lax.fori_loop(0, TRUNK_SEGS + 2, step, (s, jnp.int32(0)))
        depth_ref[s] = depth
        branch = jnp.where(depth == TRUNK_SEGS, s, parent_ref[s])
        past = (branch + 1) * (slots + 1) + jnp.where(depth > TRUNK_SEGS, s + 1, 0)
        place = jnp.where(depth < TRUNK_SEGS, depth, TRUNK_SEGS + past)
        order[s] = (root * (TRUNK_SEGS + (slots + 1) * (slots + 2)) + place) * slots + s
        return carry

    lax.fori_loop(0, slots, climb, 0)

    def place_slot(s, carry):
        here, mine = jnp.int32(0), jnp.int32(0)
        for t in range(slots):
            less = (order[t] < order[s]).astype(jnp.int32)
            here = here + less
            mine = mine + less * (t // segs % xn == x).astype(jnp.int32)
        rank[s] = here
        own[s] = mine
        zs = lax.div(s, xn * segs)
        xs = lax.rem(lax.div(s, segs), xn)
        for k in range(KN):
            row = (zs * KN + k) * segs + lax.rem(s, segs)
            for t in range(yn):
                piece = lax.rem(x + xn - xs, xn) * yn + lax.rem(y + yn - t, yn)
                key_ref[(here * yn + t) * KN + k] = piece * pieces_run + row

            @pl.when(xs == x)
            def _():
                own_ref[mine * KN + k] = row

        return carry

    lax.fori_loop(0, slots, place_slot, 0)
    for r in range(own_slots * KN, padded_slots * KN):
        own_ref[r] = jnp.int32(r)

    def clear(i, carry):
        for j in range(padded_slots):
            code_ref[i * padded_slots + j] = jnp.int32(0 if j < own_slots else 1)
        return carry

    lax.fori_loop(0, slots, clear, 0)

    def mark(s, carry):
        @pl.when(lax.rem(lax.div(s, segs), xn) == x)
        def _():
            def step(i, now):
                code_ref[rank[now] * padded_slots + own[s]] = jnp.int32(1)
                return parent_ref[now]

            lax.fori_loop(0, TRUNK_SEGS + 2, step, parent_ref[s])
            code_ref[rank[s] * padded_slots + own[s]] = jnp.int32(2)

        return carry

    lax.fori_loop(0, slots, mark, 0)

    def visit(tile, carry):
        def look(c, count):
            some = jnp.int32(0)
            for i in range(per_chunk):
                for j in range(per_tile):
                    at = tile * per_tile + j
                    code = code_ref[(c * per_chunk + i) * padded_slots + at]
                    some = some | jnp.where(at < own_slots, code, 0)

            @pl.when(some > 0)
            def _():
                seen_ref[tile * chunks + count] = c

            return count + (some > 0).astype(jnp.int32)

        count_ref[tile] = lax.fori_loop(0, chunks, look, jnp.int32(0))
        return carry

    lax.fori_loop(0, tiles, visit, 0)


def mask(code_ref, y, run, tile, c, chunk, padded_slots):
    wide = KN * run
    per_tile = TILE // wide
    lane = lax.broadcasted_iota(jnp.int32, (1, TILE), 1)
    row = lax.broadcasted_iota(jnp.int32, (SEG, TILE), 0)
    which = lax.div(lane, wide)
    offset = y * wide + lax.rem(lane, wide)
    blocks = []
    for i in range(chunk // SEG):
        code = jnp.zeros((1, TILE), jnp.int32)
        for j in range(per_tile):
            one = code_ref[(c * (chunk // SEG) + i) * padded_slots + tile * per_tile + j]
            code = jnp.where(which == j, one, code)
        last = jnp.where(code == 0, -1, jnp.where(code == 1, SEG, offset))
        blocks.append(jnp.where(row <= last, 0.0, -1e30).astype(f32))
    return jnp.concatenate(blocks, axis=0)


def logits_chunk(keys_wide, queries, rows, j):
    first, last = keys_wide[0, j, rows, :], keys_wide[1, j, rows, :]
    top, low, rest = queries[j]
    return mm(first, top) + (mm(first, low) + mm(last, rest))


def split_keys(keys, keys_wide, rows):
    for j in range(2):
        top, low, rest = thirds(keys[:, j * HD : (j + 1) * HD])
        keys_wide[0, j, rows, :HD] = top
        keys_wide[0, j, rows, HD:] = low
        keys_wide[1, j, rows, :HD] = top
        keys_wide[1, j, rows, HD:] = rest


def split_queries(q):
    out = []
    for j in range(2):
        top, low, rest = thirds(q[:, j * HD : (j + 1) * HD].T)
        out.append([jnp.concatenate(p, axis=0) for p in ((top, top), (low, low), (rest, top))])
    return out


def chunk_rows(c, size):
    return pl.ds(pl.multiple_of(c * size, size), size)


def brought(run, start_ref, first, count, source, target):
    def move(i, carry):
        target[chunk_rows(i, run), :] = source[chunk_rows(start_ref[first + i], run), :]
        return carry

    lax.fori_loop(0, count, move, 0)


def taken_back(run, start_ref, first, count, source, target):
    def move(i, carry):
        target[chunk_rows(start_ref[first + i], run), :] = source[chunk_rows(i, run), :]
        return carry

    lax.fori_loop(0, count, move, 0)


def forward_kernel(
    run, mix_ref, at_ref, seen_ref, count_ref, key_ref, own_ref, code_ref, q_ref, k_ref, v_ref,
    o_ref, stat_ref, keys_wide, vt, held, sorted_rows, sorted_q,
):
    total = k_ref.shape[0]
    chunk = vt.shape[3]
    count = total // chunk
    tile = pl.program_id(0)

    @pl.when(tile == 0)
    def _():
        brought(run, own_ref, 0, q_ref.shape[0] // run, q_ref, sorted_q)
        brought(run, key_ref, 0, total // run, k_ref, sorted_rows)

        def split(c, carry):
            rows = chunk_rows(c, chunk)
            split_keys(sorted_rows[rows, :], keys_wide, rows)
            return carry

        lax.fori_loop(0, count, split, 0)
        brought(run, key_ref, 0, total // run, v_ref, sorted_rows)

        def turn(c, carry):
            for i, p in enumerate(thirds(sorted_rows[chunk_rows(c, chunk), :].T)):
                vt[i, c] = p
            return carry

        lax.fori_loop(0, count, turn, 0)

    split = split_queries(sorted_q[chunk_rows(tile, TILE), :])
    visits = count_ref[tile]

    padded_slots = q_ref.shape[0] // (KN * run)

    def score(i, peaks):
        c = seen_ref[tile * count + i]
        rows = chunk_rows(c, chunk)
        bias = mask(code_ref, at_ref[1], run, tile, c, chunk, padded_slots)
        out = []
        for j in range(2):
            s = logits_chunk(keys_wide, split, rows, j) + bias
            held[j, rows, :] = s
            out.append(jnp.maximum(peaks[j], jnp.max(s, axis=0, keepdims=True)))
        return tuple(out)

    peaks = lax.fori_loop(0, visits, score, (jnp.full((1, TILE), -1e30, f32),) * 2)

    def weigh(i, sums):
        rows = chunk_rows(seen_ref[tile * count + i], chunk)
        out = []
        for j in range(2):
            w = jnp.exp(held[j, rows, :] - peaks[j])
            held[j, rows, :] = w
            out.append(sums[j] + jnp.sum(w, axis=0, keepdims=True))
        return tuple(out)

    sums = lax.fori_loop(0, visits, weigh, (jnp.zeros((1, TILE), f32),) * 2)
    first, second = 1.0 / sums[0], mix_ref[0] / sums[1]

    def collect(i, acc):
        c = seen_ref[tile * count + i]
        rows = chunk_rows(c, chunk)
        both = thirds(held[0, rows, :] * first - held[1, rows, :] * second)
        return acc + six([vt[i, c] for i in range(3)], both)

    out = lax.fori_loop(0, visits, collect, jnp.zeros((VD, TILE), f32)).T
    for i in range(TILE // run):
        o_ref[chunk_rows(own_ref[tile * (TILE // run) + i], run), :] = out[i * run : (i + 1) * run, :]
    for j in range(2):
        stat_ref[j : j + 1, :] = peaks[j] + jnp.log(sums[j])
        stat_ref[2 + j : 3 + j, :] = peaks[j]
    stat_ref[4:8, :] = jnp.zeros((4, TILE), f32)


def backward_kernel(
    run, mix_ref, at_ref, seen_ref, count_ref, key_ref, own_ref, code_ref, q_ref, dc_ref, stat_ref, k_ref, v_ref,
    dq_ref, dk_ref, dv_ref, inner_ref, keys_wide, kt, held, cross, sorted_v, sorted_q, sorted_dc,
):
    total = k_ref.shape[0]
    chunk = kt.shape[3]
    count = total // chunk
    mix = mix_ref[0]
    tile = pl.program_id(0)

    @pl.when(tile == 0)
    def _():
        brought(run, own_ref, 0, q_ref.shape[0] // run, q_ref, sorted_q)
        brought(run, own_ref, 0, q_ref.shape[0] // run, dc_ref, sorted_dc)
        brought(run, key_ref, 0, total // run, k_ref, sorted_v)

        def prepare(c, carry):
            rows = chunk_rows(c, chunk)
            keys = sorted_v[rows, :]
            split_keys(keys, keys_wide, rows)
            for i, p in enumerate(halves(keys.T)):
                kt[i, c] = p
            dk_ref[rows, :] = jnp.zeros(keys.shape, f32)
            dv_ref[rows, :] = jnp.zeros(keys.shape, f32)
            return carry

        lax.fori_loop(0, count, prepare, 0)
        brought(run, key_ref, 0, total // run, v_ref, sorted_v)

    queries, cotangents = sorted_q[chunk_rows(tile, TILE), :], sorted_dc[chunk_rows(tile, TILE), :]
    split = split_queries(queries)
    dct = thirds(cotangents.T)
    dc_top, dc_low = halves(cotangents)
    dc_wide = jnp.concatenate([dc_top, dc_top], axis=0)
    q_top, q_low = halves(queries)
    q_wide = jnp.concatenate([q_top, q_top], axis=0)
    norms = [stat_ref[j : j + 1, :] for j in range(2)]
    visits = count_ref[tile]

    padded_slots = q_ref.shape[0] // (KN * run)

    def first(i, inner):
        c = seen_ref[tile * count + i]
        rows = chunk_rows(c, chunk)
        bias = mask(code_ref, at_ref[1], run, tile, c, chunk, padded_slots)
        both = six(thirds(sorted_v[rows, :]), dct)
        cross[rows, :] = both
        out, probs = [], []
        for j in range(2):
            p = jnp.exp(logits_chunk(keys_wide, split, rows, j) + bias - norms[j])
            held[j, rows, :] = p
            probs.append(p)
            out.append(inner[j] + jnp.sum(p * both, axis=0, keepdims=True))
        top, low = halves(probs[0] - mix * probs[1])
        dv_ref[rows, :] += mm(jnp.concatenate([top, low], axis=1), dc_wide) + mm(top, dc_low)
        return tuple(out)

    inner = lax.fori_loop(0, visits, first, (jnp.zeros((1, TILE), f32),) * 2)

    def second(i, acc):
        c = seen_ref[tile * count + i]
        rows = chunk_rows(c, chunk)
        both = cross[rows, :]
        out = []
        for j in range(2):
            d = held[j, rows, :] * (both - inner[j])
            if j == 1:
                d = d * (-mix)
            top, low = halves(d)
            cols = slice(j * HD, (j + 1) * HD)
            dk_ref[rows, cols] += mm(jnp.concatenate([top, low], axis=1), q_wide[:, cols]) + mm(
                top, q_low[:, cols]
            )
            kt_top, kt_low = kt[0, c, cols, :], kt[1, c, cols, :]
            out.append(acc[j] + (mm(kt_top, top) + (mm(kt_top, low) + mm(kt_low, top))))
        return tuple(out)

    dq = lax.fori_loop(0, visits, second, (jnp.zeros((HD, TILE), f32),) * 2)
    dq = jnp.concatenate(dq, axis=0).T
    for i in range(TILE // run):
        dq_ref[chunk_rows(own_ref[tile * (TILE // run) + i], run), :] = dq[i * run : (i + 1) * run, :]
    for j in range(2):
        inner_ref[j : j + 1, :] = inner[j]
    inner_ref[2:8, :] = jnp.zeros((6, TILE), f32)

    @pl.when(tile == pl.num_programs(0) - 1)
    def _():
        for ref in (dk_ref, dv_ref):

            def keep(c, carry):
                rows = chunk_rows(c, chunk)
                sorted_v[rows, :] = ref[rows, :]
                return carry

            lax.fori_loop(0, count, keep, 0)
            taken_back(run, key_ref, 0, total // run, sorted_v, ref)


TILE = 128
CHUNK = 256


def whole():
    return pl.BlockSpec(memory_space=pltpu.VMEM)


def table():
    return pl.BlockSpec(memory_space=pltpu.SMEM)


def tables_of(sizes, shape, parent_slot, place):
    slots, own_slots, padded_slots, tiles, chunks = shape
    yn = sizes[1]
    counts = (tiles * chunks, tiles, slots * yn * KN, padded_slots * KN, slots * padded_slots, slots)
    return pl.pallas_call(
        lambda *refs: table_kernel(sizes, shape, *refs),
        in_specs=[table()] * 2,
        out_specs=[table()] * len(counts),
        out_shape=[jax.ShapeDtypeStruct((n,), jnp.int32) for n in counts],
        scratch_shapes=[pltpu.SMEM((slots,), jnp.int32)] * 3,
        name="tables",
    )(parent_slot, place)


def attend(run, mix, tables, queries, keys, values):
    total, count = keys.shape[0], queries.shape[0]
    chunk = math.gcd(total, CHUNK)
    lanes = lambda rows: pl.BlockSpec((rows, TILE), lambda i: (0, i))
    return pl.pallas_call(
        lambda *refs: forward_kernel(run, *refs),
        grid=(count // TILE,),
        in_specs=[table()] * 7 + [whole()] * 3,
        out_specs=[whole(), lanes(8)],
        out_shape=[
            jax.ShapeDtypeStruct((count, VD), f32), jax.ShapeDtypeStruct((8, count), f32),
        ],
        scratch_shapes=[
            pltpu.VMEM((2, 2, total, 2 * HD), bf16),
            pltpu.VMEM((3, total // chunk, VD, chunk), bf16),
            pltpu.VMEM((2, total, TILE), f32),
            pltpu.VMEM((total, 2 * HD), f32),
            pltpu.VMEM((count, 2 * HD), f32),
        ],
        compiler_params=pltpu.CompilerParams(vmem_limit_bytes=VMEM_BYTES),
        cost_estimate=pl.CostEstimate(flops=4 * 10**10, bytes_accessed=0, transcendentals=0),
        name="attend",
    )(mix, *tables, queries, keys, values)


def attend_back(run, mix, tables, queries, contrast, stat, keys, values):
    total, count = keys.shape[0], queries.shape[0]
    chunk = math.gcd(total, CHUNK)
    lanes = lambda rows: pl.BlockSpec((rows, TILE), lambda i: (0, i))
    return pl.pallas_call(
        lambda *refs: backward_kernel(run, *refs),
        grid=(count // TILE,),
        in_specs=[table()] * 7 + [whole()] * 2 + [lanes(8)] + [whole()] * 2,
        out_specs=[whole(), whole(), whole(), lanes(8)],
        out_shape=[
            jax.ShapeDtypeStruct((count, 2 * HD), f32),
            jax.ShapeDtypeStruct((total, 2 * HD), f32),
            jax.ShapeDtypeStruct((total, VD), f32),
            jax.ShapeDtypeStruct((8, count), f32),
        ],
        scratch_shapes=[
            pltpu.VMEM((2, 2, total, 2 * HD), bf16),
            pltpu.VMEM((2, total // chunk, 2 * HD, chunk), bf16),
            pltpu.VMEM((2, total, TILE), f32),
            pltpu.VMEM((total, TILE), f32),
            pltpu.VMEM((total, VD), f32),
            pltpu.VMEM((count, 2 * HD), f32),
            pltpu.VMEM((count, VD), f32),
        ],
        compiler_params=pltpu.CompilerParams(vmem_limit_bytes=VMEM_BYTES),
        cost_estimate=pl.CostEstimate(flops=4 * 10**10, bytes_accessed=0, transcendentals=0),
        name="attend_back",
    )(mix, *tables, queries, contrast, stat, keys, values)


def layer(xn, yn):
    sizes = {"x": xn, "y": yn}
    places = [(s, t) for s in range(xn) for t in range(yn)]

    def shards(
        tokens, cotangent, w_query, w_key, w_value, w_output, gain_attn, lambda_query_first,
        lambda_key_first, lambda_query_second, lambda_key_second, gain_head, w_gate, w_up, w_down,
        gain_ffn, tau, parent_slot, depth,
    ):
        z, x, y, k = (lax.axis_index(a) for a in "zxyk")
        home_rows, width = tokens.shape
        segs = home_rows // SEG
        run = SEG // (yn * KN)
        piece_rows = segs * run
        group = ZN * KN * piece_rows
        sub = BLOCKS // yn
        held_rows = w_query.shape[0]
        part_rows = held_rows // yn
        square_rows = ZN * part_rows
        total = ZN * xn * home_rows
        slot_total = parent_slot.shape[0]
        hidden_cols = w_gate.shape[1] // sub

        def block(v, i):
            return v[:, i * part_rows : (i + 1) * part_rows]

        def by_index(i, n, order):
            out = order(0)
            for j in range(1, n):
                out = jnp.where(i == j, order(j), out)
            return out

        def to_distance_x(v):
            return by_index(x, xn, lambda j: jnp.concatenate(
                [block(v, (c * xn + (j + xn - s) % xn) * yn + t)
                 for s in range(xn) for c in range(ZN) for t in range(yn)], axis=1))

        def from_distance_x(v):
            return by_index(x, xn, lambda j: jnp.concatenate(
                [block(v, ((j + xn - a) % xn * ZN + c) * yn + t)
                 for c in range(ZN) for a in range(xn) for t in range(yn)], axis=1))

        def to_distance_y(v):
            return by_index(y, yn, lambda j: jnp.concatenate(
                [block(v, (s * ZN + c) * yn + (j + yn - t) % yn)
                 for s in range(xn) for t in range(yn) for c in range(ZN)], axis=1))

        def from_distance_y(v):
            return by_index(y, yn, lambda j: jnp.concatenate(
                [block(v, (s * yn + (j + yn - t) % yn) * ZN + c)
                 for s in range(xn) for c in range(ZN) for t in range(yn)], axis=1))

        def piece(v):
            v = v.reshape(segs, yn * KN, run, width)
            return to_distance_x(at(v, y * KN + k, 1).reshape(piece_rows, width))

        def home_along(v, axis, n):
            return [v] + [shifted(v, axis, n, s) for s in range(1, n)]

        def homed(v):
            v = v.reshape(KN, yn, segs, run, width)
            return jnp.transpose(v, (2, 1, 0, 3, 4)).reshape(home_rows, width)

        def group_gather(v):
            return lax.all_gather(v, ("z", "k"), axis=0, tiled=True)

        def group_sum(v):
            return lax.psum_scatter(v, ("z", "k"), scatter_dimension=0, tiled=True)

        def packed(mats, blocks):
            rows = mats[0].shape[1] // blocks
            mats = [m.T for m in mats]
            return jnp.concatenate([m[s * rows : (s + 1) * rows] for s in range(blocks) for m in mats])

        def lanes(v, index, size):
            return lax.dynamic_slice_in_dim(v, index * size, size, 1)

        def along_y(v):
            mine = lanes(v, y, part_rows)
            return [mine] + [shifted(lanes(v, (y + s) % yn, part_rows), "y", yn, s) for s in range(1, yn)]

        def back_along_z(mats):
            v = jnp.concatenate(mats)
            size = v.shape[1] // ZN
            mine = lanes(v, z, size)
            return [mine] + [shifted(lanes(v, (z + s) % ZN, size), "z", ZN, s) for s in range(1, ZN)]

        def unpacked(v, mats, blocks):
            cols = v.shape[0] // (blocks * mats)
            part = lambda s, m: v[(s * mats + m) * cols : (s * mats + m + 1) * cols]
            return [jnp.concatenate([part(s, m) for s in range(blocks)]).T for m in range(mats)]

        def joined_up(pieces):
            return jnp.concatenate([pieces[p] for p in places], axis=1)

        def cut(g):
            return {p: g[:, i * square_rows : (i + 1) * square_rows] for i, p in enumerate(places)}

        def tiled_up(pieces):
            return jnp.concatenate(
                [jnp.concatenate([pieces[s, t] for s in range(xn)], axis=1) for t in range(yn)]
            )

        def tiles(g):
            r, c = g.shape[0] // yn, g.shape[1] // xn
            return {(s, t): g[t * r : (t + 1) * r, s * c : (s + 1) * c] for s, t in places}

        def halved(v):
            mid = v.shape[0] // 2
            return v[:mid], v[mid:]

        def rowsum(w, g):
            return jnp.sum(w * g, axis=1)

        last = []

        def now(*v):
            out = lax.optimization_barrier(tuple(v) + tuple(last))[: len(v)]
            return out[0] if len(v) == 1 else out

        def then(*v):
            last[:] = v
            return v[0] if len(v) == 1 else v

        def take(*v):
            out = now(*v)
            return then(*(out if len(v) > 1 else (out,)))

        def take_all(pieces):
            out = lax.optimization_barrier(tuple(pieces) + tuple(last))[: len(pieces)]
            then(*out)
            return list(out)

        attn_gain, ffn_gain = gain_attn[:, None], gain_ffn[:, None]
        sent = along_y(packed([w_query, w_key, w_value], sub))
        small = jnp.concatenate(
            [gain_head, lambda_query_first, lambda_key_first, lambda_query_second, lambda_key_second]
        )
        small_sent = home_along(small[None], "x", xn)
        attn_y = in_order(take_all(sent), "y", yn)
        y_gain = part(gain_attn, y, part_rows)[None, :]
        sent = exchanged(attn_y * y_gain, "z", ZN)
        output_sent = along_y(after(packed([w_output], sub), attn_y))
        sent[: 2] = take_all(sent[: 2])
        padded = -(-group // TILE) * TILE
        own_slots = ZN * segs
        chunks = total // math.gcd(total, CHUNK)
        *tables, depth_of = tables_of(
            (xn, yn, segs, run, group // run),
            (slot_total, own_slots, padded // (KN * run), padded // TILE, chunks),
            now(parent_slot), jnp.stack([x, y]),
        )
        tables = [jnp.stack([x, y])] + tables
        mine = piece(now(tokens))
        scale = lax.rsqrt(jnp.mean(mine * mine, axis=1, keepdims=True) + epsilon)
        mine_attn = to_distance_y(mine)
        plain_mine = then(mine_attn * scale)
        down_sent = now(w_down).T
        then(down_sent, plain_mine, *tables)
        small = in_order(take_all(small_sent), "x", xn).reshape(1, -1)
        small_sent = home_along(small, "z", ZN)
        output_y = in_order(take_all(output_sent), "y", yn)
        shares = down_sent.shape[1] // part_rows
        output_y = output_y.reshape(BLOCKS, shares, VD // shares, part_rows)
        output_y = jnp.concatenate([output_y[:, i] for i in range(shares)], axis=2)
        output_down = jnp.concatenate(
            [output_y, down_sent.reshape(BLOCKS, -1, down_sent.shape[1])], axis=1
        ).reshape(-1, down_sent.shape[1])
        then(output_down)
        attn_z = in_order(sent[:2] + take_all(sent[2:]), "z", ZN, 1)
        upper, lower = halved(attn_z)
        upper_out, lower_out = square_out(upper, "x", sizes), square_out(lower, "y", sizes)
        upper_side, lower_side = side_out(upper, "x", sizes), side_out(lower, "y", sizes)
        plain_sent = group_gather(after(plain_mine, attn_z))
        upper_on = square_on(take_all(upper_out), "x", sizes, upper_side)
        lower_on = square_on(take_all(lower_out), "y", sizes, lower_side)

        small = in_order(take_all(small_sent), "z", ZN).reshape(ZN * xn, -1)
        n_gain, n_lambda = gain_head.shape[0], lambda_key_first.shape[0]
        head_gain = small[:, :n_gain].reshape(1, -1)
        query_first, key_first, query_second, key_second = (
            small[:, n_gain + i * n_lambda : n_gain + (i + 1) * n_lambda] for i in range(4)
        )
        mix = (
            jnp.exp(jnp.sum(query_first * key_first))
            - jnp.exp(jnp.sum(query_second * key_second))
            + lambda_init
        ).reshape(1)

        def padded_rows(v):
            return jnp.pad(v, ((0, padded - group), (0, 0)))

        shape = (ZN, KN, segs, run)
        ks, rs = (lax.broadcasted_iota(jnp.int32, shape, d) for d in (1, 3))
        depths = at(depth_of.reshape(ZN, xn, segs), x, 1)[:, None, :, None]
        position = (depths * SEG + (y * KN + ks) * run + rs).reshape(group, 1).astype(f32)
        half_dim = HD // 2
        frequency = jnp.exp(-rope_log_base * jnp.arange(half_dim, dtype=f32) / half_dim)
        angles = position * frequency[None, :]
        cosine, sine = jnp.cos(angles), jnp.sin(angles)
        cosine = jnp.concatenate([cosine] * 4, axis=1)
        sine = jnp.concatenate([-sine, sine] * 2, axis=1)

        def rotate(v, sign):
            parts = [v[:, i * half_dim : (i + 1) * half_dim] for i in (1, 0, 3, 2)]
            return v * cosine + jnp.concatenate(parts, axis=1) * (sign * sine)

        cot_mine = piece(cotangent)
        upper = joined_up(dict(zip(places, take_all([upper_on[p] for p in places]), strict=True)))
        lower = joined_up(dict(zip(places, take_all([lower_on[p] for p in places]), strict=True)))
        plain = take(plain_sent)
        down_sent = exchanged(after(output_down, plain), "z", ZN)
        cot_sent = group_gather(after(cot_mine, plain))
        wqkv = jnp.concatenate([upper, lower])
        wqk, wv = wqkv[: 4 * HD], wqkv[4 * HD :]
        then(wqkv)
        logit_scale = 1.0 / math.sqrt(HD)
        key_own = then(rotate(fine(now(plain), wqk[2 * HD :], 1, 1), 1.0))
        key_sent = square_out(key_own, "x", sizes)
        value_own = then(fine(now(plain), wv, 1, 1))
        value_sent = square_out(value_own, "y", sizes)
        queries = rotate(fine(now(plain), wqk[: 2 * HD], 1, 1), 1.0)
        queries = then(padded_rows(queries * logit_scale))
        gate_up_sent = packed([now(w_up) * ffn_gain, now(w_gate) * ffn_gain], BLOCKS)
        then(queries, gate_up_sent)
        key_sent = square_on(take_all(key_sent), "x", sizes)
        value_sent = square_on(take_all(value_sent), "y", sizes)
        came = take_all(down_sent)
        output_rows = VD // shares
        down_z = in_order([v[output_rows:] for v in came], "z", ZN, 1)
        output_z = in_order(
            [
                jnp.concatenate([v[:output_rows, i * part_rows : (i + 1) * part_rows] for i in range(shares)])
                for v in came
            ],
            "z", ZN, 1,
        )
        gate_up_sent = exchanged(after(gate_up_sent, down_z), "z", ZN)
        key_list = take_all([key_sent[p] for p in places])
        value_list = take_all([value_sent[p] for p in places])
        output_sent = direct(after(output_z, *value_list), xn, yn)
        down_z = after(down_z, *value_list)
        down_out, down_side = square_out(down_z, "x", sizes), side_out(down_z, "x", sizes)
        keys, values = jnp.concatenate(key_list), jnp.concatenate(value_list)
        cot = take(cot_sent)
        contrast, stat = attend(run, mix, tables, now(queries), keys, values)
        then(contrast)
        gate_up_sent = take_all(gate_up_sent)
        output_sent = dict(zip(places, take_all([output_sent[p] for p in places]), strict=True))
        wo = joined_up(output_sent)
        contrast = now(contrast)[:group]
        head_scale = lax.rsqrt(jnp.mean(contrast * contrast, axis=1, keepdims=True) + epsilon)
        head_plain = contrast * head_scale
        joined = head_plain * head_gain * (1.0 - lambda_init)
        branch_part = then(fine(joined, wo))
        branch_sent = group_sum(branch_part)
        up_w, gate_w = halved(in_order(gate_up_sent, "z", ZN, 1))

        down_out, down_side = take_all(down_out), take_all(down_side)
        down_on = square_on(down_out, "x", sizes, down_side)
        up_w = after(up_w, *down_out)
        up_out, up_side = square_out(up_w, "y", sizes), side_out(up_w, "y", sizes)
        down_pieces = dict(zip(places, take_all([down_on[p] for p in places]), strict=True))
        up_side = take_all(up_side)
        gate_top, gate_low = halved(after(gate_w, *up_side))
        top_out, low_out = square_out(gate_top, "x", sizes), square_out(gate_low, "y", sizes)
        top_side, low_side = side_out(gate_top, "x", sizes), side_out(gate_low, "y", sizes)
        branch = take(branch_sent)
        residual = from_distance_y(mine_attn + branch)
        ffn_scale = lax.rsqrt(jnp.mean(residual * residual, axis=1, keepdims=True) + epsilon)
        ffn_mine = then(residual * ffn_scale)
        ffn_sent = group_gather(ffn_mine)
        wd = tiled_up(down_pieces)
        grad_hidden = then(fine(wd, cot, 1, 1))
        top_out, low_side = take_all(top_out), take_all(low_side)
        up_on = square_on(take_all(up_out), "y", sizes, up_side)
        top_on = square_on(top_out, "x", sizes, top_side)
        low_on = square_on(take_all(low_out), "y", sizes, low_side)
        up_pieces = dict(zip(places, take_all([up_on[p] for p in places]), strict=True))
        ffn_plain = take(ffn_sent)
        top_list = take_all([top_on[p] for p in places])
        low_list = take_all([low_on[p] for p in places])
        wug = jnp.concatenate(
            [
                jnp.concatenate([v[s, t] for s in range(xn)], axis=1)
                for t in range(yn)
                for v in (up_pieces,)
            ]
            + [
                jnp.concatenate([v[s, t] for s in range(xn)], axis=1)
                for t in range(yn)
                for v in (dict(zip(places, top_list, strict=True)), dict(zip(places, low_list, strict=True)))
            ]
        )

        both = fine(wug, ffn_plain, 1, 1)
        up_proj, gating = halved(both)
        gate = lax.logistic(gating)
        active = gating * gate
        hidden = active * up_proj
        grad_both = jnp.concatenate(
            [grad_hidden * active, grad_hidden * up_proj * gate * (1.0 + gating * (1.0 - gate))]
        )
        grad_ffn_part = then(fine(grad_both, wug, 0, 0))
        grad_up_proj, grad_gating = halved(grad_both)
        grad_ffn_sent = group_sum(grad_ffn_part)
        down_grad = then(dot(now(hidden), cot))
        down_first = tiles(down_grad)
        down_sent = square_back(down_first, "x", sizes)
        up_grad = then(dot(now(grad_up_proj), ffn_plain))
        up_first = tiles(up_grad)
        up_sent = square_back(up_first, "y", sizes)
        gate_grad = then(dot(now(grad_gating), ffn_plain))
        gate_tiles = {p: halved(v) for p, v in tiles(gate_grad).items()}
        top_first = {p: v[0] for p, v in gate_tiles.items()}
        low_first = {p: v[1] for p, v in gate_tiles.items()}
        out_part = then(dot(now(hidden), wd, 0, 0))
        early = (xn - 1) * (yn - 1)
        down_sent[:early], up_sent[:early] = take_all(down_sent[:early]), take_all(up_sent[:early])
        down_first = square_added(down_first, down_sent[:early], "x", sizes)
        down_sent_on = square_back_on(down_first, "y", sizes)
        up_first = square_added(up_first, up_sent[:early], "y", sizes)
        up_sent_on = square_back_on(up_first, "x", sizes)
        then(*down_first[1:], *up_first[1:])
        scaled = take(grad_ffn_sent)
        grad_residual = cot_mine + ffn_scale * (
            scaled - ffn_mine * jnp.mean(scaled * ffn_mine, axis=1, keepdims=True)
        )
        grad_residual_attn = then(to_distance_y(grad_residual))
        grad_branch_sent = group_gather(grad_residual_attn)
        down_grad = sum(take_all(down_sent[early:]), down_first[0])
        up_grad = sum(take_all(up_sent[early:]), up_first[0])
        then(down_grad, up_grad)
        grad_branch = take(grad_branch_sent)

        out_sent = group_sum(after(out_part, grad_branch))
        grad_joined = fine(grad_branch, wo, 1, 1) * (1.0 - lambda_init)
        grad_head_gain = jnp.sum(grad_joined * head_plain, axis=0)
        scaled = grad_joined * head_gain
        grad_contrast = padded_rows(
            head_scale * (scaled - head_plain * jnp.mean(scaled * head_plain, axis=1, keepdims=True))
        )
        grad_contrast = then(grad_contrast)
        down_grad = sum(take_all(down_sent_on), down_grad)
        down_back = back_along_z([down_grad])
        up_grad = sum(take_all(up_sent_on), up_grad)
        up_back = back_along_z([up_grad])
        then(down_grad, up_grad)
        top_sent = square_back({p: after(v, down_grad) for p, v in top_first.items()}, "x", sizes)
        low_sent = square_back({p: after(v, up_grad) for p, v in low_first.items()}, "y", sizes)
        grad_contrast = now(grad_contrast)
        grad_queries, grad_keys, grad_values, inner = attend_back(
            run, mix, tables, queries, grad_contrast, stat, keys, values
        )
        then(grad_queries, grad_keys, grad_values)
        rows_cut = lambda g: {p: g[i * group : (i + 1) * group] for i, p in enumerate(places)}
        key_first, value_first = rows_cut(grad_keys), rows_cut(grad_values)
        key_sent = square_back(key_first, "x", sizes)
        value_sent = square_back(value_first, "y", sizes)
        def reduced(v):
            return jnp.concatenate([jnp.max(v[:, :2], axis=0), jnp.sum(v[:, 2:], axis=0)])[None]

        peak = jnp.max(stat[2:4, :group], axis=1)
        every = jnp.concatenate([peak, grad_head_gain, -jnp.sum(inner[1:2, :group], axis=1)])[None]
        every_sent = home_along(every, "x", xn)
        top_first = square_added(top_first, take_all(top_sent), "x", sizes)
        low_first = square_added(low_first, take_all(low_sent), "y", sizes)
        then(*top_first, *low_first)
        key_first = square_added(key_first, take_all(key_sent), "x", sizes)
        key_sent = square_back_on(key_first, "y", sizes)
        value_first = square_added(value_first, take_all(value_sent), "y", sizes)
        value_sent = square_back_on(value_first, "x", sizes)
        then(*key_first, *value_first)
        every_sent = home_along(reduced(in_order(take_all(every_sent), "x", xn)), "y", yn)
        top_sent = square_back_on([after(v, *key_first) for v in top_first], "y", sizes)
        low_sent = square_back_on([after(v, *value_first) for v in low_first], "x", sizes)
        grad_q = rotate(grad_queries[:group] * logit_scale, -1.0)
        query_grad = dot(grad_q, plain, 0, 0)
        output_grad = dot(joined, grad_branch, 0, 0)
        then(query_grad, output_grad)
        down_back = in_order(take_all(down_back), "z", ZN)
        grad_k = rotate(sum(take_all(key_sent), key_first[0]), -1.0)
        grad_value_own = sum(take_all(value_sent), value_first[0])
        every = reduced(in_order(take_all(every_sent), "y", yn))
        every_sent = home_along(every, "k", KN)
        query_first, output_first = (
            cut(after(g, grad_k, grad_value_own)) for g in (query_grad, output_grad)
        )
        query_sent = square_back(query_first, "x", sizes)
        output_sent = square_back(output_first, "y", sizes)
        key_grad = then(dot(grad_k, plain, 0, 0))
        key_first = cut(key_grad)
        key_sent = square_back(key_first, "x", sizes)
        value_grad = then(dot(grad_value_own, plain, 0, 0))
        value_first = cut(value_grad)
        value_sent = square_back(value_first, "y", sizes)
        grad_qk = now(jnp.concatenate([grad_q, grad_k], axis=1))
        grad_part = then(dot(grad_qk, wqk) + dot(grad_value_own, wv))
        grad_attn_sent = group_sum(grad_part)

        every = in_order(take_all(every_sent), "k", KN)
        every = jnp.concatenate([every[:, :2].reshape(1, -1), jnp.sum(every[:, 2:], axis=0, keepdims=True)], axis=1)
        every_sent = home_along(every, "z", ZN)
        top_grad = sum(take_all(top_sent), top_first[0])
        low_grad = sum(take_all(low_sent), low_first[0])
        gate_back = back_along_z([jnp.concatenate([top_grad, low_grad])])
        query_first = square_added(query_first, take_all(query_sent), "x", sizes)
        query_sent = square_back_on(query_first, "y", sizes)
        output_first = square_added(output_first, take_all(output_sent), "y", sizes)
        output_sent = square_back_on(output_first, "x", sizes)
        then(*query_first, *output_first)
        key_first = square_added(key_first, take_all(key_sent), "x", sizes)
        key_sent = square_back_on(key_first, "y", sizes)
        value_first = square_added(value_first, take_all(value_sent), "y", sizes)
        value_sent = square_back_on(value_first, "x", sizes)
        then(*key_first, *value_first)
        every = in_order(take_all(every_sent), "z", ZN)
        up_back = in_order(take_all(up_back), "z", ZN)
        out_sum = take(out_sent)
        output = residual + out_sum
        out_sent = home_along(from_distance_x(output), "y", yn)
        query_grad = sum(take_all(query_sent), query_first[0])
        output_grad = sum(take_all(output_sent), output_first[0])
        early_sent = back_along_z([query_grad, output_grad])
        grad_down, grad_up = (v.T for v in now(down_back, up_back))
        then(grad_down, grad_up)
        key_grad = sum(take_all(key_sent), key_first[0])
        value_grad = sum(take_all(value_sent), value_first[0])
        late_sent = back_along_z([key_grad, value_grad])
        grad_gate = then(in_order(take_all(gate_back), "z", ZN).T)
        out_sent = home_along(in_order(take_all(out_sent), "y", yn), "k", KN)
        ffn_gain_part = then(rowsum(w_gate, grad_gate) + rowsum(w_up, grad_up))
        scaled = take(grad_attn_sent)
        grad_mine = grad_residual_attn + scale * (
            scaled - plain_mine * jnp.mean(scaled * plain_mine, axis=1, keepdims=True)
        )
        grad_mine = then(from_distance_x(from_distance_y(grad_mine)))
        tokens_sent = home_along(grad_mine, "y", yn)
        output = then(homed(in_order(take_all(out_sent), "k", KN)))
        early = in_order(take_all(early_sent), "z", ZN)
        early_sent = exchanged(early, "y", yn)
        tokens_sent = home_along(in_order(take_all(tokens_sent), "y", yn), "k", KN)
        late = in_order(take_all(late_sent), "z", ZN)
        late_sent = exchanged(late, "y", yn)
        grad_tokens = then(homed(in_order(take_all(tokens_sent), "k", KN)))
        by_block = lambda v, mats: v.reshape(BLOCKS, mats, 2 * HD, part_rows)
        held_w, held_early, held_late = by_block(attn_y, 3), by_block(early, 2), by_block(late, 2)
        attn_gain_part = (
            jnp.sum(held_w[:, 0] * held_early[:, 0], axis=(0, 1))
            + jnp.sum(held_w[:, 1] * held_late[:, 0], axis=(0, 1))
            + jnp.sum(held_w[:, 2] * held_late[:, 1], axis=(0, 1))
        )
        gains = then(jnp.concatenate([attn_gain_part, ffn_gain_part]))[None]
        gains_sent = home_along(gains, "k", KN)
        early = in_order(take_all(early_sent), "y", yn, 1)
        grad_query, grad_output = unpacked(early, 2, sub)
        then(grad_query, grad_output)
        gains = jnp.sum(in_order(take_all(gains_sent), "k", KN), axis=0, keepdims=True)
        gains_sent = home_along(gains, "y", yn)
        sums = jnp.sum(every[:, 2 * KN :], axis=0)
        size = gain_head.shape[0]
        grad_head_gain = lax.dynamic_slice_in_dim(sums[:VD], (z * xn + x) * size, size)
        grad_mix = sums[VD:]
        peak = every[:, : 2 * KN].reshape(yn, sub, KN, 2)
        maxima = jnp.transpose(peak, (0, 2, 1, 3)).reshape(2 * HEADS)
        late = in_order(take_all(late_sent), "y", yn, 1)
        grad_key, grad_value = unpacked(late, 2, sub)
        gains = in_order(take_all(gains_sent), "y", yn)
        grad_attn_gain = gains[:, :part_rows].reshape(-1)
        grad_ffn_gain = jnp.sum(gains[:, part_rows:], axis=0)
        factor = jnp.sqrt(tau[0] / jnp.maximum(maxima, tau[0]))
        mine_factor = lax.dynamic_slice_in_dim(factor, (y * KN + k) * 2 * sub, 2 * sub)
        wide_factor = jnp.repeat(mine_factor, HD)[None, :]
        return (
            output, grad_tokens, grad_query * attn_gain, grad_key * attn_gain, grad_value * attn_gain,
            grad_output, grad_attn_gain, grad_mix, grad_head_gain, grad_gate * ffn_gain,
            grad_up * ffn_gain, grad_down, grad_ffn_gain, maxima,
            w_query * wide_factor, w_key * wide_factor,
        )

    return shards


def solution(mesh):
    xn, yn = mesh.shape["row"] // ZN, mesh.shape["col"] // KN
    split = Mesh(mesh.devices.reshape(ZN, xn, yn, KN), ("z", "x", "y", "k"))
    row, col = ("z", "x"), ("y", "k")
    rows, both, vector = P(row, None), P(row, col), P(row)
    return jax.shard_map(
        layer(xn, yn),
        mesh=split,
        in_specs=(rows, rows, both, both, both, both, vector, vector, vector, vector, vector, vector,
                  both, both, both, vector, P(), P(), vector),
        out_specs=(rows, rows, both, both, both, both, vector, P(), vector, both, both, both, vector,
                   P(), both, both),
        check_vma=False,
    )
```

```python
import math

import jax
import jax.numpy as jnp
from jax import lax
from jax.experimental import pallas as pl
from jax.experimental.pallas import tpu as pltpu
from jax.sharding import Mesh
from jax.sharding import PartitionSpec as P

HEADS = 8
HD = 128
VD = 256
SEG = 64
ZN = 4
KN = 2
BLOCKS = ZN
TRUNK_SEGS = 8

epsilon = 1e-05
lambda_init = 0.2
rope_log_base = 9.210340371976184
high = lax.Precision.HIGH
highest = lax.Precision.HIGHEST
f32 = jnp.float32
bf16 = jnp.bfloat16
VMEM_BYTES = 60 * 1024 * 1024


def dot(a, b, contract_a=1, contract_b=0):
    return lax.dot_general(
        a, b, (((contract_a,), (contract_b,)), ((), ())), precision=high, preferred_element_type=f32
    )


def fine(a, b, contract_a=1, contract_b=0):
    return lax.dot_general(
        a, b, (((contract_a,), (contract_b,)), ((), ())), precision=highest, preferred_element_type=f32
    )


def thirds(v):
    top = v.astype(bf16)
    rest = v - top.astype(f32)
    low = rest.astype(bf16)
    return top, low, (rest - low.astype(f32)).astype(bf16)


def six(a, b):
    (a1, a2, a3), (b1, b2, b3) = a, b
    return mm(a1, b1) + (mm(a1, b2) + mm(a2, b1)) + (mm(a2, b2) + mm(a1, b3) + mm(a3, b1))


def halves(v):
    top = v.astype(bf16)
    return top, (v - top.astype(f32)).astype(bf16)


def mm(a, b):
    return jnp.dot(a, b, preferred_element_type=f32)


def after(v, *others):
    return lax.optimization_barrier((v,) + others)[0]


def shifted(v, axis, n, shift):
    return lax.ppermute(v, axis, [(i, (i + shift) % n) for i in range(n)])


def at(v, index, dim):
    return lax.dynamic_index_in_dim(v, index, dim, keepdims=False)


def part(v, index, rows):
    return lax.dynamic_slice_in_dim(v, index * rows, rows)


def exchanged(v, axis, n):
    i = lax.axis_index(axis)
    rows = v.shape[0] // n
    return [part(v, i, rows)] + [
        shifted(part(v, (i + s) % n, rows), axis, n, s) for s in range(1, n)
    ]


def in_order(pieces, axis, n, dim=0):
    i = lax.axis_index(axis)

    def source(j):
        shift = (i + n - j) % n
        out = pieces[0]
        for s in range(1, n):
            out = jnp.where(shift == s, pieces[s], out)
        return out

    return jnp.concatenate([source(j) for j in range(n)], axis=dim)


def small_gather(v, axis, n):
    return in_order([v[None]] + [shifted(v[None], axis, n, s) for s in range(1, n)], axis, n)


def small_fold(v, axis, n, fold):
    out = v
    for s in range(1, n):
        out = fold(out, shifted(v, axis, n, s))
    return out


def direct(v, xn, yn):
    out = {}
    for s in range(xn):
        for t in range(yn):
            pairs = [
                (a * yn + b, (a + s) % xn * yn + (b + t) % yn) for a in range(xn) for b in range(yn)
            ]
            out[s, t] = lax.ppermute(v, ("x", "y"), pairs) if s or t else v
    return out


def square_out(v, first, sizes):
    n = sizes[first]
    return [v] + [shifted(v, first, n, s) for s in range(1, n)]


def side_out(v, first, sizes):
    second = "y" if first == "x" else "x"
    n = sizes[second]
    return [shifted(v, second, n, t) for t in range(1, n)]


def square_on(came, first, sizes, side=None):
    second = "y" if first == "x" else "x"
    n = sizes[second]
    out = {}
    for s, v in enumerate(came):
        out[s, 0] = v
        for t in range(1, n):
            out[s, t] = side[t - 1] if side and s == 0 else shifted(v, second, n, t)
    return out if first == "x" else {(s, t): v for (t, s), v in out.items()}


def along_first(pieces, first):
    return pieces if first == "x" else {(t, s): v for (s, t), v in pieces.items()}


def square_back(pieces, first, sizes):
    m, n = sizes[first], sizes["y" if first == "x" else "x"]
    v = along_first(pieces, first)
    return [shifted(v[s, t], first, m, -s) for t in reversed(range(n)) for s in range(1, m)]


def square_added(pieces, came, first, sizes):
    m, n = sizes[first], sizes["y" if first == "x" else "x"]
    v = along_first(pieces, first)
    out = [v[0, t] for t in range(n)]
    order = [t for t in reversed(range(n)) for s in range(1, m)]
    for t, what in zip(order, came):
        out[t] = out[t] + what
    return out


def square_back_on(sums, second, sizes):
    n = sizes[second]
    return [shifted(sums[t], second, n, -t) for t in range(1, n)]


def table_kernel(sizes, shape, parent_ref, at_ref, seen_ref, count_ref, key_ref, own_ref, code_ref, depth_ref, order, rank, own):
    xn, yn, segs, run, pieces_run = sizes
    slots, own_slots, padded_slots, tiles, chunks = shape
    x, y = at_ref[0], at_ref[1]
    per_chunk, per_tile = slots // chunks, padded_slots // tiles

    def climb(s, carry):
        def step(i, now):
            above = parent_ref[now[0]]
            return above, now[1] + (above != now[0]).astype(jnp.int32)

        root, depth = lax.fori_loop(0, TRUNK_SEGS + 2, step, (s, jnp.int32(0)))
        depth_ref[s] = depth
        branch = jnp.where(depth == TRUNK_SEGS, s, parent_ref[s])
        past = (branch + 1) * (slots + 1) + jnp.where(depth > TRUNK_SEGS, s + 1, 0)
        place = jnp.where(depth < TRUNK_SEGS, depth, TRUNK_SEGS + past)
        order[s] = (root * (TRUNK_SEGS + (slots + 1) * (slots + 2)) + place) * slots + s
        return carry

    lax.fori_loop(0, slots, climb, 0)

    def place_slot(s, carry):
        here, mine = jnp.int32(0), jnp.int32(0)
        for t in range(slots):
            less = (order[t] < order[s]).astype(jnp.int32)
            here = here + less
            mine = mine + less * (t // segs % xn == x).astype(jnp.int32)
        rank[s] = here
        own[s] = mine
        zs = lax.div(s, xn * segs)
        xs = lax.rem(lax.div(s, segs), xn)
        for k in range(KN):
            row = (zs * KN + k) * segs + lax.rem(s, segs)
            for t in range(yn):
                piece = lax.rem(x + xn - xs, xn) * yn + lax.rem(y + yn - t, yn)
                key_ref[(here * yn + t) * KN + k] = piece * pieces_run + row

            @pl.when(xs == x)
            def _():
                own_ref[mine * KN + k] = row

        return carry

    lax.fori_loop(0, slots, place_slot, 0)
    for r in range(own_slots * KN, padded_slots * KN):
        own_ref[r] = jnp.int32(r)

    def clear(i, carry):
        for j in range(padded_slots):
            code_ref[i * padded_slots + j] = jnp.int32(0 if j < own_slots else 1)
        return carry

    lax.fori_loop(0, slots, clear, 0)

    def mark(s, carry):
        @pl.when(lax.rem(lax.div(s, segs), xn) == x)
        def _():
            def step(i, now):
                code_ref[rank[now] * padded_slots + own[s]] = jnp.int32(1)
                return parent_ref[now]

            lax.fori_loop(0, TRUNK_SEGS + 2, step, parent_ref[s])
            code_ref[rank[s] * padded_slots + own[s]] = jnp.int32(2)

        return carry

    lax.fori_loop(0, slots, mark, 0)

    def visit(tile, carry):
        def look(c, count):
            some = jnp.int32(0)
            for i in range(per_chunk):
                for j in range(per_tile):
                    at = tile * per_tile + j
                    code = code_ref[(c * per_chunk + i) * padded_slots + at]
                    some = some | jnp.where(at < own_slots, code, 0)

            @pl.when(some > 0)
            def _():
                seen_ref[tile * chunks + count] = c

            return count + (some > 0).astype(jnp.int32)

        count_ref[tile] = lax.fori_loop(0, chunks, look, jnp.int32(0))
        return carry

    lax.fori_loop(0, tiles, visit, 0)


def mask(code_ref, y, run, tile, c, chunk, padded_slots):
    wide = KN * run
    per_tile = TILE // wide
    lane = lax.broadcasted_iota(jnp.int32, (1, TILE), 1)
    row = lax.broadcasted_iota(jnp.int32, (SEG, TILE), 0)
    which = lax.div(lane, wide)
    offset = y * wide + lax.rem(lane, wide)
    blocks = []
    for i in range(chunk // SEG):
        code = jnp.zeros((1, TILE), jnp.int32)
        for j in range(per_tile):
            one = code_ref[(c * (chunk // SEG) + i) * padded_slots + tile * per_tile + j]
            code = jnp.where(which == j, one, code)
        last = jnp.where(code == 0, -1, jnp.where(code == 1, SEG, offset))
        blocks.append(jnp.where(row <= last, 0.0, -1e30).astype(f32))
    return jnp.concatenate(blocks, axis=0)


def logits_chunk(keys_wide, queries, rows, j):
    first, last = keys_wide[0, j, rows, :], keys_wide[1, j, rows, :]
    top, low, rest = queries[j]
    return mm(first, top) + (mm(first, low) + mm(last, rest))


def split_keys(keys, keys_wide, rows):
    for j in range(2):
        top, low, rest = thirds(keys[:, j * HD : (j + 1) * HD])
        keys_wide[0, j, rows, :HD] = top
        keys_wide[0, j, rows, HD:] = low
        keys_wide[1, j, rows, :HD] = top
        keys_wide[1, j, rows, HD:] = rest


def split_queries(q):
    out = []
    for j in range(2):
        top, low, rest = thirds(q[:, j * HD : (j + 1) * HD].T)
        out.append([jnp.concatenate(p, axis=0) for p in ((top, top), (low, low), (rest, top))])
    return out


def chunk_rows(c, size):
    return pl.ds(pl.multiple_of(c * size, size), size)


def brought(run, start_ref, first, count, source, target):
    def move(i, carry):
        target[chunk_rows(i, run), :] = source[chunk_rows(start_ref[first + i], run), :]
        return carry

    lax.fori_loop(0, count, move, 0)


def taken_back(run, start_ref, first, count, source, target):
    def move(i, carry):
        target[chunk_rows(start_ref[first + i], run), :] = source[chunk_rows(i, run), :]
        return carry

    lax.fori_loop(0, count, move, 0)


def forward_kernel(
    run, mix_ref, at_ref, seen_ref, count_ref, key_ref, own_ref, code_ref, q_ref, k_ref, v_ref,
    o_ref, stat_ref, keys_wide, vt, held, sorted_rows, sorted_q,
):
    total = k_ref.shape[0]
    chunk = vt.shape[3]
    count = total // chunk
    tile = pl.program_id(0)

    @pl.when(tile == 0)
    def _():
        brought(run, own_ref, 0, q_ref.shape[0] // run, q_ref, sorted_q)
        brought(run, key_ref, 0, total // run, k_ref, sorted_rows)

        def split(c, carry):
            rows = chunk_rows(c, chunk)
            split_keys(sorted_rows[rows, :], keys_wide, rows)
            return carry

        lax.fori_loop(0, count, split, 0)
        brought(run, key_ref, 0, total // run, v_ref, sorted_rows)

        def turn(c, carry):
            for i, p in enumerate(thirds(sorted_rows[chunk_rows(c, chunk), :].T)):
                vt[i, c] = p
            return carry

        lax.fori_loop(0, count, turn, 0)

    split = split_queries(sorted_q[chunk_rows(tile, TILE), :])
    visits = count_ref[tile]

    padded_slots = q_ref.shape[0] // (KN * run)

    def score(i, peaks):
        c = seen_ref[tile * count + i]
        rows = chunk_rows(c, chunk)
        bias = mask(code_ref, at_ref[1], run, tile, c, chunk, padded_slots)
        out = []
        for j in range(2):
            s = logits_chunk(keys_wide, split, rows, j) + bias
            held[j, rows, :] = s
            out.append(jnp.maximum(peaks[j], jnp.max(s, axis=0, keepdims=True)))
        return tuple(out)

    peaks = lax.fori_loop(0, visits, score, (jnp.full((1, TILE), -1e30, f32),) * 2)

    def weigh(i, sums):
        rows = chunk_rows(seen_ref[tile * count + i], chunk)
        out = []
        for j in range(2):
            w = jnp.exp(held[j, rows, :] - peaks[j])
            held[j, rows, :] = w
            out.append(sums[j] + jnp.sum(w, axis=0, keepdims=True))
        return tuple(out)

    sums = lax.fori_loop(0, visits, weigh, (jnp.zeros((1, TILE), f32),) * 2)
    first, second = 1.0 / sums[0], mix_ref[0] / sums[1]

    def collect(i, acc):
        c = seen_ref[tile * count + i]
        rows = chunk_rows(c, chunk)
        both = thirds(held[0, rows, :] * first - held[1, rows, :] * second)
        return acc + six([vt[i, c] for i in range(3)], both)

    out = lax.fori_loop(0, visits, collect, jnp.zeros((VD, TILE), f32)).T
    for i in range(TILE // run):
        o_ref[chunk_rows(own_ref[tile * (TILE // run) + i], run), :] = out[i * run : (i + 1) * run, :]
    for j in range(2):
        stat_ref[j : j + 1, :] = peaks[j] + jnp.log(sums[j])
        stat_ref[2 + j : 3 + j, :] = peaks[j]
    stat_ref[4:8, :] = jnp.zeros((4, TILE), f32)


def backward_kernel(
    run, mix_ref, at_ref, seen_ref, count_ref, key_ref, own_ref, code_ref, q_ref, dc_ref, stat_ref, k_ref, v_ref,
    dq_ref, dk_ref, dv_ref, inner_ref, keys_wide, kt, held, cross, sorted_v, sorted_q, sorted_dc,
):
    total = k_ref.shape[0]
    chunk = kt.shape[3]
    count = total // chunk
    mix = mix_ref[0]
    tile = pl.program_id(0)

    @pl.when(tile == 0)
    def _():
        brought(run, own_ref, 0, q_ref.shape[0] // run, q_ref, sorted_q)
        brought(run, own_ref, 0, q_ref.shape[0] // run, dc_ref, sorted_dc)
        brought(run, key_ref, 0, total // run, k_ref, sorted_v)

        def prepare(c, carry):
            rows = chunk_rows(c, chunk)
            keys = sorted_v[rows, :]
            split_keys(keys, keys_wide, rows)
            for i, p in enumerate(halves(keys.T)):
                kt[i, c] = p
            dk_ref[rows, :] = jnp.zeros(keys.shape, f32)
            dv_ref[rows, :] = jnp.zeros(keys.shape, f32)
            return carry

        lax.fori_loop(0, count, prepare, 0)
        brought(run, key_ref, 0, total // run, v_ref, sorted_v)

    queries, cotangents = sorted_q[chunk_rows(tile, TILE), :], sorted_dc[chunk_rows(tile, TILE), :]
    split = split_queries(queries)
    dct = thirds(cotangents.T)
    dc_top, dc_low = halves(cotangents)
    dc_wide = jnp.concatenate([dc_top, dc_top], axis=0)
    q_top, q_low = halves(queries)
    q_wide = jnp.concatenate([q_top, q_top], axis=0)
    norms = [stat_ref[j : j + 1, :] for j in range(2)]
    visits = count_ref[tile]

    padded_slots = q_ref.shape[0] // (KN * run)

    def first(i, inner):
        c = seen_ref[tile * count + i]
        rows = chunk_rows(c, chunk)
        bias = mask(code_ref, at_ref[1], run, tile, c, chunk, padded_slots)
        both = six(thirds(sorted_v[rows, :]), dct)
        cross[rows, :] = both
        out, probs = [], []
        for j in range(2):
            p = jnp.exp(logits_chunk(keys_wide, split, rows, j) + bias - norms[j])
            held[j, rows, :] = p
            probs.append(p)
            out.append(inner[j] + jnp.sum(p * both, axis=0, keepdims=True))
        top, low = halves(probs[0] - mix * probs[1])
        dv_ref[rows, :] += mm(jnp.concatenate([top, low], axis=1), dc_wide) + mm(top, dc_low)
        return tuple(out)

    inner = lax.fori_loop(0, visits, first, (jnp.zeros((1, TILE), f32),) * 2)

    def second(i, acc):
        c = seen_ref[tile * count + i]
        rows = chunk_rows(c, chunk)
        both = cross[rows, :]
        out = []
        for j in range(2):
            d = held[j, rows, :] * (both - inner[j])
            if j == 1:
                d = d * (-mix)
            top, low = halves(d)
            cols = slice(j * HD, (j + 1) * HD)
            dk_ref[rows, cols] += mm(jnp.concatenate([top, low], axis=1), q_wide[:, cols]) + mm(
                top, q_low[:, cols]
            )
            kt_top, kt_low = kt[0, c, cols, :], kt[1, c, cols, :]
            out.append(acc[j] + (mm(kt_top, top) + (mm(kt_top, low) + mm(kt_low, top))))
        return tuple(out)

    dq = lax.fori_loop(0, visits, second, (jnp.zeros((HD, TILE), f32),) * 2)
    dq = jnp.concatenate(dq, axis=0).T
    for i in range(TILE // run):
        dq_ref[chunk_rows(own_ref[tile * (TILE // run) + i], run), :] = dq[i * run : (i + 1) * run, :]
    for j in range(2):
        inner_ref[j : j + 1, :] = inner[j]
    inner_ref[2:8, :] = jnp.zeros((6, TILE), f32)

    @pl.when(tile == pl.num_programs(0) - 1)
    def _():
        for ref in (dk_ref, dv_ref):

            def keep(c, carry):
                rows = chunk_rows(c, chunk)
                sorted_v[rows, :] = ref[rows, :]
                return carry

            lax.fori_loop(0, count, keep, 0)
            taken_back(run, key_ref, 0, total // run, sorted_v, ref)


TILE = 128
CHUNK = 256


def whole():
    return pl.BlockSpec(memory_space=pltpu.VMEM)


def table():
    return pl.BlockSpec(memory_space=pltpu.SMEM)


def tables_of(sizes, shape, parent_slot, place):
    slots, own_slots, padded_slots, tiles, chunks = shape
    yn = sizes[1]
    counts = (tiles * chunks, tiles, slots * yn * KN, padded_slots * KN, slots * padded_slots, slots)
    return pl.pallas_call(
        lambda *refs: table_kernel(sizes, shape, *refs),
        in_specs=[table()] * 2,
        out_specs=[table()] * len(counts),
        out_shape=[jax.ShapeDtypeStruct((n,), jnp.int32) for n in counts],
        scratch_shapes=[pltpu.SMEM((slots,), jnp.int32)] * 3,
        name="tables",
    )(parent_slot, place)


def attend(run, mix, tables, queries, keys, values):
    total, count = keys.shape[0], queries.shape[0]
    chunk = math.gcd(total, CHUNK)
    lanes = lambda rows: pl.BlockSpec((rows, TILE), lambda i: (0, i))
    return pl.pallas_call(
        lambda *refs: forward_kernel(run, *refs),
        grid=(count // TILE,),
        in_specs=[table()] * 7 + [whole()] * 3,
        out_specs=[whole(), lanes(8)],
        out_shape=[
            jax.ShapeDtypeStruct((count, VD), f32), jax.ShapeDtypeStruct((8, count), f32),
        ],
        scratch_shapes=[
            pltpu.VMEM((2, 2, total, 2 * HD), bf16),
            pltpu.VMEM((3, total // chunk, VD, chunk), bf16),
            pltpu.VMEM((2, total, TILE), f32),
            pltpu.VMEM((total, 2 * HD), f32),
            pltpu.VMEM((count, 2 * HD), f32),
        ],
        compiler_params=pltpu.CompilerParams(vmem_limit_bytes=VMEM_BYTES),
        cost_estimate=pl.CostEstimate(flops=4 * 10**10, bytes_accessed=0, transcendentals=0),
        name="attend",
    )(mix, *tables, queries, keys, values)


def attend_back(run, mix, tables, queries, contrast, stat, keys, values):
    total, count = keys.shape[0], queries.shape[0]
    chunk = math.gcd(total, CHUNK)
    lanes = lambda rows: pl.BlockSpec((rows, TILE), lambda i: (0, i))
    return pl.pallas_call(
        lambda *refs: backward_kernel(run, *refs),
        grid=(count // TILE,),
        in_specs=[table()] * 7 + [whole()] * 2 + [lanes(8)] + [whole()] * 2,
        out_specs=[whole(), whole(), whole(), lanes(8)],
        out_shape=[
            jax.ShapeDtypeStruct((count, 2 * HD), f32),
            jax.ShapeDtypeStruct((total, 2 * HD), f32),
            jax.ShapeDtypeStruct((total, VD), f32),
            jax.ShapeDtypeStruct((8, count), f32),
        ],
        scratch_shapes=[
            pltpu.VMEM((2, 2, total, 2 * HD), bf16),
            pltpu.VMEM((2, total // chunk, 2 * HD, chunk), bf16),
            pltpu.VMEM((2, total, TILE), f32),
            pltpu.VMEM((total, TILE), f32),
            pltpu.VMEM((total, VD), f32),
            pltpu.VMEM((count, 2 * HD), f32),
            pltpu.VMEM((count, VD), f32),
        ],
        compiler_params=pltpu.CompilerParams(vmem_limit_bytes=VMEM_BYTES),
        cost_estimate=pl.CostEstimate(flops=4 * 10**10, bytes_accessed=0, transcendentals=0),
        name="attend_back",
    )(mix, *tables, queries, contrast, stat, keys, values)


def layer(xn, yn):
    sizes = {"x": xn, "y": yn}
    places = [(s, t) for s in range(xn) for t in range(yn)]

    def shards(
        tokens, cotangent, w_query, w_key, w_value, w_output, gain_attn, lambda_query_first,
        lambda_key_first, lambda_query_second, lambda_key_second, gain_head, w_gate, w_up, w_down,
        gain_ffn, tau, parent_slot, depth,
    ):
        z, x, y, k = (lax.axis_index(a) for a in "zxyk")
        home_rows, width = tokens.shape
        segs = home_rows // SEG
        run = SEG // (yn * KN)
        piece_rows = segs * run
        group = ZN * KN * piece_rows
        sub = BLOCKS // yn
        held_rows = w_query.shape[0]
        part_rows = held_rows // yn
        square_rows = ZN * part_rows
        total = ZN * xn * home_rows
        slot_total = parent_slot.shape[0]
        hidden_cols = w_gate.shape[1] // sub

        def block(v, i):
            return v[:, i * part_rows : (i + 1) * part_rows]

        def by_index(i, n, order):
            out = order(0)
            for j in range(1, n):
                out = jnp.where(i == j, order(j), out)
            return out

        def to_distance_x(v):
            return by_index(x, xn, lambda j: jnp.concatenate(
                [block(v, (c * xn + (j + xn - s) % xn) * yn + t)
                 for s in range(xn) for c in range(ZN) for t in range(yn)], axis=1))

        def from_distance_x(v):
            return by_index(x, xn, lambda j: jnp.concatenate(
                [block(v, ((j + xn - a) % xn * ZN + c) * yn + t)
                 for c in range(ZN) for a in range(xn) for t in range(yn)], axis=1))

        def to_distance_y(v):
            return by_index(y, yn, lambda j: jnp.concatenate(
                [block(v, (s * ZN + c) * yn + (j + yn - t) % yn)
                 for s in range(xn) for t in range(yn) for c in range(ZN)], axis=1))

        def from_distance_y(v):
            return by_index(y, yn, lambda j: jnp.concatenate(
                [block(v, (s * yn + (j + yn - t) % yn) * ZN + c)
                 for s in range(xn) for c in range(ZN) for t in range(yn)], axis=1))

        def piece(v):
            v = v.reshape(segs, yn * KN, run, width)
            return to_distance_x(at(v, y * KN + k, 1).reshape(piece_rows, width))

        def home_along(v, axis, n):
            return [v] + [shifted(v, axis, n, s) for s in range(1, n)]

        def homed(v):
            v = v.reshape(KN, yn, segs, run, width)
            return jnp.transpose(v, (2, 1, 0, 3, 4)).reshape(home_rows, width)

        def group_gather(v):
            return lax.all_gather(v, ("z", "k"), axis=0, tiled=True)

        def group_sum(v):
            return lax.psum_scatter(v, ("z", "k"), scatter_dimension=0, tiled=True)

        def packed(mats, blocks):
            rows = mats[0].shape[1] // blocks
            mats = [m.T for m in mats]
            return jnp.concatenate([m[s * rows : (s + 1) * rows] for s in range(blocks) for m in mats])

        def lanes(v, index, size):
            return lax.dynamic_slice_in_dim(v, index * size, size, 1)

        def along_y(v):
            mine = lanes(v, y, part_rows)
            return [mine] + [shifted(lanes(v, (y + s) % yn, part_rows), "y", yn, s) for s in range(1, yn)]

        def back_along_z(mats):
            v = jnp.concatenate(mats)
            size = v.shape[1] // ZN
            mine = lanes(v, z, size)
            return [mine] + [shifted(lanes(v, (z + s) % ZN, size), "z", ZN, s) for s in range(1, ZN)]

        def unpacked(v, mats, blocks):
            cols = v.shape[0] // (blocks * mats)
            part = lambda s, m: v[(s * mats + m) * cols : (s * mats + m + 1) * cols]
            return [jnp.concatenate([part(s, m) for s in range(blocks)]).T for m in range(mats)]

        def joined_up(pieces):
            return jnp.concatenate([pieces[p] for p in places], axis=1)

        def cut(g):
            return {p: g[:, i * square_rows : (i + 1) * square_rows] for i, p in enumerate(places)}

        def tiled_up(pieces):
            return jnp.concatenate(
                [jnp.concatenate([pieces[s, t] for s in range(xn)], axis=1) for t in range(yn)]
            )

        def tiles(g):
            r, c = g.shape[0] // yn, g.shape[1] // xn
            return {(s, t): g[t * r : (t + 1) * r, s * c : (s + 1) * c] for s, t in places}

        def halved(v):
            mid = v.shape[0] // 2
            return v[:mid], v[mid:]

        def rowsum(w, g):
            return jnp.sum(w * g, axis=1)

        last = []

        def now(*v):
            out = lax.optimization_barrier(tuple(v) + tuple(last))[: len(v)]
            return out[0] if len(v) == 1 else out

        def then(*v):
            last[:] = v
            return v[0] if len(v) == 1 else v

        def take(*v):
            out = now(*v)
            return then(*(out if len(v) > 1 else (out,)))

        def take_all(pieces):
            out = lax.optimization_barrier(tuple(pieces) + tuple(last))[: len(pieces)]
            then(*out)
            return list(out)

        attn_gain, ffn_gain = gain_attn[:, None], gain_ffn[:, None]
        sent = along_y(packed([w_query, w_key, w_value], sub))
        small = jnp.concatenate(
            [gain_head, lambda_query_first, lambda_key_first, lambda_query_second, lambda_key_second]
        )
        small_sent = home_along(small[None], "x", xn)
        attn_y = in_order(take_all(sent), "y", yn)
        y_gain = part(gain_attn, y, part_rows)[None, :]
        sent = exchanged(attn_y * y_gain, "z", ZN)
        output_sent = along_y(after(packed([w_output], sub), attn_y))
        sent[: 2] = take_all(sent[: 2])
        padded = -(-group // TILE) * TILE
        own_slots = ZN * segs
        chunks = total // math.gcd(total, CHUNK)
        *tables, depth_of = tables_of(
            (xn, yn, segs, run, group // run),
            (slot_total, own_slots, padded // (KN * run), padded // TILE, chunks),
            now(parent_slot), jnp.stack([x, y]),
        )
        tables = [jnp.stack([x, y])] + tables
        mine = piece(now(tokens))
        scale = lax.rsqrt(jnp.mean(mine * mine, axis=1, keepdims=True) + epsilon)
        mine_attn = to_distance_y(mine)
        plain_mine = then(mine_attn * scale)
        down_sent = now(w_down).T
        then(down_sent, plain_mine, *tables)
        small = in_order(take_all(small_sent), "x", xn).reshape(1, -1)
        small_sent = home_along(small, "z", ZN)
        output_y = in_order(take_all(output_sent), "y", yn)
        shares = down_sent.shape[1] // part_rows
        output_y = output_y.reshape(BLOCKS, shares, VD // shares, part_rows)
        output_y = jnp.concatenate([output_y[:, i] for i in range(shares)], axis=2)
        output_down = jnp.concatenate(
            [output_y, down_sent.reshape(BLOCKS, -1, down_sent.shape[1])], axis=1
        ).reshape(-1, down_sent.shape[1])
        then(output_down)
        attn_z = in_order(sent[:2] + take_all(sent[2:]), "z", ZN, 1)
        upper, lower = halved(attn_z)
        upper_out, lower_out = square_out(upper, "x", sizes), square_out(lower, "y", sizes)
        upper_side, lower_side = side_out(upper, "x", sizes), side_out(lower, "y", sizes)
        plain_sent = group_gather(after(plain_mine, attn_z))
        upper_on = square_on(take_all(upper_out), "x", sizes, upper_side)
        lower_on = square_on(take_all(lower_out), "y", sizes, lower_side)

        small = in_order(take_all(small_sent), "z", ZN).reshape(ZN * xn, -1)
        n_gain, n_lambda = gain_head.shape[0], lambda_key_first.shape[0]
        head_gain = small[:, :n_gain].reshape(1, -1)
        query_first, key_first, query_second, key_second = (
            small[:, n_gain + i * n_lambda : n_gain + (i + 1) * n_lambda] for i in range(4)
        )
        mix = (
            jnp.exp(jnp.sum(query_first * key_first))
            - jnp.exp(jnp.sum(query_second * key_second))
            + lambda_init
        ).reshape(1)

        def padded_rows(v):
            return jnp.pad(v, ((0, padded - group), (0, 0)))

        shape = (ZN, KN, segs, run)
        ks, rs = (lax.broadcasted_iota(jnp.int32, shape, d) for d in (1, 3))
        depths = at(depth_of.reshape(ZN, xn, segs), x, 1)[:, None, :, None]
        position = (depths * SEG + (y * KN + ks) * run + rs).reshape(group, 1).astype(f32)
        half_dim = HD // 2
        frequency = jnp.exp(-rope_log_base * jnp.arange(half_dim, dtype=f32) / half_dim)
        angles = position * frequency[None, :]
        cosine, sine = jnp.cos(angles), jnp.sin(angles)
        cosine = jnp.concatenate([cosine] * 4, axis=1)
        sine = jnp.concatenate([-sine, sine] * 2, axis=1)

        def rotate(v, sign):
            parts = [v[:, i * half_dim : (i + 1) * half_dim] for i in (1, 0, 3, 2)]
            return v * cosine + jnp.concatenate(parts, axis=1) * (sign * sine)

        cot_mine = piece(cotangent)
        upper = joined_up(dict(zip(places, take_all([upper_on[p] for p in places]), strict=True)))
        lower = joined_up(dict(zip(places, take_all([lower_on[p] for p in places]), strict=True)))
        plain = take(plain_sent)
        down_sent = exchanged(after(output_down, plain), "z", ZN)
        cot_sent = group_gather(after(cot_mine, plain))
        wqkv = jnp.concatenate([upper, lower])
        wqk, wv = wqkv[: 4 * HD], wqkv[4 * HD :]
        then(wqkv)
        logit_scale = 1.0 / math.sqrt(HD)
        key_own = then(rotate(fine(now(plain), wqk[2 * HD :], 1, 1), 1.0))
        key_sent = square_out(key_own, "x", sizes)
        value_own = then(fine(now(plain), wv, 1, 1))
        value_sent = square_out(value_own, "y", sizes)
        queries = rotate(fine(now(plain), wqk[: 2 * HD], 1, 1), 1.0)
        queries = then(padded_rows(queries * logit_scale))
        gate_up_sent = packed([now(w_up) * ffn_gain, now(w_gate) * ffn_gain], BLOCKS)
        then(queries, gate_up_sent)
        key_sent = square_on(take_all(key_sent), "x", sizes)
        value_sent = square_on(take_all(value_sent), "y", sizes)
        came = take_all(down_sent)
        output_rows = VD // shares
        down_z = in_order([v[output_rows:] for v in came], "z", ZN, 1)
        output_z = in_order(
            [
                jnp.concatenate([v[:output_rows, i * part_rows : (i + 1) * part_rows] for i in range(shares)])
                for v in came
            ],
            "z", ZN, 1,
        )
        gate_up_sent = exchanged(after(gate_up_sent, down_z), "z", ZN)
        key_list = take_all([key_sent[p] for p in places])
        value_list = take_all([value_sent[p] for p in places])
        output_sent = direct(after(output_z, *value_list), xn, yn)
        down_z = after(down_z, *value_list)
        down_out, down_side = square_out(down_z, "x", sizes), side_out(down_z, "x", sizes)
        keys, values = jnp.concatenate(key_list), jnp.concatenate(value_list)
        cot = take(cot_sent)
        contrast, stat = attend(run, mix, tables, now(queries), keys, values)
        then(contrast)
        gate_up_sent = take_all(gate_up_sent)
        output_sent = dict(zip(places, take_all([output_sent[p] for p in places]), strict=True))
        wo = joined_up(output_sent)
        contrast = now(contrast)[:group]
        head_scale = lax.rsqrt(jnp.mean(contrast * contrast, axis=1, keepdims=True) + epsilon)
        head_plain = contrast * head_scale
        joined = head_plain * head_gain * (1.0 - lambda_init)
        branch_part = then(fine(joined, wo))
        branch_sent = group_sum(branch_part)
        up_w, gate_w = halved(in_order(gate_up_sent, "z", ZN, 1))

        down_out, down_side = take_all(down_out), take_all(down_side)
        down_on = square_on(down_out, "x", sizes, down_side)
        up_w = after(up_w, *down_out)
        up_out, up_side = square_out(up_w, "y", sizes), side_out(up_w, "y", sizes)
        down_pieces = dict(zip(places, take_all([down_on[p] for p in places]), strict=True))
        up_side = take_all(up_side)
        gate_w = after(gate_w, *up_side)
        gate_out, gate_side = square_out(gate_w, "x", sizes), side_out(gate_w, "x", sizes)
        branch = take(branch_sent)
        residual = from_distance_y(mine_attn + branch)
        ffn_scale = lax.rsqrt(jnp.mean(residual * residual, axis=1, keepdims=True) + epsilon)
        ffn_mine = then(residual * ffn_scale)
        ffn_sent = group_gather(ffn_mine)
        wd = tiled_up(down_pieces)
        grad_hidden = then(fine(wd, cot, 1, 1))
        gate_out = take_all(gate_out)
        up_on = square_on(take_all(up_out), "y", sizes, up_side)
        gate_on = square_on(gate_out, "x", sizes, gate_side)
        up_pieces = dict(zip(places, take_all([up_on[p] for p in places]), strict=True))
        ffn_plain = take(ffn_sent)
        gate_list = take_all([gate_on[p] for p in places])
        wug = jnp.concatenate(
            [
                jnp.concatenate([v[s, t] for s in range(xn)], axis=1)
                for t in range(yn)
                for v in (up_pieces,)
            ]
            + [
                jnp.concatenate([v[s, t] for s in range(xn)], axis=1)
                for t in range(yn)
                for v in (dict(zip(places, gate_list, strict=True)),)
            ]
        )

        both = fine(wug, ffn_plain, 1, 1)
        up_proj, gating = halved(both)
        gate = lax.logistic(gating)
        active = gating * gate
        hidden = active * up_proj
        grad_both = jnp.concatenate(
            [grad_hidden * active, grad_hidden * up_proj * gate * (1.0 + gating * (1.0 - gate))]
        )
        grad_ffn_part = then(fine(grad_both, wug, 0, 0))
        grad_up_proj, grad_gating = halved(grad_both)
        grad_ffn_sent = group_sum(grad_ffn_part)
        down_grad = then(dot(now(hidden), cot))
        down_first = tiles(down_grad)
        down_sent = square_back(down_first, "x", sizes)
        up_grad = then(dot(now(grad_up_proj), ffn_plain))
        up_first = tiles(up_grad)
        up_sent = square_back(up_first, "y", sizes)
        gate_grad = then(dot(now(grad_gating), ffn_plain))
        gate_tiles = {p: halved(v) for p, v in tiles(gate_grad).items()}
        top_first = {p: v[0] for p, v in gate_tiles.items()}
        low_first = {p: v[1] for p, v in gate_tiles.items()}
        out_part = then(dot(now(hidden), wd, 0, 0))
        early = (xn - 1) * (yn - 1)
        down_sent[:early], up_sent[:early] = take_all(down_sent[:early]), take_all(up_sent[:early])
        down_first = square_added(down_first, down_sent[:early], "x", sizes)
        down_sent_on = square_back_on(down_first, "y", sizes)
        up_first = square_added(up_first, up_sent[:early], "y", sizes)
        up_sent_on = square_back_on(up_first, "x", sizes)
        then(*down_first[1:], *up_first[1:])
        scaled = take(grad_ffn_sent)
        grad_residual = cot_mine + ffn_scale * (
            scaled - ffn_mine * jnp.mean(scaled * ffn_mine, axis=1, keepdims=True)
        )
        grad_residual_attn = then(to_distance_y(grad_residual))
        grad_branch_sent = group_gather(grad_residual_attn)
        down_grad = sum(take_all(down_sent[early:]), down_first[0])
        up_grad = sum(take_all(up_sent[early:]), up_first[0])
        then(down_grad, up_grad)
        grad_branch = take(grad_branch_sent)

        out_sent = group_sum(after(out_part, grad_branch))
        grad_joined = fine(grad_branch, wo, 1, 1) * (1.0 - lambda_init)
        grad_head_gain = jnp.sum(grad_joined * head_plain, axis=0)
        scaled = grad_joined * head_gain
        grad_contrast = padded_rows(
            head_scale * (scaled - head_plain * jnp.mean(scaled * head_plain, axis=1, keepdims=True))
        )
        grad_contrast = then(grad_contrast)
        down_grad = sum(take_all(down_sent_on), down_grad)
        down_back = back_along_z([down_grad])
        up_grad = sum(take_all(up_sent_on), up_grad)
        up_back = back_along_z([up_grad])
        then(down_grad, up_grad)
        top_sent = square_back({p: after(v, down_grad) for p, v in top_first.items()}, "x", sizes)
        low_sent = square_back({p: after(v, up_grad) for p, v in low_first.items()}, "y", sizes)
        grad_contrast = now(grad_contrast)
        grad_queries, grad_keys, grad_values, inner = attend_back(
            run, mix, tables, queries, grad_contrast, stat, keys, values
        )
        then(grad_queries, grad_keys, grad_values)
        rows_cut = lambda g: {p: g[i * group : (i + 1) * group] for i, p in enumerate(places)}
        key_first, value_first = rows_cut(grad_keys), rows_cut(grad_values)
        key_sent = square_back(key_first, "x", sizes)
        value_sent = square_back(value_first, "y", sizes)
        def reduced(v):
            return jnp.concatenate([jnp.max(v[:, :2], axis=0), jnp.sum(v[:, 2:], axis=0)])[None]

        peak = jnp.max(stat[2:4, :group], axis=1)
        every = jnp.concatenate([peak, grad_head_gain, -jnp.sum(inner[1:2, :group], axis=1)])[None]
        every_sent = home_along(every, "x", xn)
        top_first = square_added(top_first, take_all(top_sent), "x", sizes)
        low_first = square_added(low_first, take_all(low_sent), "y", sizes)
        then(*top_first, *low_first)
        key_first = square_added(key_first, take_all(key_sent), "x", sizes)
        key_sent = square_back_on(key_first, "y", sizes)
        value_first = square_added(value_first, take_all(value_sent), "y", sizes)
        value_sent = square_back_on(value_first, "x", sizes)
        then(*key_first, *value_first)
        every_sent = home_along(reduced(in_order(take_all(every_sent), "x", xn)), "y", yn)
        top_sent = square_back_on([after(v, *key_first) for v in top_first], "y", sizes)
        low_sent = square_back_on([after(v, *value_first) for v in low_first], "x", sizes)
        grad_q = rotate(grad_queries[:group] * logit_scale, -1.0)
        query_grad = dot(grad_q, plain, 0, 0)
        output_grad = dot(joined, grad_branch, 0, 0)
        then(query_grad, output_grad)
        down_back = in_order(take_all(down_back), "z", ZN)
        grad_k = rotate(sum(take_all(key_sent), key_first[0]), -1.0)
        grad_value_own = sum(take_all(value_sent), value_first[0])
        every = reduced(in_order(take_all(every_sent), "y", yn))
        every_sent = home_along(every, "k", KN)
        query_first, output_first = (
            cut(after(g, grad_k, grad_value_own)) for g in (query_grad, output_grad)
        )
        query_sent = square_back(query_first, "x", sizes)
        output_sent = square_back(output_first, "y", sizes)
        key_grad = then(dot(grad_k, plain, 0, 0))
        key_first = cut(key_grad)
        key_sent = square_back(key_first, "x", sizes)
        value_grad = then(dot(grad_value_own, plain, 0, 0))
        value_first = cut(value_grad)
        value_sent = square_back(value_first, "y", sizes)
        grad_qk = now(jnp.concatenate([grad_q, grad_k], axis=1))
        grad_part = then(dot(grad_qk, wqk) + dot(grad_value_own, wv))
        grad_attn_sent = group_sum(grad_part)

        every = in_order(take_all(every_sent), "k", KN)
        every = jnp.concatenate([every[:, :2].reshape(1, -1), jnp.sum(every[:, 2:], axis=0, keepdims=True)], axis=1)
        every_sent = home_along(every, "z", ZN)
        top_grad = sum(take_all(top_sent), top_first[0])
        low_grad = sum(take_all(low_sent), low_first[0])
        gate_back = back_along_z([jnp.concatenate([top_grad, low_grad])])
        query_first = square_added(query_first, take_all(query_sent), "x", sizes)
        query_sent = square_back_on(query_first, "y", sizes)
        output_first = square_added(output_first, take_all(output_sent), "y", sizes)
        output_sent = square_back_on(output_first, "x", sizes)
        then(*query_first, *output_first)
        key_first = square_added(key_first, take_all(key_sent), "x", sizes)
        key_sent = square_back_on(key_first, "y", sizes)
        value_first = square_added(value_first, take_all(value_sent), "y", sizes)
        value_sent = square_back_on(value_first, "x", sizes)
        then(*key_first, *value_first)
        every = in_order(take_all(every_sent), "z", ZN)
        up_back = in_order(take_all(up_back), "z", ZN)
        out_sum = take(out_sent)
        output = residual + out_sum
        out_sent = home_along(from_distance_x(output), "y", yn)
        query_grad = sum(take_all(query_sent), query_first[0])
        output_grad = sum(take_all(output_sent), output_first[0])
        early_sent = back_along_z([query_grad, output_grad])
        grad_down, grad_up = (v.T for v in now(down_back, up_back))
        then(grad_down, grad_up)
        key_grad = sum(take_all(key_sent), key_first[0])
        value_grad = sum(take_all(value_sent), value_first[0])
        late_sent = back_along_z([key_grad, value_grad])
        grad_gate = then(in_order(take_all(gate_back), "z", ZN).T)
        out_sent = home_along(in_order(take_all(out_sent), "y", yn), "k", KN)
        ffn_gain_part = then(rowsum(w_gate, grad_gate) + rowsum(w_up, grad_up))
        scaled = take(grad_attn_sent)
        grad_mine = grad_residual_attn + scale * (
            scaled - plain_mine * jnp.mean(scaled * plain_mine, axis=1, keepdims=True)
        )
        grad_mine = then(from_distance_x(from_distance_y(grad_mine)))
        tokens_sent = home_along(grad_mine, "y", yn)
        output = then(homed(in_order(take_all(out_sent), "k", KN)))
        early = in_order(take_all(early_sent), "z", ZN)
        early_sent = exchanged(early, "y", yn)
        tokens_sent = home_along(in_order(take_all(tokens_sent), "y", yn), "k", KN)
        late = in_order(take_all(late_sent), "z", ZN)
        late_sent = exchanged(late, "y", yn)
        grad_tokens = then(homed(in_order(take_all(tokens_sent), "k", KN)))
        by_block = lambda v, mats: v.reshape(BLOCKS, mats, 2 * HD, part_rows)
        held_w, held_early, held_late = by_block(attn_y, 3), by_block(early, 2), by_block(late, 2)
        attn_gain_part = (
            jnp.sum(held_w[:, 0] * held_early[:, 0], axis=(0, 1))
            + jnp.sum(held_w[:, 1] * held_late[:, 0], axis=(0, 1))
            + jnp.sum(held_w[:, 2] * held_late[:, 1], axis=(0, 1))
        )
        gains = then(jnp.concatenate([attn_gain_part, ffn_gain_part]))[None]
        gains_sent = home_along(gains, "k", KN)
        early = in_order(take_all(early_sent), "y", yn, 1)
        grad_query, grad_output = unpacked(early, 2, sub)
        then(grad_query, grad_output)
        gains = jnp.sum(in_order(take_all(gains_sent), "k", KN), axis=0, keepdims=True)
        gains_sent = home_along(gains, "y", yn)
        sums = jnp.sum(every[:, 2 * KN :], axis=0)
        size = gain_head.shape[0]
        grad_head_gain = lax.dynamic_slice_in_dim(sums[:VD], (z * xn + x) * size, size)
        grad_mix = sums[VD:]
        peak = every[:, : 2 * KN].reshape(yn, sub, KN, 2)
        maxima = jnp.transpose(peak, (0, 2, 1, 3)).reshape(2 * HEADS)
        late = in_order(take_all(late_sent), "y", yn, 1)
        grad_key, grad_value = unpacked(late, 2, sub)
        gains = in_order(take_all(gains_sent), "y", yn)
        grad_attn_gain = gains[:, :part_rows].reshape(-1)
        grad_ffn_gain = jnp.sum(gains[:, part_rows:], axis=0)
        factor = jnp.sqrt(tau[0] / jnp.maximum(maxima, tau[0]))
        mine_factor = lax.dynamic_slice_in_dim(factor, (y * KN + k) * 2 * sub, 2 * sub)
        wide_factor = jnp.repeat(mine_factor, HD)[None, :]
        return (
            output, grad_tokens, grad_query * attn_gain, grad_key * attn_gain, grad_value * attn_gain,
            grad_output, grad_attn_gain, grad_mix, grad_head_gain, grad_gate * ffn_gain,
            grad_up * ffn_gain, grad_down, grad_ffn_gain, maxima,
            w_query * wide_factor, w_key * wide_factor,
        )

    return shards


def solution(mesh):
    xn, yn = mesh.shape["row"] // ZN, mesh.shape["col"] // KN
    split = Mesh(mesh.devices.reshape(ZN, xn, yn, KN), ("z", "x", "y", "k"))
    row, col = ("z", "x"), ("y", "k")
    rows, both, vector = P(row, None), P(row, col), P(row)
    return jax.shard_map(
        layer(xn, yn),
        mesh=split,
        in_specs=(rows, rows, both, both, both, both, vector, vector, vector, vector, vector, vector,
                  both, both, both, vector, P(), P(), vector),
        out_specs=(rows, rows, both, both, both, both, vector, P(), vector, both, both, both, vector,
                   P(), both, both),
        check_vma=False,
    )
```
